32 devices in a mesh: dp: 4 (over x, core), pts: 8 (over z, y).
Axes of the slice: x: 2, y: 2, z: 4, core: 2. Of those that a mesh axis runs over, the one named last changes fastest.
Arguments:
- samples_in: float32 [64, 2, 2048], P('dp', None, 'pts'), may hold values from -6 to 6, as said below
- target: float32 [64, 2048], P('dp', 'pts'), may hold values from -6 to 6
- mask: int32 [64, 2048], P('dp', 'pts'), may hold values from 0 to 1
- attn_w: float32 [2, 128, 512], replicated, may hold values from -0.5 to 0.5
- ffn_w: float32 [2, 2, 128, 256], replicated, may hold values from -0.5 to 0.5
- spec_w: float32 [2, 16, 2, 64, 64], replicated, may hold values from -0.5 to 0.5
- dense_w: float32 [320, 64], replicated, may hold values from -0.5 to 0.5
- vectors: float32 [1984], replicated, may hold values from -4 to 4, as said below
- attn_m: float32 [2, 128, 512], replicated
- ffn_m: float32 [2, 2, 128, 256], replicated
- spec_m: float32 [2, 16, 2, 64, 64], replicated
- dense_m: float32 [320, 64], replicated
- vector_m: float32 [1984], replicated
- attn_v: float32 [2, 128, 512], replicated, as said below
- ffn_v: float32 [2, 2, 128, 256], replicated, as said below
- spec_v: float32 [2, 16, 2, 64, 64], replicated, as said below
- dense_v: float32 [320, 64], replicated, as said below
- vector_v: float32 [1984], replicated, as said below
Outputs:
- loss_sum: float32 [], replicated
- valid_count: float32 [], replicated
- attn_m_new: float32 [2, 128, 512], replicated
- attn_v_new: float32 [2, 128, 512], replicated
- attn_w_new: float32 [2, 128, 512], replicated
- attn_w_low: bfloat16 [2, 128, 512], replicated
- ffn_m_new: float32 [2, 2, 128, 256], replicated
- ffn_v_new: float32 [2, 2, 128, 256], replicated
- ffn_w_new: float32 [2, 2, 128, 256], replicated
- ffn_w_low: bfloat16 [2, 2, 128, 256], replicated
- spec_m_new: float32 [2, 16, 2, 64, 64], replicated
- spec_v_new: float32 [2, 16, 2, 64, 64], replicated
- spec_w_new: float32 [2, 16, 2, 64, 64], replicated
- spec_w_low: bfloat16 [2, 16, 2, 64, 64], replicated
- dense_m_new: float32 [320, 64], replicated
- dense_v_new: float32 [320, 64], replicated
- dense_w_new: float32 [320, 64], replicated
- dense_w_low: bfloat16 [320, 64], replicated
- vector_m_new: float32 [1984], replicated
- vector_v_new: float32 [1984], replicated
- vector_w_new: float32 [1984], replicated
- vector_w_low: bfloat16 [1984], replicated
- weight_norms: float32 [8], replicated
- update_norms: float32 [8], replicated
- trust_ratios: float32 [8], replicated
The draws below stay inside these ranges and needn't reach their ends.
Inputs may be any that keep to these rules, and one draw needn't show every extreme that they name: `samples_in`: row 1 holds the grid points' coordinates, rising by about 1 / 2048 from point to point. `vectors`: the norm gains are positive. `attn_v`: Positive. `ffn_v`: Positive. `spec_v`: Positive. `dense_v`: Positive. `vector_v`: Positive.
All inputs are finite; a program needn't handle non-finite values.
Results may differ from the reference program's by a relative error of at most 0.001.
Values sent between devices are 32-bit elements; how exact they have to be, the bound alone decides.
A program may use at most 192 MiB of HBM per device.

```python
import math
import jax
import jax.numpy as jnp
from jax import lax

D = 128
HEADS = 4
FF = 256
FREQ = 64
MODES = 16
LAYERS = 2
FLAYERS = 2
STEP = 5
SAMPLES = 64
POINTS = 2048
NVEC = 1984


def grad_scale():
    return 4.0 / math.sqrt(SAMPLES * POINTS)


def attn_scale():
    return 0.5


def moment(key, shape, scale, second):
    if second:
        factor = jnp.exp(jax.random.uniform(key, shape, minval=math.log(0.5), maxval=math.log(8.0)))
        return scale * scale * factor
    return scale * jnp.clip(jax.random.normal(key, shape), -4.0, 4.0)


def draw_samples_in(key, part):
    key = jax.random.fold_in(key, 1)
    keys = jax.random.split(key, 4)
    index = jnp.arange(POINTS, dtype=jnp.float32)[None, :]
    coord = (index + 0.5 + 0.4 * jax.random.uniform(keys[0], (SAMPLES, POINTS), minval=-1.0, maxval=1.0)) / POINTS
    amplitude = jnp.clip(0.3 * jax.random.normal(keys[1], (SAMPLES, 3, 1)), -0.5, 0.5)
    shift = jax.random.uniform(keys[2], (SAMPLES, 3, 1), minval=-math.pi, maxval=math.pi)
    waves = jnp.arange(1, 4, dtype=jnp.float32)[None, :, None]
    smooth = jnp.sum(amplitude * jnp.cos(2.0 * math.pi * waves * coord[:, None, :] + shift), axis=1)
    rough = jnp.clip(jax.random.normal(keys[3], (SAMPLES, POINTS)), -4.0, 4.0)
    return jnp.stack([rough + smooth, coord], 1)


def draw_mask(key, part):
    key = jax.random.fold_in(key, 2)
    chance = jax.random.randint(key, (SAMPLES, POINTS), 0, 1000)
    sample_id = jnp.arange(SAMPLES, dtype=jnp.int32)[:, None]
    point_id = jnp.arange(POINTS, dtype=jnp.int32)[None, :]
    limit = 200 + 300 * sample_id // SAMPLES + 300 * point_id // POINTS
    return (chance < limit).astype(jnp.int32)


def draw_vectors(key, part):
    key = jax.random.fold_in(key, 3)
    plan = [(D, 1.0), (D, 1.0), (D, 0.3)]
    for layer in range(LAYERS):
        plan = plan + [(D, -1.0), (D, -1.0), (FF, 0.3), (D, 0.3)]
    plan = plan + [(FREQ, 0.3)] * (FLAYERS + 2) + [(FREQ, FREQ ** (-0.5))]
    pieces = []
    for index, item in enumerate(plan):
        subkey = jax.random.fold_in(key, index)
        length, scale = item
        if scale < 0:
            pieces.append(jnp.exp(jax.random.uniform(subkey, (length,), minval=math.log(0.5), maxval=math.log(2.0))))
        else:
            pieces.append(scale * jnp.clip(jax.random.normal(subkey, (length,)), -4.0, 4.0))
    return jnp.concatenate(pieces)


def draw_attn_m(key, part):
    key = jax.random.fold_in(key, 11)
    scale = attn_scale()
    return moment(key, (LAYERS, D, 4 * D), scale, False)


def draw_ffn_m(key, part):
    key = jax.random.fold_in(key, 12)
    return moment(key, (LAYERS, 2, D, FF), grad_scale(), False)


def draw_spec_m(key, part):
    key = jax.random.fold_in(key, 13)
    return moment(key, (FLAYERS, MODES, 2, FREQ, FREQ), 0.5 * grad_scale(), False)


def draw_dense_m(key, part):
    key = jax.random.fold_in(key, 14)
    return moment(key, (D + (FLAYERS + 1) * FREQ, FREQ), grad_scale(), False)


def draw_vector_m(key, part):
    key = jax.random.fold_in(key, 15)
    return moment(key, (NVEC,), grad_scale(), False)


def draw_attn_v(key, part):
    key = jax.random.fold_in(key, 21)
    scale = attn_scale()
    return moment(key, (LAYERS, D, 4 * D), scale, True)


def draw_ffn_v(key, part):
    key = jax.random.fold_in(key, 22)
    return moment(key, (LAYERS, 2, D, FF), grad_scale(), True)


def draw_spec_v(key, part):
    key = jax.random.fold_in(key, 23)
    return moment(key, (FLAYERS, MODES, 2, FREQ, FREQ), 0.5 * grad_scale(), True)


def draw_dense_v(key, part):
    key = jax.random.fold_in(key, 24)
    return moment(key, (D + (FLAYERS + 1) * FREQ, FREQ), grad_scale(), True)


def draw_vector_v(key, part):
    key = jax.random.fold_in(key, 25)
    return moment(key, (NVEC,), grad_scale(), True)


def steps_of(own_key, extent, cuts, least, high):
    def one(dim, blocks):
        draws = jax.random.uniform(jax.random.fold_in(jax.random.fold_in(own_key, 6), dim), (blocks,), jnp.float32, least / len(cuts), high / len(cuts))
        return jnp.repeat(jnp.exp(draws), extent[dim] // blocks).reshape((-1,) + (1,) * (len(extent) - dim - 1))

    level = one(*cuts[0])
    for cut in cuts[1:]:
        level = level * one(*cut)
    return level


def scatter_about(key, dims, spread, reach, cuts=(), kind=jnp.bfloat16):
    drawn = spread * jax.random.normal(key, dims, jnp.float32)
    if cuts:
        drawn = drawn * steps_of(key, dims, cuts, -0.22, 0.18)
    return jnp.clip(drawn, -reach, reach).astype(kind)


def setup_inputs(seed: int = 0) -> dict:
    key_of = jax.random.split(jax.random.key(seed), 19)
    samples_in = draw_samples_in(jax.random.fold_in(key_of[18], 71), 0)
    target = scatter_about(key_of[1], (SAMPLES, POINTS), 1.0, 6.0, ((0, 4), (1, 8)), jnp.float32)
    mask = draw_mask(jax.random.fold_in(key_of[18], 71), 0)
    attn_w = scatter_about(key_of[3], (LAYERS, D, 4 * D), D ** -0.5, 0.5, (), jnp.float32)
    ffn_w = scatter_about(key_of[4], (LAYERS, 2, D, FF), D ** -0.5, 0.5, (), jnp.float32)
    spec_w = scatter_about(key_of[5], (FLAYERS, MODES, 2, FREQ, FREQ), (2 * FREQ) ** -0.5, 0.5, (), jnp.float32)
    dense_w = scatter_about(key_of[6], (D + (FLAYERS + 1) * FREQ, FREQ), D ** -0.5, 0.5, (), jnp.float32)
    vectors = draw_vectors(jax.random.fold_in(key_of[18], 71), 0)
    attn_m = draw_attn_m(jax.random.fold_in(key_of[18], 71), 0)
    ffn_m = draw_ffn_m(jax.random.fold_in(key_of[18], 71), 0)
    spec_m = draw_spec_m(jax.random.fold_in(key_of[18], 71), 0)
    dense_m = draw_dense_m(jax.random.fold_in(key_of[18], 71), 0)
    vector_m = draw_vector_m(jax.random.fold_in(key_of[18], 71), 0)
    attn_v = draw_attn_v(jax.random.fold_in(key_of[18], 71), 0)
    ffn_v = draw_ffn_v(jax.random.fold_in(key_of[18], 71), 0)
    spec_v = draw_spec_v(jax.random.fold_in(key_of[18], 71), 0)
    dense_v = draw_dense_v(jax.random.fold_in(key_of[18], 71), 0)
    vector_v = draw_vector_v(jax.random.fold_in(key_of[18], 71), 0)
    return {"samples_in": samples_in, "target": target, "mask": mask, "attn_w": attn_w, "ffn_w": ffn_w, "spec_w": spec_w, "dense_w": dense_w, "vectors": vectors, "attn_m": attn_m, "ffn_m": ffn_m, "spec_m": spec_m, "dense_m": dense_m, "vector_m": vector_m, "attn_v": attn_v, "ffn_v": ffn_v, "spec_v": spec_v, "dense_v": dense_v, "vector_v": vector_v}


HIGH = lax.Precision.HIGHEST
NORM_EPS = 1e-05
BETA_ONE = 0.5
BETA_TWO = 0.5
RATE = 0.2
DECAY = 0.01
ADAM_EPS = 1e-06

@jax.custom_vjp
def low(v):
    return lax.optimization_barrier(v.astype(jnp.bfloat16)).astype(jnp.float32)

@jax.custom_vjp
def low_back(v):
    return v

def low_keep(v):
    return (low(v), None)

def low_pass(kept, grad):
    return (grad,)

def back_keep(v):
    return (v, None)

def back_low(kept, grad):
    return (low(grad),)
low.defvjp(low_keep, low_pass)
low_back.defvjp(back_keep, back_low)

def vector_table():
    entries = [('lift_value', 0, D), ('lift_coord', 0, D), ('lift_bias', 0, D)]
    for layer in range(LAYERS):
        entries = entries + [('key_gain', layer, D), ('value_gain', layer, D), ('inner_bias', layer, FF), ('outer_bias', layer, D)]
    entries = entries + [('proj_bias', 0, FREQ)]
    for layer in range(FLAYERS):
        entries = entries + [('fourier_bias', layer, FREQ)]
    entries = entries + [('head_bias', 0, FREQ), ('head_out', 0, FREQ)]
    offsets = {}
    start = 0
    for label, layer, length in entries:
        offsets[label, layer] = (start, length)
        start = start + length
    return offsets

def pick(vectors, label, layer):
    start, length = vector_table()[label, layer]
    return vectors[start:start + length]

def head_norm(values, gain):
    centred = values - lax.optimization_barrier(jnp.mean(values, -1, keepdims=True))
    scaled = centred * lax.rsqrt(lax.optimization_barrier(jnp.mean(centred * centred, -1, keepdims=True)) + NORM_EPS)
    return scaled * gain.reshape(HEADS, D // HEADS)

def lift(params, inputs):
    vectors = params[4]
    value = inputs[..., 0, :, None]
    coord = inputs[..., 1, :, None]
    return value * pick(vectors, 'lift_value', 0) + coord * pick(vectors, 'lift_coord', 0) + pick(vectors, 'lift_bias', 0)

def attn_front(params, rows, layer, points):
    weight = params[0][layer]
    vectors = params[4]
    mixed = jnp.einsum('...d,de->...e', rows, weight[:, :3 * D], precision=HIGH)
    shape = rows.shape[:-1] + (HEADS, D // HEADS)
    query = mixed[..., :D].reshape(shape)
    keys = head_norm(mixed[..., D:2 * D].reshape(shape), pick(vectors, 'key_gain', layer))
    values = head_norm(mixed[..., 2 * D:].reshape(shape), pick(vectors, 'value_gain', layer))
    partial_sum = jnp.einsum('...phe,...phf->...hef', keys, values, precision=HIGH) / points
    return (query, partial_sum)

def attn_rear(params, rows, query, summary, layer):
    weight = params[0][layer]
    attended = jnp.einsum('...phe,...hef->...phf', query, summary, precision=HIGH).reshape(rows.shape)
    return rows + jnp.einsum('...d,de->...e', attended, weight[:, 3 * D:], precision=HIGH)

def ffn_block(params, rows, layer):
    weight = params[1][layer]
    vectors = params[4]
    inner = jnp.einsum('...d,df->...f', rows, weight[0], precision=HIGH) + pick(vectors, 'inner_bias', layer)
    outer = jnp.einsum('...f,df->...d', jax.nn.gelu(inner), weight[1], precision=HIGH)
    return rows + outer + pick(vectors, 'outer_bias', layer)

def project(params, rows):
    return jnp.einsum('...d,df->...f', rows, params[3][:D], precision=HIGH) + pick(params[4], 'proj_bias', 0)

def mode_table(count, first, total):
    position = first + jnp.arange(count, dtype=jnp.int32)
    orders = jnp.arange(MODES, dtype=jnp.int32)
    phase = orders[:, None] * position[None, :] % total
    angle = phase.astype(jnp.float32) * (2.0 * math.pi / total)
    return jnp.concatenate([jnp.cos(angle), jnp.sin(angle)], 0)

def spectral_mix(coef, spec, first, width):
    columns = lax.dynamic_slice_in_dim(spec, first, width, 3)
    cosine = coef[..., :MODES, :]
    sine = coef[..., MODES:, :]
    real_part = columns[:, 0]
    imag_part = columns[:, 1]
    mixed_cos = jnp.einsum('...mf,mfg->...mg', cosine, real_part, precision=HIGH) + jnp.einsum('...mf,mfg->...mg', sine, imag_part, precision=HIGH)
    mixed_sin = jnp.einsum('...mf,mfg->...mg', sine, real_part, precision=HIGH) - jnp.einsum('...mf,mfg->...mg', cosine, imag_part, precision=HIGH)
    return jnp.concatenate([mixed_cos, mixed_sin], -2)

def fourier_end(params, back, rows, layer):
    local = params[3][D + layer * FREQ:D + (layer + 1) * FREQ]
    inner = back + jnp.einsum('...f,fg->...g', rows, local, precision=HIGH)
    return jax.nn.gelu(inner + pick(params[4], 'fourier_bias', layer))

def head_loss(params, rows, target, mask_f):
    start = D + FLAYERS * FREQ
    hidden = jax.nn.gelu(jnp.einsum('...f,fg->...g', rows, params[3][start:start + FREQ], precision=HIGH) + pick(params[4], 'head_bias', 0))
    pred = jnp.einsum('...f,f->...', hidden, pick(params[4], 'head_out', 0), precision=HIGH)
    diff = pred - target
    return jnp.sum(mask_f * diff * diff)

def sample_loss(params, inputs, target, mask_f, grid):
    rows = lift(params, inputs)
    for layer in range(LAYERS):
        query, summary = attn_front(params, rows, layer, POINTS)
        rows = ffn_block(params, attn_rear(params, rows, query, summary, layer), layer)
    field = project(params, rows)
    for layer in range(FLAYERS):
        coef = jnp.einsum('kp,pc->kc', grid, field, precision=HIGH) / math.sqrt(POINTS)
        mixed = spectral_mix(coef, params[2][layer], 0, FREQ)
        back = jnp.einsum('kp,kc->pc', grid, mixed, precision=HIGH) / math.sqrt(MODES)
        field = fourier_end(params, back, field, layer)
    return head_loss(params, field, target, mask_f)

def lamb(weight, grad, first, second):
    first_new = BETA_ONE * first + (1.0 - BETA_ONE) * grad
    second_new = BETA_TWO * second + (1.0 - BETA_TWO) * grad * grad
    update = first_new / (1.0 - BETA_ONE ** STEP) / (jnp.sqrt(second_new / (1.0 - BETA_TWO ** STEP)) + ADAM_EPS) + DECAY * weight
    return (first_new, second_new, update)

def trust_step(weight, update, stacked):
    axes = tuple(range(1, weight.ndim)) if stacked else tuple(range(weight.ndim))
    weight_norm = jnp.sqrt(lax.optimization_barrier(jnp.sum(weight * weight, axes)))
    update_norm = jnp.sqrt(lax.optimization_barrier(jnp.sum(update * update, axes)))
    ratio = weight_norm / (update_norm + ADAM_EPS)
    scale = ratio.reshape(ratio.shape + (1,) * (weight.ndim - ratio.ndim))
    return (weight - RATE * scale * update, jnp.atleast_1d(weight_norm), jnp.atleast_1d(update_norm), jnp.atleast_1d(ratio))

def finish(loss_sum, valid_count, params, grads, firsts, seconds):
    results = [loss_sum, valid_count]
    weight_norms, update_norms, ratios = ([], [], [])
    for weight, grad, first, second, stacked in zip(params, grads, firsts, seconds, (True, True, True, False, False)):
        first_new, second_new, update = lamb(weight, grad, first, second)
        fresh, weight_norm, update_norm, ratio = trust_step(weight, update, stacked)
        results = results + [first_new, second_new, fresh, fresh.astype(jnp.bfloat16)]
        weight_norms.append(weight_norm)
        update_norms.append(update_norm)
        ratios.append(ratio)
    return results + [jnp.concatenate(weight_norms), jnp.concatenate(update_norms), jnp.concatenate(ratios)]

def reference(samples_in, target, mask, attn_w, ffn_w, spec_w, dense_w, vectors, attn_m, ffn_m, spec_m, dense_m, vector_m, attn_v, ffn_v, spec_v, dense_v, vector_v):
    mask_f = mask.astype(jnp.float32)
    valid_count = jnp.sum(mask_f)
    params = (attn_w, ffn_w, spec_w, dense_w, vectors)
    grid = mode_table(POINTS, 0, POINTS)
    per_sample = jax.checkpoint(sample_loss)

    def total_loss(weights):

        def one_sample(carry, item):
            return (carry + per_sample(weights, item[0], item[1], item[2], grid), None)
        summed, _ = lax.scan(one_sample, jnp.zeros((), jnp.float32), (samples_in, target, mask_f))
        return summed
    loss_sum, pullback = jax.vjp(total_loss, params)
    grads = pullback(1.0 / valid_count)[0]
    out = finish(loss_sum, valid_count, params, grads, (attn_m, ffn_m, spec_m, dense_m, vector_m), (attn_v, ffn_v, spec_v, dense_v, vector_v))
    return (out[0], out[1], out[2], out[3], out[4], out[5], out[6], out[7], out[8], out[9], out[10], out[11], out[12], out[13], out[14], out[15], out[16], out[17], out[18], out[19], out[20], out[21], out[22], out[23], out[24])
```

```python
import math

import jax
import jax.numpy as jnp
import ml_dtypes
import numpy as np
from jax import lax
from jax.experimental import pallas as pl
from jax.experimental.pallas import tpu as pltpu
from jax.sharding import PartitionSpec as P

D = 128
HEADS = 4
FF = 256
FREQ = 64
MODES = 16
LAYERS = 2
FLAYERS = 2
STEP = 5


HIGH = lax.Precision.HIGHEST
NORM_EPS = 1e-05
BETA_ONE = 0.5
BETA_TWO = 0.5
RATE = 0.2
DECAY = 0.01
ADAM_EPS = 1e-06


def vector_table():
    entries = [("lift_value", 0, D), ("lift_coord", 0, D), ("lift_bias", 0, D)]
    for layer in range(LAYERS):
        entries = entries + [
            ("key_gain", layer, D),
            ("value_gain", layer, D),
            ("inner_bias", layer, FF),
            ("outer_bias", layer, D),
        ]
    entries = entries + [("proj_bias", 0, FREQ)]
    for layer in range(FLAYERS):
        entries = entries + [("fourier_bias", layer, FREQ)]
    entries = entries + [("head_bias", 0, FREQ), ("head_out", 0, FREQ)]
    offsets = {}
    start = 0
    for label, layer, length in entries:
        offsets[label, layer] = (start, length)
        start = start + length
    return offsets


def pick(vectors, label, layer):
    start, length = vector_table()[label, layer]
    return vectors[start : start + length]


def head_norm(values, gain):
    centred = values - jnp.mean(values, -1, keepdims=True)
    scaled = centred * lax.rsqrt(jnp.mean(centred * centred, -1, keepdims=True) + NORM_EPS)
    return scaled * gain.reshape(HEADS, D // HEADS)


def lift(params, inputs):
    vectors = params[4]
    value = inputs[..., 0, :, None]
    coord = inputs[..., 1, :, None]
    return (
        value * pick(vectors, "lift_value", 0)
        + coord * pick(vectors, "lift_coord", 0)
        + pick(vectors, "lift_bias", 0)
    )


def attn_front(params, rows, layer, points):
    weight = params[0][layer]
    vectors = params[4]
    mixed = jnp.einsum("...d,de->...e", rows, weight[:, : 3 * D], precision=HIGH)
    shape = rows.shape[:-1] + (HEADS, D // HEADS)
    query = mixed[..., :D].reshape(shape)
    keys = head_norm(mixed[..., D : 2 * D].reshape(shape), pick(vectors, "key_gain", layer))
    values = head_norm(mixed[..., 2 * D :].reshape(shape), pick(vectors, "value_gain", layer))
    partial_sum = jnp.einsum("...phe,...phf->...hef", keys, values, precision=HIGH) / points
    return (query, partial_sum)


def attn_rear(params, rows, query, summary, layer):
    weight = params[0][layer]
    attended = jnp.einsum("...phe,...hef->...phf", query, summary, precision=HIGH).reshape(
        rows.shape
    )
    return rows + jnp.einsum("...d,de->...e", attended, weight[:, 3 * D :], precision=HIGH)


def ffn_block(params, rows, layer):
    weight = params[1][layer]
    vectors = params[4]
    inner = jnp.einsum("...d,df->...f", rows, weight[0], precision=HIGH) + pick(
        vectors, "inner_bias", layer
    )
    outer = jnp.einsum("...f,df->...d", jax.nn.gelu(inner), weight[1], precision=HIGH)
    return rows + outer + pick(vectors, "outer_bias", layer)


def project(params, rows):
    return jnp.einsum("...d,df->...f", rows, params[3][:D], precision=HIGH) + pick(
        params[4], "proj_bias", 0
    )


def mode_table(count, total):
    position = jnp.arange(count, dtype=jnp.int32)
    orders = jnp.arange(MODES, dtype=jnp.int32)
    phase = orders[:, None] * position[None, :] % total
    angle = phase.astype(jnp.float32) * (2.0 * math.pi / total)
    return jnp.concatenate([jnp.cos(angle), jnp.sin(angle)], 0)


def spectral_mix(coef, spec, first, width):
    columns = lax.dynamic_slice_in_dim(spec, first, width, 3)
    cosine = coef[..., :MODES, :]
    sine = coef[..., MODES:, :]
    real_part = columns[:, 0]
    imag_part = columns[:, 1]
    mixed_cos = jnp.einsum("...mf,mfg->...mg", cosine, real_part, precision=HIGH) + jnp.einsum(
        "...mf,mfg->...mg", sine, imag_part, precision=HIGH
    )
    mixed_sin = jnp.einsum("...mf,mfg->...mg", sine, real_part, precision=HIGH) - jnp.einsum(
        "...mf,mfg->...mg", cosine, imag_part, precision=HIGH
    )
    return jnp.concatenate([mixed_cos, mixed_sin], -2)


def fourier_end(params, back, rows, layer):
    local = params[3][D + layer * FREQ : D + (layer + 1) * FREQ]
    inner = back + jnp.einsum("...f,fg->...g", rows, local, precision=HIGH)
    return jax.nn.gelu(inner + pick(params[4], "fourier_bias", layer))


def head_loss(params, rows, target, mask_f):
    start = D + FLAYERS * FREQ
    hidden = jax.nn.gelu(
        jnp.einsum("...f,fg->...g", rows, params[3][start : start + FREQ], precision=HIGH)
        + pick(params[4], "head_bias", 0)
    )
    pred = jnp.einsum("...f,f->...", hidden, pick(params[4], "head_out", 0), precision=HIGH)
    diff = pred - target
    return jnp.sum(mask_f * diff * diff)


def add_all(first, second):
    return jax.tree.map(jnp.add, first, second)


def spectral_setup(points, parts):
    width = FREQ // parts
    return (mode_table(points, points), lax.axis_index("pts") * width, width, points)


def fourier_mix(spec, field, setup):
    grid, column, width, points = setup
    channel_rows = lax.all_to_all(field, "pts", split_axis=2, concat_axis=1, tiled=True)
    own_coef = jnp.einsum("kp,spc->skc", grid, channel_rows, precision=HIGH) / math.sqrt(points)
    full = lax.all_gather(own_coef, "pts", axis=2, tiled=True)
    mixed = spectral_mix(full, spec, column, width)
    spread = jnp.einsum("kp,skc->spc", grid, mixed, precision=HIGH) / math.sqrt(MODES)
    back = lax.all_to_all(spread, "pts", split_axis=1, concat_axis=2, tiled=True)
    return (back, full)


def fourier_back(params, grad_out, kept_item, layer, setup):
    field, full, back = kept_item
    grid, column, width, points = setup
    _, end_pull = jax.vjp(
        lambda weights, spread, inner: fourier_end(weights, spread, inner, layer),
        params,
        back,
        field,
    )
    grads, grad_back, grad_field = end_pull(grad_out)
    _, mix_pull = jax.vjp(
        lambda coef, weight: spectral_mix(coef, weight, column, width), full, params[2][layer]
    )
    grad_rows = lax.all_to_all(grad_back, "pts", split_axis=2, concat_axis=1, tiled=True)
    grad_mixed = jnp.einsum("kp,spc->skc", grid, grad_rows, precision=HIGH) / math.sqrt(MODES)
    grad_full, grad_spec = mix_pull(grad_mixed)
    grad_coef = lax.psum_scatter(grad_full, "pts", scatter_dimension=2, tiled=True)
    grad_chan = jnp.einsum("kp,skc->spc", grid, grad_coef, precision=HIGH) / math.sqrt(points)
    grad_field = grad_field + lax.all_to_all(
        grad_chan, "pts", split_axis=1, concat_axis=2, tiled=True
    )
    grads = (grads[0], grads[1], grads[2].at[layer].add(grad_spec), grads[3], grads[4])
    return (grads, grad_field)


def attention_back(params, grad_rows, kept_item, layer, points):
    rows, summary = kept_item
    (query, partial_sum), front_pull = jax.vjp(
        lambda weights, inner: attn_front(weights, inner, layer, points), params, rows
    )
    summary = lax.psum(partial_sum, "pts")
    middle, rear_pull = jax.vjp(
        lambda weights, inner, asked, summed: attn_rear(weights, inner, asked, summed, layer),
        params,
        rows,
        query,
        summary,
    )
    _, ffn_pull = jax.vjp(lambda weights, inner: ffn_block(weights, inner, layer), params, middle)
    ffn_grads, grad_middle = ffn_pull(grad_rows)
    rear_grads, grad_direct, grad_query, grad_summary = rear_pull(grad_middle)
    grad_summary = lax.psum(grad_summary, "pts")
    front_grads, grad_front = front_pull((grad_query, grad_summary))
    return (add_all(add_all(ffn_grads, rear_grads), front_grads), grad_direct + grad_front)


def lamb(weight, grad, first, second):
    first_new = BETA_ONE * first + (1.0 - BETA_ONE) * grad
    second_new = BETA_TWO * second + (1.0 - BETA_TWO) * grad * grad
    update = (
        first_new
        / (1.0 - BETA_ONE**STEP)
        / (jnp.sqrt(second_new / (1.0 - BETA_TWO**STEP)) + ADAM_EPS)
        + DECAY * weight
    )
    return (first_new, second_new, update)


def trust_step(weight, update, stacked):
    axes = tuple(range(1, weight.ndim)) if stacked else tuple(range(weight.ndim))
    weight_norm = jnp.sqrt(jnp.sum(weight * weight, axes))
    update_norm = jnp.sqrt(jnp.sum(update * update, axes))
    ratio = weight_norm / (update_norm + ADAM_EPS)
    scale = ratio.reshape(ratio.shape + (1,) * (weight.ndim - ratio.ndim))
    return (
        weight - RATE * scale * update,
        jnp.atleast_1d(weight_norm),
        jnp.atleast_1d(update_norm),
        jnp.atleast_1d(ratio),
    )


def finish(loss_sum, valid_count, params, grads, firsts, seconds):
    results = [loss_sum, valid_count]
    weight_norms, update_norms, ratios = ([], [], [])
    for weight, grad, first, second, stacked in zip(
        params, grads, firsts, seconds, (True, True, True, False, False)
    ):
        first_new, second_new, update = lamb(weight, grad, first, second)
        fresh, weight_norm, update_norm, ratio = trust_step(weight, update, stacked)
        results = results + [first_new, second_new, fresh, fresh.astype(jnp.bfloat16)]
        weight_norms.append(weight_norm)
        update_norms.append(update_norm)
        ratios.append(ratio)
    return results + [
        jnp.concatenate(weight_norms),
        jnp.concatenate(update_norms),
        jnp.concatenate(ratios),
    ]


def body(
    samples_in,
    target,
    mask,
    attn_w,
    ffn_w,
    spec_w,
    dense_w,
    vectors,
    attn_m,
    ffn_m,
    spec_m,
    dense_m,
    vector_m,
    attn_v,
    ffn_v,
    spec_v,
    dense_v,
    vector_v,
):
    params = (attn_w, ffn_w, spec_w, dense_w, vectors)
    parts = lax.axis_size("pts")
    local_pts = samples_in.shape[2]
    points = local_pts * parts
    mask_f = mask.astype(jnp.float32)
    valid_count = lax.psum(jnp.sum(mask_f), ("dp", "pts"))
    setup = spectral_setup(points, parts)
    rows, lift_pull = jax.vjp(lambda weights: lift(weights, samples_in), params)
    kept = []
    for layer in range(LAYERS):
        query, partial_sum = attn_front(params, rows, layer, points)
        summary = lax.psum(partial_sum, "pts")
        kept.append((rows, summary))
        rows = ffn_block(params, attn_rear(params, rows, query, summary, layer), layer)
    field, proj_pull = jax.vjp(project, params, rows)
    spectral_kept = []
    for layer in range(FLAYERS):
        back, full = fourier_mix(params[2][layer], field, setup)
        spectral_kept.append((field, full, back))
        field = fourier_end(params, back, field, layer)
    loss_part, head_pull = jax.vjp(
        lambda weights, inner: head_loss(weights, inner, target, mask_f), params, field
    )
    grads, grad_field = head_pull(1.0 / valid_count)
    for layer in reversed(range(FLAYERS)):
        layer_grads, grad_field = fourier_back(
            params, grad_field, spectral_kept[layer], layer, setup
        )
        grads = add_all(grads, layer_grads)
    proj_grads, grad_rows = proj_pull(grad_field)
    grads = add_all(grads, proj_grads)
    for layer in reversed(range(LAYERS)):
        layer_grads, grad_rows = attention_back(params, grad_rows, kept[layer], layer, points)
        grads = add_all(grads, layer_grads)
    grads = add_all(grads, lift_pull(grad_rows)[0])
    summed = lax.psum((grads[0], grads[1], grads[2], grads[3], grads[4], loss_part), ("dp", "pts"))
    out = finish(
        summed[5],
        valid_count,
        params,
        summed[:5],
        (attn_m, ffn_m, spec_m, dense_m, vector_m),
        (attn_v, ffn_v, spec_v, dense_v, vector_v),
    )
    return (
        out[0],
        out[1],
        out[2],
        out[3],
        out[4],
        out[5],
        out[6],
        out[7],
        out[8],
        out[9],
        out[10],
        out[11],
        out[12],
        out[13],
        out[14],
        out[15],
        out[16],
        out[17],
        out[18],
        out[19],
        out[20],
        out[21],
        out[22],
        out[23],
        out[24],
    )


F32 = jnp.float32
BF16 = jnp.bfloat16
ROWS = 512


def dot(first, second, left=1, right=0, precision=None):
    return lax.dot_general(
        first,
        second,
        (((left,), (right,)), ((), ())),
        precision=precision,
        preferred_element_type=F32,
    )


def exact(first, second, left=1, right=0):
    return dot(first, second, left, right, HIGH)


def halves(value):
    high = value.astype(BF16)
    return high, (value - high.astype(F32)).astype(BF16)


def thirds(value):
    high = value.astype(BF16)
    rest = value - high.astype(F32)
    middle = rest.astype(BF16)
    return high, middle, (rest - middle.astype(F32)).astype(BF16)


def beside(*pieces):
    return jnp.concatenate(pieces, 1)


def above(*pieces):
    return jnp.concatenate(pieces, 0)


def fold(value):
    half = value.shape[1] // 2
    return value[:, :half] + value[:, half:]


def column_sum(value):
    rows, width = value.shape
    return jnp.sum(value.reshape(rows // 8, 8, width), 0)


def gelu_pair(inner):
    scale = math.sqrt(2.0 / math.pi)
    square = inner * inner
    bend = jnp.tanh(inner * (scale + (scale * 0.044715) * square))
    half = 0.5 + 0.5 * bend
    slope = half + (0.5 * inner) * (1.0 - bend * bend) * (scale + (3.0 * scale * 0.044715) * square)
    return inner * half, slope


def wide6_weight(weight):
    high, middle, low = thirds(weight)
    return above(high, high, middle, middle, low, high)


def wide6(pieces, weight):
    high, middle, low = pieces
    return dot(beside(high, middle, high, middle, high, low), weight)


def tall6_weight(weight):
    high, middle, low = thirds(weight)
    pair = beside(high, middle)
    return above(pair, pair), above(low, high)


def tall6(pieces, weights):
    high, middle, low = pieces
    return fold(dot(beside(high, middle), weights[0])) + dot(beside(high, low), weights[1])


def wide4_weight(weight):
    high, low = halves(weight)
    return above(high, high, low, low)


def wide4(pieces, weight):
    high, low = pieces
    return dot(beside(high, low, high, low), weight)


def tall4_weight(weight):
    high, low = halves(weight)
    pair = beside(high, low)
    return above(pair, pair)


def tall4(pieces, weight):
    return fold(dot(beside(*pieces), weight))


def head_blocks(width):
    row = lax.broadcasted_iota(jnp.int32, (width, width), 0)
    column = lax.broadcasted_iota(jnp.int32, (width, width), 1)
    return row // (D // HEADS) == column // (D // HEADS)


def doubled(weight):
    zero = jnp.zeros_like(weight)
    return above(beside(weight, zero), beside(zero, weight))


def local_kernel(
    inputs_ref,
    attn_ref,
    ffn_ref,
    spec_ref,
    dense_ref,
    vec_ref,
    table_ref,
    trow_ref,
    g_attn,
    g_ffn,
    g_spec,
    g_dense,
    g_vec,
    g_loss,
    lifted,
    lrows,
    w_kv,
    w_kvt,
    w_in,
    w_int,
    w0_u,
    mid_rows,
    w_out0,
    w_out1,
    w_outt,
    x_keep,
    r_keep,
    slope_keep,
    act_keep,
    mid_keep,
    h1_keep,
    h2_keep,
    z_keep,
    zs_keep,
    e_keep,
    s_acc,
    w0_kv,
    w0_g,
    n_keep,
    small_keep,
    nt_keep,
    cent_keep,
    coef_acc,
    coef_keep,
    stack_ref,
    sq_acc,
    p_acc,
    y_acc,
    w2_acc,
    w1_acc,
    kv_acc,
    v_acc,
    u_acc,
    vt_acc,
    b_acc,
    d_keep,
    t_keep,
    wz,
):
    count, points = inputs_ref.shape[0], inputs_ref.shape[2]
    total = count * points
    steps = points // ROWS
    rows_all = total // ROWS
    blocks = head_blocks(D)
    block_f = jnp.where(blocks, 1.0, 0.0).astype(F32)
    block_b = block_f.astype(BF16)
    mean_weight = above(block_b, block_b)
    centre = (
        jnp.where(
            lax.broadcasted_iota(jnp.int32, (D, D), 0) == lax.broadcasted_iota(jnp.int32, (D, D), 1),
            1.0,
            0.0,
        ).astype(F32)
        - block_f * (HEADS / D)
    )
    eye = jnp.where(
        lax.broadcasted_iota(jnp.int32, (D, D), 0) == lax.broadcasted_iota(jnp.int32, (D, D), 1), 1.0, 0.0
    ).astype(F32)

    def vector(label, layer):
        start, length = vector_table()[label, layer]
        if length == 2 * D:
            row = start // D
            return beside(vec_ref[row : row + 1, :], vec_ref[row + 1 : row + 2, :])
        row = start // D
        if length == D:
            return vec_ref[row : row + 1, :]
        offset = start - row * D
        piece = vec_ref[row : row + 1, offset : offset + FREQ]
        return beside(piece, piece)

    def block(index):
        return pl.ds(pl.multiple_of(index * ROWS, ROWS), ROWS)

    for s in range(count):
        data = inputs_ref[s]
        value, coord, target, valid = data[0:1], data[1:2], data[2:3], data[3:4]
        one = jnp.ones_like(value)
        vh, vm, vl = [item.astype(F32) for item in thirds(value)]
        ch, cm, cl = [item.astype(F32) for item in thirds(coord)]
        th, tm, tl = [item.astype(F32) for item in thirds(target)]
        zero = jnp.zeros((D - 19, points), F32)
        stack = above(vh, vm, vh, vm, vh, vl, ch, cm, ch, cm, ch, cl, one, one, one, th, tm, tl, valid, zero)
        lifted[s * points : (s + 1) * points, :] = stack.T.astype(BF16)
        short = above(vh, vm, vl, ch, cm, cl, one, jnp.zeros((9, points), F32)).astype(BF16)
        for i in range(steps):
            lrows[s * steps + i] = short[:, i * ROWS : (i + 1) * ROWS]

    lift_rows = above(
        vector("lift_value", 0), vector("lift_coord", 0), vector("lift_bias", 0), jnp.zeros((5, D), F32)
    )

    def lift_weight(mixed):
        high, middle, low = [item.astype(F32) for item in thirds(mixed)]
        parts = []
        for i in range(2):
            hi, mi, lo = high[i : i + 1], middle[i : i + 1], low[i : i + 1]
            parts += [hi, hi, mi, mi, lo, hi]
        parts += [high[2:3], middle[2:3], low[2:3]]
        parts.append(jnp.zeros((D - 15, mixed.shape[1]), F32))
        return above(*parts).astype(BF16)

    for layer in range(LAYERS):
        weight = attn_ref[layer]
        keyed = beside(exact(weight[:, D : 2 * D], centre), exact(weight[:, 2 * D : 3 * D], centre))
        cent_keep[layer] = keyed
        if layer == 0:
            w0_kv[...] = lift_weight(exact(lift_rows, keyed))
        else:
            w_kv[...] = wide6_weight(keyed)
            w_kvt[...] = tall4_weight(keyed.T)
        first, second = ffn_ref[layer, 0], ffn_ref[layer, 1]
        if layer:
            w_in[...] = wide6_weight(first)
            w_int[...] = tall4_weight(first.T)
        pair, rest = tall6_weight(second.T)
        w_out0[layer] = pair
        w_out1[layer] = rest
        w_outt[layer] = wide4_weight(second)

    s_acc[...] = jnp.zeros_like(s_acc)
    coef_acc[...] = jnp.zeros_like(coef_acc)
    sq_acc[...] = jnp.zeros_like(sq_acc)
    p_acc[...] = jnp.zeros_like(p_acc)
    y_acc[...] = jnp.zeros_like(y_acc)
    w2_acc[...] = jnp.zeros_like(w2_acc)
    w1_acc[...] = jnp.zeros_like(w1_acc)
    kv_acc[...] = jnp.zeros_like(kv_acc)
    v_acc[...] = jnp.zeros_like(v_acc)
    u_acc[...] = jnp.zeros_like(u_acc)
    vt_acc[...] = jnp.zeros_like(vt_acc)
    b_acc[...] = jnp.zeros_like(b_acc)

    def head_scale(centred):
        high, low = halves(centred * centred)
        var = beside(
            dot(beside(high[:, :D], low[:, :D]), mean_weight), dot(beside(high[:, D:], low[:, D:]), mean_weight)
        )
        return lax.rsqrt(var * (HEADS / D) + NORM_EPS)

    def normalise(layer, index, centred):
        scale = head_scale(centred)
        normal = centred * scale
        if layer:
            where = block(index)
            x_keep[where, :] = normal
            r_keep[where, :] = scale
        high, low = halves(normal)
        s_acc[layer, index // steps] += dot(
            beside(high[:, :D], low[:, :D]), beside(high[:, D:], low[:, D:]), 0, 0
        )

    def quarters(value):
        half_row, half_col = value.shape[0] // 2, value.shape[1] // 2
        return (
            value[:half_row, :half_col]
            + value[half_row:, :half_col]
            + (value[:half_row, half_col:] + value[half_row:, half_col:])
        )

    def summarise(layer):
        weight = attn_ref[layer]
        key_gain = vector("key_gain", layer).reshape(1, D)
        value_gain = vector("value_gain", layer).reshape(1, D)
        key_column = jnp.sum(eye * key_gain, 1, keepdims=True)
        for s in range(count):
            plain = jnp.where(blocks, quarters(s_acc[layer, s]), 0.0) * (1.0 / points)
            summary = key_column * plain * value_gain
            mixed = exact(summary, weight[:, 3 * D :])
            both = exact(weight[:, :D], mixed)
            n_keep[layer, s] = both
            small_keep[layer, s, 0] = plain
            small_keep[layer, s, 1] = summary
            small_keep[layer, s, 2] = mixed
            if layer == 0:
                rows = exact(lift_rows, eye + both)
                mid_rows[s] = rows
                w0_g[s] = lift_weight(rows)
                w0_u[s] = lift_weight(exact(rows, ffn_ref[0, 0]))
            else:
                pair, rest = tall6_weight(both)
                wz[s, : 2 * D, :] = pair
                wz[s, 2 * D :, :D] = rest
                nt_keep[s] = tall4_weight(both.T)

    def feed(layer, index, mid, inner):
        where = block(index)
        act, slope = gelu_pair(inner + vector("inner_bias", layer))
        slope_keep[layer, where, :] = slope
        pieces = thirds(act)
        act_keep[layer, where, :] = beside(pieces[0], pieces[1])
        return mid + tall6(pieces, (w_out0[layer], w_out1[layer])) + vector("outer_bias", layer)

    def front_zero(index, _):
        normalise(0, index, dot(lifted[block(index), :], w0_kv[...]))
        return 0

    lax.fori_loop(0, rows_all, front_zero, 0)
    summarise(0)

    def layer_zero(index, _):
        where = block(index)
        s = index // steps
        data = lifted[where, :]
        out = feed(0, index, dot(data, w0_g[s]), dot(data, w0_u[s]))
        d_keep[where, :] = out
        pieces = thirds(out)
        h1_keep[where, :] = beside(*pieces)
        normalise(1, index, wide6(pieces, w_kv[...]))
        return 0

    lax.fori_loop(0, rows_all, layer_zero, 0)
    summarise(1)

    def pieces_of(ref, where, number=3):
        value = ref[where, : number * D]
        return [value[:, i * D : (i + 1) * D] for i in range(number)]

    def layer_one(index, _):
        where = block(index)
        s = index // steps
        pieces = pieces_of(h1_keep, where)
        mid = d_keep[where, :] + tall6(pieces, (wz[s, : 2 * D, :], wz[s, 2 * D :, :D]))
        pieces = thirds(mid)
        mid_keep[where, :] = beside(pieces[0], pieces[1])
        out = feed(1, index, mid, wide6(pieces, w_in[...]))
        h2_keep[where, :] = beside(*thirds(out))
        return 0

    lax.fori_loop(0, rows_all, layer_one, 0)

    def dense_rows(part):
        start = D + (part - 1) * FREQ if part else 0
        return dense_ref[start : start + (FREQ if part else D), :]

    proj0, proj1 = tall6_weight(doubled(dense_rows(0)))
    locals6 = [tall6_weight(doubled(dense_rows(part))) for part in (1, 2, 3)]
    locals4 = [tall4_weight(doubled(dense_rows(part).T)) for part in (1, 2, 3)]
    own = lax.broadcasted_iota(jnp.int32, (2 * count * MODES, MODES * D), 1) // D == lax.rem(
        lax.broadcasted_iota(jnp.int32, (2 * count * MODES, MODES * D), 0), MODES
    )

    def mode_rows(coef):
        cosine, sine = coef[:MODES], coef[MODES:]
        c = [cosine[:, s * FREQ : (s + 1) * FREQ] for s in range(count)]
        d = [sine[:, s * FREQ : (s + 1) * FREQ] for s in range(count)]
        return above(
            *[beside(c[s], d[s]) for s in range(count)], *[beside(d[s], -c[s]) for s in range(count)]
        )

    def spread_rows(rows):
        return jnp.where(own, beside(*([rows] * MODES)), 0.0)

    def unpack(rows):
        lead = count * MODES
        return above(
            *[beside(*[rows[j * lead + s * MODES : j * lead + (s + 1) * MODES] for s in range(count)]) for j in (0, 1)]
        )

    def pack(value):
        return above(
            *[
                value[j * MODES : (j + 1) * MODES, s * FREQ : (s + 1) * FREQ]
                for j in (0, 1)
                for s in range(count)
            ]
        )

    def set_stack(value):
        high, middle, low = thirds(value)
        stack_ref[...] = above(
            high, high, middle, middle, low, high, jnp.zeros((4 * MODES, D), BF16)
        )

    def take_coef(index, high, low):
        coef_acc[...] += dot(trow_ref[index], beside(high, low))

    def mix_forward(layer):
        coef = quarters(coef_acc[...]) * (1.0 / math.sqrt(points))
        coef_acc[...] = jnp.zeros_like(coef_acc)
        rows = mode_rows(coef)
        coef_keep[layer] = rows
        set_stack(unpack(exact(spread_rows(rows), spec_ref[layer])) * (1.0 / math.sqrt(MODES)))

    def mix_back(layer):
        cot = pack(quarters(coef_acc[...])) * (1.0 / math.sqrt(MODES))
        coef_acc[...] = jnp.zeros_like(coef_acc)
        g_spec[layer] = exact(spread_rows(coef_keep[layer]), cot, 0, 0)
        wide = jnp.where(own, exact(cot, spec_ref[layer], 1, 1), 0.0)
        kept = wide[:, :D]
        for k in range(1, MODES):
            kept = kept + wide[:, k * D : (k + 1) * D]
        lead = count * MODES
        first, second = kept[:lead], kept[lead:]
        rows = above(first[:, :FREQ] - second[:, FREQ:], first[:, FREQ:] + second[:, :FREQ])
        set_stack(unpack(rows) * (1.0 / math.sqrt(points)))

    def project_step(index, _):
        where = block(index)
        first = h2_keep[block(index), :]
        second = h2_keep[block(index + steps), :]
        pieces = [beside(first[:, i * D : (i + 1) * D], second[:, i * D : (i + 1) * D]) for i in range(3)]
        field = tall6(pieces, (proj0, proj1)) + vector("proj_bias", 0)
        pieces = thirds(field)
        z_keep[0, where, :] = beside(*pieces)
        take_coef(index, pieces[0], pieces[1])
        return 0

    lax.fori_loop(0, steps, project_step, 0)
    mix_forward(0)

    def fourier_field(layer, where):
        pieces = pieces_of(z_keep.at[layer], where)
        inner = dot(table_ref[where, :], stack_ref[...]) + (
            tall6(pieces, locals6[layer]) + vector("fourier_bias", layer)
        )
        return gelu_pair(inner)

    def fourier_one(index, _):
        where = block(index)
        field, slope = fourier_field(0, where)
        zs_keep[where, :] = slope
        pieces = thirds(field)
        z_keep[1, where, :] = beside(*pieces)
        take_coef(index, pieces[0], pieces[1])
        return 0

    lax.fori_loop(0, steps, fourier_one, 0)
    mix_forward(1)

    lane = lax.broadcasted_iota(jnp.int32, (2 * D, 2 * D), 1)
    row = lax.broadcasted_iota(jnp.int32, (2 * D, 2 * D), 0)
    inner_row = lax.rem(row, D)
    same = row // D == lax.rem(lane, D) // FREQ
    pick_target = (lane < D) & (inner_row >= 15) & (inner_row < 18)
    pick_mask = (lane >= D) & (inner_row == 18)
    spread = jnp.where(same & (pick_target | pick_mask), 1.0, 0.0).astype(BF16)
    out_row = vector("head_out", 0)
    out_column = jnp.sum(eye * out_row, 1, keepdims=True)
    half_blocks = (
        lax.broadcasted_iota(jnp.int32, (D, D), 0) // FREQ == lax.broadcasted_iota(jnp.int32, (D, D), 1) // FREQ
    )
    out_weight = tall6_weight(jnp.where(half_blocks, out_column, 0.0))

    def pair_product(first, second):
        return dot(beside(*first), beside(*second), 0, 0)

    def loss_step(index, _):
        where = block(index)
        field, slope = fourier_field(1, where)
        pieces = thirds(field)
        hidden, hidden_slope = gelu_pair(tall6(pieces, locals6[2]) + vector("head_bias", 0))
        pred = tall6(thirds(hidden), out_weight)
        known = dot(beside(lifted[where, :], lifted[block(index + steps), :]), spread)
        diff = pred - known[:, :D]
        valid = known[:, D:]
        cot = (2.0 * valid) * diff
        b_acc[0:8, :D] += column_sum(valid * diff * diff)
        b_acc[8:16, :D] += column_sum(valid)
        b_acc[16:24, :D] += column_sum(hidden * cot)
        cot = cot * out_row * hidden_slope
        b_acc[24:32, :D] += column_sum(cot)
        split = halves(cot)
        sq_acc[2] += pair_product(pieces[:2], split)
        cot = tall4(split, locals4[2]) * slope
        b_acc[32:40, :D] += column_sum(cot)
        split = halves(cot)
        e_keep[where, :] = beside(*split)
        sq_acc[1] += pair_product(pieces_of(z_keep.at[1], where, 2), split)
        take_coef(index, *split)
        return 0

    lax.fori_loop(0, steps, loss_step, 0)
    mix_back(1)

    def fourier_cot(layer, where):
        return tall4(pieces_of(e_keep, where, 2), locals4[layer]) + dot(table_ref[where, :], stack_ref[...])

    def fourier_back(index, _):
        where = block(index)
        cot = fourier_cot(1, where) * zs_keep[where, :]
        b_acc[40:48, :D] += column_sum(cot)
        split = halves(cot)
        e_keep[where, :] = beside(*split)
        sq_acc[0] += pair_product(pieces_of(z_keep.at[0], where, 2), split)
        take_coef(index, *split)
        return 0

    lax.fori_loop(0, steps, fourier_back, 0)
    mix_back(0)
    turned = dense_rows(0).T
    proj_back = wide4_weight(doubled(turned))

    def project_back(index, _):
        where = block(index)
        later = block(index + steps)
        cot = fourier_cot(0, where)
        b_acc[48:56, :D] += column_sum(cot)
        split = halves(cot)
        first = pieces_of(h2_keep, where, 2)
        second = pieces_of(h2_keep, later, 2)
        p_acc[...] += dot(beside(first[0], second[0], first[1], second[1]), beside(*split), 0, 0)
        rows = wide4(split, proj_back)
        d_keep[where, :] = rows[:, :D]
        d_keep[later, :] = rows[:, D:]
        return 0

    lax.fori_loop(0, steps, project_back, 0)

    def feed_back(layer, index, cot):
        where = block(index)
        base = 56 + layer * 16
        b_acc[base : base + 8, :D] += column_sum(cot)
        split = halves(cot)
        act = act_keep[layer, where, :]
        w2_acc[layer] += dot(beside(*split), act[:, :FF], 0, 0)
        w2_acc[layer, :D, :] += dot(split[0], act[:, FF:], 0, 0)
        inner = wide4(split, w_outt[layer]) * slope_keep[layer, where, :]
        b_acc[base + 8 : base + 16, :] += column_sum(inner)
        return split, halves(inner)

    def layer_one_back(index, _):
        where = block(index)
        cot = d_keep[where, :]
        _, (high, low) = feed_back(1, index, cot)
        mid = mid_keep[where, :]
        w1_acc[...] += dot(mid, high, 0, 0)
        w1_acc[:D, :] += dot(mid[:, :D], low, 0, 0)
        cot = cot + tall4((high, low), w_int[...])
        d_keep[where, :] = cot
        y_acc[index // steps] += pair_product(pieces_of(h1_keep, where, 2), halves(cot))
        return 0

    lax.fori_loop(0, rows_all, layer_one_back, 0)

    def attend_back(layer, products):
        weight = attn_ref[layer]
        query, outer = weight[:, :D], weight[:, 3 * D :]
        key_gain, value_gain = vector("key_gain", layer), vector("value_gain", layer)
        key_column = jnp.sum(eye * key_gain, 1, keepdims=True)
        key_total = jnp.zeros((D, 1), F32)
        value_total = jnp.zeros((1, D), F32)
        query_grad = jnp.zeros((D, D), F32)
        outer_grad = jnp.zeros((D, D), F32)
        for s in range(count):
            plain, summary, mixed = small_keep[layer, s, 0], small_keep[layer, s, 1], small_keep[layer, s, 2]
            turned = exact(query, products[s], 0, 0)
            outer_grad += exact(summary, turned, 0, 0)
            query_grad += exact(products[s], mixed, 1, 1)
            cot = jnp.where(blocks, exact(turned, outer, 1, 1), 0.0)
            both = cot * plain
            key_total += jnp.sum(both * value_gain, 1, keepdims=True)
            value_total += jnp.sum(both * key_column, 0, keepdims=True)
            scaled = key_column * cot * value_gain * (1.0 / points)
            t_keep[s, 0] = tall4_weight(scaled.T)
            t_keep[s, 1] = tall4_weight(scaled)
        g_attn[layer, :, :D] = query_grad
        g_attn[layer, :, 3 * D :] = outer_grad
        return jnp.sum(eye * key_total, 0, keepdims=True), value_total

    gains = [None, None]
    gains[1] = attend_back(1, [quarters(y_acc[s]) for s in range(count)])

    def norm_back(index, normal, scale):
        s = index // steps
        key, value = normal[:, :D], normal[:, D:]
        key_cot = tall4(halves(value), t_keep[s, 0])
        value_cot = tall4(halves(key), t_keep[s, 1])
        mean = dot(beside(*halves(key_cot * key)), mean_weight) * (HEADS / D)
        return beside(scale[:, :D] * (key_cot - key * mean), scale[:, D:] * (value_cot - value * mean))

    def middle_back(index, _):
        where = block(index)
        s = index // steps
        cot = norm_back(index, x_keep[where, :], r_keep[where, :])
        high, low = halves(cot)
        kept = h1_keep[where, : 2 * D]
        kv_acc[...] += dot(kept, high, 0, 0)
        kv_acc[:D, :] += dot(kept[:, :D], low, 0, 0)
        out = d_keep[where, :]
        out = out + tall4(halves(out), nt_keep[s]) + tall4((high, low), w_kvt[...])
        outer, inner = feed_back(0, index, out)
        v_acc[s] += dot(lrows[index], beside(*outer))
        u_acc[s] += dot(lrows[index], beside(*inner))
        return 0

    lax.fori_loop(0, rows_all, middle_back, 0)

    def lift_sum(value):
        value = fold(value)
        return above(
            value[0:1] + value[1:2] + value[2:3],
            value[3:4] + value[4:5] + value[5:6],
            value[6:7],
            jnp.zeros((5, value.shape[1]), F32),
        )

    inner_rows = [lift_sum(u_acc[s]) for s in range(count)]
    value_rows = [lift_sum(v_acc[s]) + exact(inner_rows[s], ffn_ref[0, 0], 1, 1) for s in range(count)]
    gains[0] = attend_back(0, [exact(lift_rows, value_rows[s], 0, 0) for s in range(count)])

    def front_back(index, _):
        centred = dot(lifted[block(index), :], w0_kv[...])
        scale = head_scale(centred)
        cot = norm_back(index, centred * scale, scale)
        vt_acc[...] += dot(lrows[index], beside(*halves(cot)))
        return 0

    lax.fori_loop(0, rows_all, front_back, 0)

    turned = lift_sum(vt_acc[...])
    lift_grad = exact(turned, cent_keep[0], 1, 1)
    for s in range(count):
        lift_grad += value_rows[s] + exact(value_rows[s], n_keep[0, s], 1, 1)
    joined = [exact(lift_rows, turned, 0, 0), kv_acc[:D, :] + kv_acc[D:, :]]
    for layer in range(LAYERS):
        g_attn[layer, :, D : 2 * D] = exact(joined[layer][:, :D], centre)
        g_attn[layer, :, 2 * D : 3 * D] = exact(joined[layer][:, D:], centre)
        g_ffn[layer, 1] = w2_acc[layer, :D, :] + w2_acc[layer, D:, :]

    first = exact(mid_rows[0], inner_rows[0], 0, 0)
    for s in range(1, count):
        first += exact(mid_rows[s], inner_rows[s], 0, 0)
    g_ffn[0, 0] = first
    g_ffn[1, 0] = w1_acc[:D, :] + w1_acc[D:, :]
    sums = p_acc[...]
    sums = fold(sums[: 2 * D] + sums[2 * D :])
    g_dense[:D, :] = sums[:D, :FREQ] + sums[D:, FREQ:]
    for part in range(3):
        sums = quarters(sq_acc[part])
        start = D + part * FREQ
        g_dense[start : start + FREQ, :] = sums[:FREQ, :FREQ] + sums[FREQ:, FREQ:]

    def bias(slot, width=D):
        return jnp.sum(b_acc[slot * 8 : slot * 8 + 8, :width], 0, keepdims=True)

    rows = [lift_grad[0:1], lift_grad[1:2], lift_grad[2:3]]
    for layer in range(LAYERS):
        inner = bias(8 + 2 * layer, FF)
        rows += [gains[layer][0], gains[layer][1], inner[:, :D], inner[:, D:], bias(7 + 2 * layer)]
    short = [fold(bias(slot)) for slot in (6, 5, 4, 3, 2)]
    rows += [beside(short[0], short[1]), beside(short[2], short[3]), beside(short[4], jnp.zeros((1, FREQ), F32))]
    g_vec[...] = above(*rows)
    lanes = lax.broadcasted_iota(jnp.int32, (1, D), 1)
    first = jnp.where(lax.rem(lanes, FREQ) == 0, bias(0), 0.0)
    second = jnp.where(lax.rem(lanes, FREQ) == 0, bias(1), 0.0)
    g_loss[...] = above(first, second, jnp.zeros((6, D), F32))


def tables(points):
    order = np.arange(MODES)[:, None]
    angle = (order * np.arange(points)[None, :]) % points * (2.0 * math.pi / points)
    full = np.concatenate([np.cos(angle), np.sin(angle)], 0).astype(np.float32)
    kind = np.dtype(ml_dtypes.bfloat16)
    high = full.astype(kind)
    rest = full - high.astype(np.float32)
    middle = rest.astype(kind)
    low = (rest - middle.astype(np.float32)).astype(kind)
    zero = np.zeros((4 * MODES, points), kind)
    column = np.concatenate([high, middle, high, middle, high, low, zero], 0).T
    row = np.concatenate([high, middle], 0).reshape(4 * MODES, points // ROWS, ROWS).transpose(1, 0, 2)
    return np.ascontiguousarray(column), np.ascontiguousarray(row)


def local_grads(inputs, attn_w, ffn_w, spec_w, dense_w, vec):
    count, _, points = inputs.shape
    total = count * points
    steps = points // ROWS
    column, row = tables(points)
    vmem = pl.BlockSpec(memory_space=pltpu.VMEM)
    scratch = [
        ((total, D), BF16),
        ((total // ROWS, 16, ROWS), BF16),
        ((6 * D, 2 * D), BF16),
        ((4 * D, 2 * D), BF16),
        ((6 * D, FF), BF16),
        ((2 * FF, 2 * D), BF16),
        ((count, D, FF), BF16),
        ((count, 8, D), F32),
        ((LAYERS, 2 * FF, 2 * D), BF16),
        ((LAYERS, 2 * FF, D), BF16),
        ((LAYERS, 4 * D, FF), BF16),
        ((total, 2 * D), F32),
        ((total, 2 * D), F32),
        ((LAYERS, total, FF), F32),
        ((LAYERS, total, 2 * FF), BF16),
        ((total, 2 * D), BF16),
        ((total, 3 * D), BF16),
        ((total, 3 * D), BF16),
        ((FLAYERS, points, 3 * D), BF16),
        ((points, D), F32),
        ((points, 2 * D), BF16),
        ((LAYERS, count, 2 * D, 2 * D), F32),
        ((D, 2 * D), BF16),
        ((count, D, D), BF16),
        ((LAYERS, count, D, D), F32),
        ((LAYERS, count, 3, D, D), F32),
        ((count, 2 * D, 2 * D), BF16),
        ((LAYERS, D, 2 * D), F32),
        ((4 * MODES, 2 * D), F32),
        ((FLAYERS, 2 * count * MODES, D), F32),
        ((2 * D, D), BF16),
        ((3, 2 * D, 2 * D), F32),
        ((4 * D, 2 * D), F32),
        ((count, 2 * D, 2 * D), F32),
        ((LAYERS, 2 * D, FF), F32),
        ((2 * D, FF), F32),
        ((2 * D, 2 * D), F32),
        ((count, 16, 2 * D), F32),
        ((count, 16, 2 * FF), F32),
        ((16, 4 * D), F32),
        ((96, FF), F32),
        ((total, D), F32),
        ((count, 2, 2 * D, 2 * D), BF16),
        ((count, 4 * D, 2 * D), BF16),
    ]
    shapes = [attn_w.shape, ffn_w.shape, spec_w.shape, dense_w.shape, vec.shape, (8, D)]
    return pl.pallas_call(
        local_kernel,
        out_shape=[jax.ShapeDtypeStruct(shape, F32) for shape in shapes],
        in_specs=[vmem] * 8,
        out_specs=[vmem] * 6,
        scratch_shapes=[pltpu.VMEM(*item) for item in scratch],
        compiler_params=pltpu.CompilerParams(vmem_limit_bytes=64 * 2**20 - 2**17),
    )(inputs, attn_w, ffn_w, spec_w, dense_w, vec, jnp.asarray(column), jnp.asarray(row))


def fast_body(samples_in, target, mask, attn_w, ffn_w, spec_w, dense_w, vectors, *moments):
    packed = jnp.concatenate([samples_in, target[:, None], mask.astype(F32)[:, None]], 1)
    whole = lax.all_to_all(packed, "pts", split_axis=0, concat_axis=2, tiled=True)
    vec = jnp.pad(vectors, (0, -vectors.shape[0] % D)).reshape(-1, D)
    pieces = local_grads(
        whole, attn_w, ffn_w, spec_w.reshape(FLAYERS, MODES * 2 * FREQ, FREQ), dense_w, vec
    )
    summed = lax.psum(tuple(pieces), ("dp", "pts"))
    loss_sum, valid_count = jnp.sum(summed[5][0]), jnp.sum(summed[5][1])
    grads = (
        summed[0],
        summed[1],
        summed[2].reshape(spec_w.shape),
        summed[3],
        summed[4].reshape(-1)[: vectors.shape[0]],
    )
    grads = tuple(grad * (1.0 / valid_count) for grad in grads)
    params = (attn_w, ffn_w, spec_w, dense_w, vectors)
    return tuple(finish(loss_sum, valid_count, params, grads, moments[:5], moments[5:]))


def choose_body(*arrays):
    samples_in = arrays[0]
    parts = lax.axis_size("pts")
    regular = samples_in.shape[0] == 2 * parts and samples_in.shape[2] * parts % ROWS == 0
    return (fast_body if regular else body)(*arrays)


def solution(mesh):
    placed = (
        P("dp", None, "pts"),
        P("dp", "pts"),
        P("dp", "pts"),
        P(),
        P(),
        P(),
        P(),
        P(),
        P(),
        P(),
        P(),
        P(),
        P(),
        P(),
        P(),
        P(),
        P(),
        P(),
    )
    return jax.shard_map(
        choose_body,
        mesh=mesh,
        in_specs=placed,
        out_specs=(
            P(),
            P(),
            P(),
            P(),
            P(),
            P(),
            P(),
            P(),
            P(),
            P(),
            P(),
            P(),
            P(),
            P(),
            P(),
            P(),
            P(),
            P(),
            P(),
            P(),
            P(),
            P(),
            P(),
            P(),
            P(),
        ),
        check_vma=False,
    )
```

```python
import math

import jax
import jax.numpy as jnp
import ml_dtypes
import numpy as np
from jax import lax
from jax.experimental import pallas as pl
from jax.experimental.pallas import tpu as pltpu
from jax.sharding import PartitionSpec as P

D = 128
HEADS = 4
FF = 256
FREQ = 64
MODES = 16
LAYERS = 2
FLAYERS = 2
STEP = 5


HIGH = lax.Precision.HIGHEST
NORM_EPS = 1e-05
BETA_ONE = 0.5
BETA_TWO = 0.5
RATE = 0.2
DECAY = 0.01
ADAM_EPS = 1e-06


def vector_table():
    entries = [("lift_value", 0, D), ("lift_coord", 0, D), ("lift_bias", 0, D)]
    for layer in range(LAYERS):
        entries = entries + [
            ("key_gain", layer, D),
            ("value_gain", layer, D),
            ("inner_bias", layer, FF),
            ("outer_bias", layer, D),
        ]
    entries = entries + [("proj_bias", 0, FREQ)]
    for layer in range(FLAYERS):
        entries = entries + [("fourier_bias", layer, FREQ)]
    entries = entries + [("head_bias", 0, FREQ), ("head_out", 0, FREQ)]
    offsets = {}
    start = 0
    for label, layer, length in entries:
        offsets[label, layer] = (start, length)
        start = start + length
    return offsets


def pick(vectors, label, layer):
    start, length = vector_table()[label, layer]
    return vectors[start : start + length]


def head_norm(values, gain):
    centred = values - jnp.mean(values, -1, keepdims=True)
    scaled = centred * lax.rsqrt(jnp.mean(centred * centred, -1, keepdims=True) + NORM_EPS)
    return scaled * gain.reshape(HEADS, D // HEADS)


def lift(params, inputs):
    vectors = params[4]
    value = inputs[..., 0, :, None]
    coord = inputs[..., 1, :, None]
    return (
        value * pick(vectors, "lift_value", 0)
        + coord * pick(vectors, "lift_coord", 0)
        + pick(vectors, "lift_bias", 0)
    )


def attn_front(params, rows, layer, points):
    weight = params[0][layer]
    vectors = params[4]
    mixed = jnp.einsum("...d,de->...e", rows, weight[:, : 3 * D], precision=HIGH)
    shape = rows.shape[:-1] + (HEADS, D // HEADS)
    query = mixed[..., :D].reshape(shape)
    keys = head_norm(mixed[..., D : 2 * D].reshape(shape), pick(vectors, "key_gain", layer))
    values = head_norm(mixed[..., 2 * D :].reshape(shape), pick(vectors, "value_gain", layer))
    partial_sum = jnp.einsum("...phe,...phf->...hef", keys, values, precision=HIGH) / points
    return (query, partial_sum)


def attn_rear(params, rows, query, summary, layer):
    weight = params[0][layer]
    attended = jnp.einsum("...phe,...hef->...phf", query, summary, precision=HIGH).reshape(
        rows.shape
    )
    return rows + jnp.einsum("...d,de->...e", attended, weight[:, 3 * D :], precision=HIGH)


def ffn_block(params, rows, layer):
    weight = params[1][layer]
    vectors = params[4]
    inner = jnp.einsum("...d,df->...f", rows, weight[0], precision=HIGH) + pick(
        vectors, "inner_bias", layer
    )
    outer = jnp.einsum("...f,df->...d", jax.nn.gelu(inner), weight[1], precision=HIGH)
    return rows + outer + pick(vectors, "outer_bias", layer)


def project(params, rows):
    return jnp.einsum("...d,df->...f", rows, params[3][:D], precision=HIGH) + pick(
        params[4], "proj_bias", 0
    )


def mode_table(count, total):
    position = jnp.arange(count, dtype=jnp.int32)
    orders = jnp.arange(MODES, dtype=jnp.int32)
    phase = orders[:, None] * position[None, :] % total
    angle = phase.astype(jnp.float32) * (2.0 * math.pi / total)
    return jnp.concatenate([jnp.cos(angle), jnp.sin(angle)], 0)


def spectral_mix(coef, spec, first, width):
    columns = lax.dynamic_slice_in_dim(spec, first, width, 3)
    cosine = coef[..., :MODES, :]
    sine = coef[..., MODES:, :]
    real_part = columns[:, 0]
    imag_part = columns[:, 1]
    mixed_cos = jnp.einsum("...mf,mfg->...mg", cosine, real_part, precision=HIGH) + jnp.einsum(
        "...mf,mfg->...mg", sine, imag_part, precision=HIGH
    )
    mixed_sin = jnp.einsum("...mf,mfg->...mg", sine, real_part, precision=HIGH) - jnp.einsum(
        "...mf,mfg->...mg", cosine, imag_part, precision=HIGH
    )
    return jnp.concatenate([mixed_cos, mixed_sin], -2)


def fourier_end(params, back, rows, layer):
    local = params[3][D + layer * FREQ : D + (layer + 1) * FREQ]
    inner = back + jnp.einsum("...f,fg->...g", rows, local, precision=HIGH)
    return jax.nn.gelu(inner + pick(params[4], "fourier_bias", layer))


def head_loss(params, rows, target, mask_f):
    start = D + FLAYERS * FREQ
    hidden = jax.nn.gelu(
        jnp.einsum("...f,fg->...g", rows, params[3][start : start + FREQ], precision=HIGH)
        + pick(params[4], "head_bias", 0)
    )
    pred = jnp.einsum("...f,f->...", hidden, pick(params[4], "head_out", 0), precision=HIGH)
    diff = pred - target
    return jnp.sum(mask_f * diff * diff)


def add_all(first, second):
    return jax.tree.map(jnp.add, first, second)


def spectral_setup(points, parts):
    width = FREQ // parts
    return (mode_table(points, points), lax.axis_index("pts") * width, width, points)


def fourier_mix(spec, field, setup):
    grid, column, width, points = setup
    channel_rows = lax.all_to_all(field, "pts", split_axis=2, concat_axis=1, tiled=True)
    own_coef = jnp.einsum("kp,spc->skc", grid, channel_rows, precision=HIGH) / math.sqrt(points)
    full = lax.all_gather(own_coef, "pts", axis=2, tiled=True)
    mixed = spectral_mix(full, spec, column, width)
    spread = jnp.einsum("kp,skc->spc", grid, mixed, precision=HIGH) / math.sqrt(MODES)
    back = lax.all_to_all(spread, "pts", split_axis=1, concat_axis=2, tiled=True)
    return (back, full)


def fourier_back(params, grad_out, kept_item, layer, setup):
    field, full, back = kept_item
    grid, column, width, points = setup
    _, end_pull = jax.vjp(
        lambda weights, spread, inner: fourier_end(weights, spread, inner, layer),
        params,
        back,
        field,
    )
    grads, grad_back, grad_field = end_pull(grad_out)
    _, mix_pull = jax.vjp(
        lambda coef, weight: spectral_mix(coef, weight, column, width), full, params[2][layer]
    )
    grad_rows = lax.all_to_all(grad_back, "pts", split_axis=2, concat_axis=1, tiled=True)
    grad_mixed = jnp.einsum("kp,spc->skc", grid, grad_rows, precision=HIGH) / math.sqrt(MODES)
    grad_full, grad_spec = mix_pull(grad_mixed)
    grad_coef = lax.psum_scatter(grad_full, "pts", scatter_dimension=2, tiled=True)
    grad_chan = jnp.einsum("kp,skc->spc", grid, grad_coef, precision=HIGH) / math.sqrt(points)
    grad_field = grad_field + lax.all_to_all(
        grad_chan, "pts", split_axis=1, concat_axis=2, tiled=True
    )
    grads = (grads[0], grads[1], grads[2].at[layer].add(grad_spec), grads[3], grads[4])
    return (grads, grad_field)


def attention_back(params, grad_rows, kept_item, layer, points):
    rows, summary = kept_item
    (query, partial_sum), front_pull = jax.vjp(
        lambda weights, inner: attn_front(weights, inner, layer, points), params, rows
    )
    summary = lax.psum(partial_sum, "pts")
    middle, rear_pull = jax.vjp(
        lambda weights, inner, asked, summed: attn_rear(weights, inner, asked, summed, layer),
        params,
        rows,
        query,
        summary,
    )
    _, ffn_pull = jax.vjp(lambda weights, inner: ffn_block(weights, inner, layer), params, middle)
    ffn_grads, grad_middle = ffn_pull(grad_rows)
    rear_grads, grad_direct, grad_query, grad_summary = rear_pull(grad_middle)
    grad_summary = lax.psum(grad_summary, "pts")
    front_grads, grad_front = front_pull((grad_query, grad_summary))
    return (add_all(add_all(ffn_grads, rear_grads), front_grads), grad_direct + grad_front)


def lamb(weight, grad, first, second):
    first_new = BETA_ONE * first + (1.0 - BETA_ONE) * grad
    second_new = BETA_TWO * second + (1.0 - BETA_TWO) * grad * grad
    update = (
        first_new
        / (1.0 - BETA_ONE**STEP)
        / (jnp.sqrt(second_new / (1.0 - BETA_TWO**STEP)) + ADAM_EPS)
        + DECAY * weight
    )
    return (first_new, second_new, update)


def trust_step(weight, update, stacked):
    axes = tuple(range(1, weight.ndim)) if stacked else tuple(range(weight.ndim))
    weight_norm = jnp.sqrt(jnp.sum(weight * weight, axes))
    update_norm = jnp.sqrt(jnp.sum(update * update, axes))
    ratio = weight_norm / (update_norm + ADAM_EPS)
    scale = ratio.reshape(ratio.shape + (1,) * (weight.ndim - ratio.ndim))
    return (
        weight - RATE * scale * update,
        jnp.atleast_1d(weight_norm),
        jnp.atleast_1d(update_norm),
        jnp.atleast_1d(ratio),
    )


def finish(loss_sum, valid_count, params, grads, firsts, seconds):
    results = [loss_sum, valid_count]
    weight_norms, update_norms, ratios = ([], [], [])
    for weight, grad, first, second, stacked in zip(
        params, grads, firsts, seconds, (True, True, True, False, False)
    ):
        first_new, second_new, update = lamb(weight, grad, first, second)
        fresh, weight_norm, update_norm, ratio = trust_step(weight, update, stacked)
        results = results + [first_new, second_new, fresh, fresh.astype(jnp.bfloat16)]
        weight_norms.append(weight_norm)
        update_norms.append(update_norm)
        ratios.append(ratio)
    return results + [
        jnp.concatenate(weight_norms),
        jnp.concatenate(update_norms),
        jnp.concatenate(ratios),
    ]


def body(
    samples_in,
    target,
    mask,
    attn_w,
    ffn_w,
    spec_w,
    dense_w,
    vectors,
    attn_m,
    ffn_m,
    spec_m,
    dense_m,
    vector_m,
    attn_v,
    ffn_v,
    spec_v,
    dense_v,
    vector_v,
):
    params = (attn_w, ffn_w, spec_w, dense_w, vectors)
    parts = lax.axis_size("pts")
    local_pts = samples_in.shape[2]
    points = local_pts * parts
    mask_f = mask.astype(jnp.float32)
    valid_count = lax.psum(jnp.sum(mask_f), ("dp", "pts"))
    setup = spectral_setup(points, parts)
    rows, lift_pull = jax.vjp(lambda weights: lift(weights, samples_in), params)
    kept = []
    for layer in range(LAYERS):
        query, partial_sum = attn_front(params, rows, layer, points)
        summary = lax.psum(partial_sum, "pts")
        kept.append((rows, summary))
        rows = ffn_block(params, attn_rear(params, rows, query, summary, layer), layer)
    field, proj_pull = jax.vjp(project, params, rows)
    spectral_kept = []
    for layer in range(FLAYERS):
        back, full = fourier_mix(params[2][layer], field, setup)
        spectral_kept.append((field, full, back))
        field = fourier_end(params, back, field, layer)
    loss_part, head_pull = jax.vjp(
        lambda weights, inner: head_loss(weights, inner, target, mask_f), params, field
    )
    grads, grad_field = head_pull(1.0 / valid_count)
    for layer in reversed(range(FLAYERS)):
        layer_grads, grad_field = fourier_back(
            params, grad_field, spectral_kept[layer], layer, setup
        )
        grads = add_all(grads, layer_grads)
    proj_grads, grad_rows = proj_pull(grad_field)
    grads = add_all(grads, proj_grads)
    for layer in reversed(range(LAYERS)):
        layer_grads, grad_rows = attention_back(params, grad_rows, kept[layer], layer, points)
        grads = add_all(grads, layer_grads)
    grads = add_all(grads, lift_pull(grad_rows)[0])
    summed = lax.psum((grads[0], grads[1], grads[2], grads[3], grads[4], loss_part), ("dp", "pts"))
    out = finish(
        summed[5],
        valid_count,
        params,
        summed[:5],
        (attn_m, ffn_m, spec_m, dense_m, vector_m),
        (attn_v, ffn_v, spec_v, dense_v, vector_v),
    )
    return (
        out[0],
        out[1],
        out[2],
        out[3],
        out[4],
        out[5],
        out[6],
        out[7],
        out[8],
        out[9],
        out[10],
        out[11],
        out[12],
        out[13],
        out[14],
        out[15],
        out[16],
        out[17],
        out[18],
        out[19],
        out[20],
        out[21],
        out[22],
        out[23],
        out[24],
    )


F32 = jnp.float32
BF16 = jnp.bfloat16
ROWS = 512
NVEC_ROWS = 16


def dot(first, second, left=1, right=0, precision=None):
    return lax.dot_general(
        first,
        second,
        (((left,), (right,)), ((), ())),
        precision=precision,
        preferred_element_type=F32,
    )


def exact(first, second, left=1, right=0):
    return dot(first, second, left, right, HIGH)


def halves(value):
    high = value.astype(BF16)
    return high, (value - high.astype(F32)).astype(BF16)


def thirds(value):
    high = value.astype(BF16)
    rest = value - high.astype(F32)
    middle = rest.astype(BF16)
    return high, middle, (rest - middle.astype(F32)).astype(BF16)


def beside(*pieces):
    return jnp.concatenate(pieces, 1)


def above(*pieces):
    return jnp.concatenate(pieces, 0)


def fold(value):
    half = value.shape[1] // 2
    return value[:, :half] + value[:, half:]


def column_sum(value):
    rows, width = value.shape
    return jnp.sum(value.reshape(rows // 8, 8, width), 0)


def gelu_pair(inner):
    scale = math.sqrt(2.0 / math.pi)
    square = inner * inner
    bend = jnp.tanh(inner * (scale + (scale * 0.044715) * square))
    half = 0.5 + 0.5 * bend
    slope = half + (0.5 * inner) * (1.0 - bend * bend) * (scale + (3.0 * scale * 0.044715) * square)
    return inner * half, slope


def wide6_weight(weight):
    high, middle, low = thirds(weight)
    return above(high, high, middle, middle, low, high)


def wide6(pieces, weight):
    high, middle, low = pieces
    return dot(beside(high, middle, high, middle, high, low), weight)


def tall6_weight(weight):
    high, middle, low = thirds(weight)
    pair = beside(high, middle)
    return above(pair, pair), above(low, high)


def tall6(pieces, weights):
    high, middle, low = pieces
    return fold(dot(beside(high, middle), weights[0])) + dot(beside(high, low), weights[1])


def wide4_weight(weight):
    high, low = halves(weight)
    return above(high, high, low, low)


def wide4(pieces, weight):
    high, low = pieces
    return dot(beside(high, low, high, low), weight)


def tall4_weight(weight):
    high, low = halves(weight)
    pair = beside(high, low)
    return above(pair, pair)


def tall4(pieces, weight):
    return fold(dot(beside(*pieces), weight))


def head_blocks(width):
    row = lax.broadcasted_iota(jnp.int32, (width, width), 0)
    column = lax.broadcasted_iota(jnp.int32, (width, width), 1)
    return row // (D // HEADS) == column // (D // HEADS)


def doubled(weight):
    zero = jnp.zeros_like(weight)
    return above(beside(weight, zero), beside(zero, weight))


MESH = pl.DeviceIdType.MESH


def position():
    dp, pts = lax.axis_index("dp"), lax.axis_index("pts")
    x, core, z, y = dp // 2, dp % 2, pts // 2, pts % 2
    return x, core, z, y


def device_of(x, core, z, y):
    return (2 * x + core, 2 * z + y)


def device_at(number):
    core, a, b, z = number // 16, number // 8 % 2, number // 4 % 2, number % 4
    x = (1 - core) * a + core * b
    y = (1 - core) * b + core * a
    return device_of(x, core, z, y)


class Route:
    def __init__(self, rows, full, flat, landing, sends, receives, first):
        x, core, z, y = position()
        a = (1 - core) * x + core * y
        b = (1 - core) * y + core * x
        self.keep = (core, a, b, z)
        self.rows, self.full, self.flat, self.landing = rows, full, flat, landing
        self.sends, self.receives, self.first = sends, receives, first
        self.peers = [
            device_of(x, 1 - core, z, y),
            device_of(x + (1 - core) * (1 - 2 * x), core, z, y + core * (1 - 2 * y)),
            device_of(x + core * (1 - 2 * x), core, z, y + (1 - core) * (1 - 2 * y)),
        ]
        self.far = [device_of(x, core, (z + k) % 4, y) for k in (1, 2, 3)]
        half, quarter, eighth, least = rows // 2, rows // 4, rows // 8, rows // 32
        self.least = least
        self.sizes = [half, quarter, eighth]
        self.starts = [core * half, core * half + a * quarter, core * half + a * quarter + b * eighth]
        self.own = self.starts[2] + z * least
        self.others = [
            (1 - core) * half,
            core * half + (1 - a) * quarter,
            core * half + a * quarter + (1 - b) * eighth,
        ]

    def area(self, start, size):
        return pl.ds(pl.multiple_of(start, self.least), size)

    def link(self, source, target, slot, device):
        return pltpu.make_async_remote_copy(
            src_ref=source,
            dst_ref=target,
            send_sem=self.sends.at[self.first + slot],
            recv_sem=self.receives.at[self.first + slot],
            device_id=device,
            device_id_type=MESH,
        )

    def copies(self, stage, receiving=False):
        z = self.keep[3]
        if stage < 3:
            place = self.landing.at[pl.ds(self.rows - 2 * self.sizes[stage], self.sizes[stage])]
            source = self.flat.at[self.area(self.others[stage], self.sizes[stage])]
            return [self.link(source, place, stage, self.peers[stage])]
        if stage == 3:
            found = []
            for k in (1, 2, 3):
                start = self.starts[2] + (z + k) % 4 * self.least
                place = self.landing.at[pl.ds(self.rows - self.sizes[2] + (k - 1) * self.least, self.least)]
                found.append(self.link(self.flat.at[self.area(start, self.least)], place, 2 + k, self.far[k - 1]))
            return found
        if stage == 4:
            piece = self.full.at[self.area(self.own, self.least)]
            found = []
            for k in (1, 2, 3):
                start = self.starts[2] + (z + 4 - k) % 4 * self.least if receiving else self.own
                found.append(self.link(piece, self.full.at[self.area(start, self.least)], 5 + k, self.far[k - 1]))
            return found
        level = 7 - stage
        size = self.sizes[level]
        piece = self.full.at[self.area(self.starts[level], size)]
        target = self.full.at[self.area(self.others[level], size)] if receiving else piece
        return [self.link(piece, target, 4 + stage, self.peers[level])]

    def start(self, stage):
        if stage == 4 and self.flat is not None:
            self.full[self.area(self.own, self.least), :] = self.flat[self.area(self.own, self.least), :]
        for copy in self.copies(stage):
            copy.start()

    def finish(self, stage):
        for copy in self.copies(stage, True):
            copy.wait()
        if stage < 3:
            mine = self.area(self.starts[stage], self.sizes[stage])
            place = pl.ds(self.rows - 2 * self.sizes[stage], self.sizes[stage])
            self.flat[mine, :] += self.landing[place, :]
        if stage == 3:
            mine = self.area(self.own, self.least)
            total = self.flat[mine, :]
            for k in range(3):
                total = total + self.landing[pl.ds(self.rows - self.sizes[2] + k * self.least, self.least), :]
            self.flat[mine, :] = total

    def step(self, stage):
        self.finish(stage)
        self.start(stage + 1)


def spread_to_all(devices, mine, source_of, target, sends, receives, start):
    def one(i, _):
        other = lax.rem(mine + 1 + i, devices)
        sender = lax.rem(mine + devices - 1 - i, devices)
        copy = pltpu.make_async_remote_copy(
            src_ref=source_of(other),
            dst_ref=target.at[mine if start else sender],
            send_sem=sends.at[i],
            recv_sem=receives.at[i],
            device_id=device_at(other),
            device_id_type=MESH,
        )
        if start:
            copy.start()
        else:
            copy.wait()
        return 0

    lax.fori_loop(0, devices - 1, one, 0)


def step_kernel(
    samples_ref,
    target_ref,
    mask_ref,
    attn_ref,
    ffn_ref,
    spec_ref,
    turned_ref,
    vectors_ref,
    table_ref,
    trow_ref,
    early_out,
    late_out,
    mode_out,
    tail_out,
    outgoing,
    incoming,
    vec_ref,
    early,
    early_land,
    late,
    late_land,
    mode_send,
    mode_land,
    tail_send,
    tail_land,
    route_send,
    route_recv,
    point_send,
    point_recv,
    mode_sends,
    mode_recvs,
    tail_sends,
    tail_recvs,
    lifted,
    lrows,
    w_kv,
    w_kvt,
    w_in,
    w_int,
    w0_u,
    mid_rows,
    w_out0,
    w_out1,
    w_outt,
    x_keep,
    r_keep,
    slope_keep,
    act_keep,
    mid_keep,
    h1_keep,
    h2_keep,
    z_keep,
    zs_keep,
    e_keep,
    s_acc,
    w0_kv,
    w0_g,
    n_keep,
    small_keep,
    nt_keep,
    cent_keep,
    coef_acc,
    coef_keep,
    stack_ref,
    sq_acc,
    p_acc,
    y_acc,
    w2_acc,
    w1_acc,
    kv_acc,
    v_acc,
    u_acc,
    vt_acc,
    b_acc,
    d_keep,
    t_keep,
    wz,
):
    parts = samples_ref.shape[0] // 2
    count = 2
    points = samples_ref.shape[2] * parts
    devices = FLAYERS * MODES
    x, core, z, y = position()
    pts = 2 * z + y
    mine = 16 * core + 8 * ((1 - core) * x + core * y) + 4 * ((1 - core) * y + core * x) + z
    early_route = Route(early.shape[0], early_out, early, early_land, route_send, route_recv, 0)
    late_route = Route(late.shape[0], late_out, late, late_land, route_send, route_recv, 12)
    mode_route = Route(mode_out.shape[0], mode_out, None, None, route_send, route_recv, 24)

    barrier = pltpu.get_barrier_semaphore()

    def greet(i, _):
        pl.semaphore_signal(
            barrier, inc=1, device_id=device_at(lax.rem(mine + 1 + i, devices)), device_id_type=MESH
        )
        return 0

    lax.fori_loop(0, devices - 1, greet, 0)
    for p in range(parts):
        outgoing[p, 0:2, :] = samples_ref[2 * p]
        outgoing[p, 2:4, :] = samples_ref[2 * p + 1]
        outgoing[p, 4:6, :] = target_ref[2 * p : 2 * p + 2, :]
        outgoing[p, 6:8, :] = mask_ref[2 * p : 2 * p + 2, :].astype(F32)
    incoming[pts] = outgoing[pts]
    pl.semaphore_wait(barrier, devices - 1)

    def point_copy(k, start):
        other = lax.rem(pts + k, parts)
        sender = lax.rem(pts + parts - k, parts)
        return pltpu.make_async_remote_copy(
            src_ref=outgoing.at[other],
            dst_ref=incoming.at[pts if start else sender],
            send_sem=point_send.at[k - 1],
            recv_sem=point_recv.at[k - 1],
            device_id=(2 * x + core, other),
            device_id_type=MESH,
        )

    for k in range(1, parts):
        point_copy(k, True).start()
    for i in range(NVEC_ROWS - 1):
        vec_ref[i : i + 1, :] = vectors_ref[i * D : (i + 1) * D].reshape(1, D)
    last = vectors_ref.shape[0] - (NVEC_ROWS - 1) * D
    vec_ref[NVEC_ROWS - 1 :, :last] = vectors_ref[(NVEC_ROWS - 1) * D :].reshape(1, last)
    total = count * points
    steps = points // ROWS
    rows_all = total // ROWS
    blocks = head_blocks(D)
    block_f = jnp.where(blocks, 1.0, 0.0).astype(F32)
    block_b = block_f.astype(BF16)
    mean_weight = above(block_b, block_b)
    centre = (
        jnp.where(
            lax.broadcasted_iota(jnp.int32, (D, D), 0) == lax.broadcasted_iota(jnp.int32, (D, D), 1),
            1.0,
            0.0,
        ).astype(F32)
        - block_f * (HEADS / D)
    )
    eye = jnp.where(
        lax.broadcasted_iota(jnp.int32, (D, D), 0) == lax.broadcasted_iota(jnp.int32, (D, D), 1), 1.0, 0.0
    ).astype(F32)

    def vector(label, layer):
        start, length = vector_table()[label, layer]
        if length == 2 * D:
            row = start // D
            return beside(vec_ref[row : row + 1, :], vec_ref[row + 1 : row + 2, :])
        row = start // D
        if length == D:
            return vec_ref[row : row + 1, :]
        offset = start - row * D
        piece = vec_ref[row : row + 1, offset : offset + FREQ]
        return beside(piece, piece)

    def block(index):
        return pl.ds(pl.multiple_of(index * ROWS, ROWS), ROWS)

    lift_rows = above(
        vector("lift_value", 0), vector("lift_coord", 0), vector("lift_bias", 0), jnp.zeros((5, D), F32)
    )

    def lift_weight(mixed):
        high, middle, low = [item.astype(F32) for item in thirds(mixed)]
        parts = []
        for i in range(2):
            hi, mi, lo = high[i : i + 1], middle[i : i + 1], low[i : i + 1]
            parts += [hi, hi, mi, mi, lo, hi]
        parts += [high[2:3], middle[2:3], low[2:3]]
        parts.append(jnp.zeros((D - 15, mixed.shape[1]), F32))
        return above(*parts).astype(BF16)

    for layer in range(LAYERS):
        weight = attn_ref[layer]
        keyed = beside(exact(weight[:, D : 2 * D], centre), exact(weight[:, 2 * D : 3 * D], centre))
        cent_keep[layer] = keyed
        if layer == 0:
            w0_kv[...] = lift_weight(exact(lift_rows, keyed))
        else:
            w_kv[...] = wide6_weight(keyed)
            w_kvt[...] = tall4_weight(keyed.T)
        first, second = ffn_ref[layer, 0], ffn_ref[layer, 1]
        if layer:
            w_in[...] = wide6_weight(first)
            w_int[...] = tall4_weight(first.T)
        pair, rest = tall6_weight(second.T)
        w_out0[layer] = pair
        w_out1[layer] = rest
        w_outt[layer] = wide4_weight(second)

    s_acc[...] = jnp.zeros_like(s_acc)
    coef_acc[...] = jnp.zeros_like(coef_acc)
    sq_acc[...] = jnp.zeros_like(sq_acc)
    p_acc[...] = jnp.zeros_like(p_acc)
    y_acc[...] = jnp.zeros_like(y_acc)
    w2_acc[...] = jnp.zeros_like(w2_acc)
    w1_acc[...] = jnp.zeros_like(w1_acc)
    kv_acc[...] = jnp.zeros_like(kv_acc)
    v_acc[...] = jnp.zeros_like(v_acc)
    u_acc[...] = jnp.zeros_like(u_acc)
    vt_acc[...] = jnp.zeros_like(vt_acc)
    b_acc[...] = jnp.zeros_like(b_acc)

    for k in range(1, parts):
        point_copy(k, False).wait()
    whole = beside(*[incoming[p] for p in range(parts)])
    for s in range(count):
        value, coord = whole[2 * s : 2 * s + 1], whole[2 * s + 1 : 2 * s + 2]
        target, valid = whole[4 + s : 5 + s], whole[6 + s : 7 + s]
        one = jnp.ones_like(value)
        vh, vm, vl = [item.astype(F32) for item in thirds(value)]
        ch, cm, cl = [item.astype(F32) for item in thirds(coord)]
        th, tm, tl = [item.astype(F32) for item in thirds(target)]
        zero = jnp.zeros((D - 19, points), F32)
        stack = above(vh, vm, vh, vm, vh, vl, ch, cm, ch, cm, ch, cl, one, one, one, th, tm, tl, valid, zero)
        lifted[s * points : (s + 1) * points, :] = stack.T.astype(BF16)
        short = above(vh, vm, vl, ch, cm, cl, one, jnp.zeros((9, points), F32)).astype(BF16)
        for i in range(steps):
            lrows[s * steps + i] = short[:, i * ROWS : (i + 1) * ROWS]

    def head_scale(centred):
        high, low = halves(centred * centred)
        var = beside(
            dot(beside(high[:, :D], low[:, :D]), mean_weight), dot(beside(high[:, D:], low[:, D:]), mean_weight)
        )
        return lax.rsqrt(var * (HEADS / D) + NORM_EPS)

    def normalise(layer, index, centred):
        scale = head_scale(centred)
        normal = centred * scale
        if layer:
            where = block(index)
            x_keep[where, :] = normal
            r_keep[where, :] = scale
        high, low = halves(normal)
        s_acc[layer, index // steps] += dot(
            beside(high[:, :D], low[:, :D]), beside(high[:, D:], low[:, D:]), 0, 0
        )

    def quarters(value):
        half_row, half_col = value.shape[0] // 2, value.shape[1] // 2
        return (
            value[:half_row, :half_col]
            + value[half_row:, :half_col]
            + (value[:half_row, half_col:] + value[half_row:, half_col:])
        )

    def summarise(layer):
        weight = attn_ref[layer]
        key_gain = vector("key_gain", layer).reshape(1, D)
        value_gain = vector("value_gain", layer).reshape(1, D)
        key_column = jnp.sum(eye * key_gain, 1, keepdims=True)
        for s in range(count):
            plain = jnp.where(blocks, quarters(s_acc[layer, s]), 0.0) * (1.0 / points)
            summary = key_column * plain * value_gain
            mixed = exact(summary, weight[:, 3 * D :])
            both = exact(weight[:, :D], mixed)
            n_keep[layer, s] = both
            small_keep[layer, s, 0] = plain
            small_keep[layer, s, 1] = summary
            small_keep[layer, s, 2] = mixed
            if layer == 0:
                rows = exact(lift_rows, eye + both)
                mid_rows[s] = rows
                w0_g[s] = lift_weight(rows)
                w0_u[s] = lift_weight(exact(rows, ffn_ref[0, 0]))
            else:
                pair, rest = tall6_weight(both)
                wz[s, : 2 * D, :] = pair
                wz[s, 2 * D :, :D] = rest
                nt_keep[s] = tall4_weight(both.T)

    def feed(layer, index, mid, inner):
        where = block(index)
        act, slope = gelu_pair(inner + vector("inner_bias", layer))
        slope_keep[layer, where, :] = slope
        pieces = thirds(act)
        act_keep[layer, where, :] = beside(pieces[0], pieces[1])
        return mid + tall6(pieces, (w_out0[layer], w_out1[layer])) + vector("outer_bias", layer)

    def front_zero(index, _):
        normalise(0, index, dot(lifted[block(index), :], w0_kv[...]))
        return 0

    lax.fori_loop(0, rows_all, front_zero, 0)
    summarise(0)

    def layer_zero(index, _):
        where = block(index)
        s = index // steps
        data = lifted[where, :]
        out = feed(0, index, dot(data, w0_g[s]), dot(data, w0_u[s]))
        d_keep[where, :] = out
        pieces = thirds(out)
        h1_keep[where, :] = beside(*pieces)
        normalise(1, index, wide6(pieces, w_kv[...]))
        return 0

    lax.fori_loop(0, rows_all, layer_zero, 0)
    summarise(1)

    def pieces_of(ref, where, number=3):
        value = ref[where, : number * D]
        return [value[:, i * D : (i + 1) * D] for i in range(number)]

    def layer_one(index, _):
        where = block(index)
        s = index // steps
        pieces = pieces_of(h1_keep, where)
        mid = d_keep[where, :] + tall6(pieces, (wz[s, : 2 * D, :], wz[s, 2 * D :, :D]))
        pieces = thirds(mid)
        mid_keep[where, :] = beside(pieces[0], pieces[1])
        out = feed(1, index, mid, wide6(pieces, w_in[...]))
        h2_keep[where, :] = beside(*thirds(out))
        return 0

    lax.fori_loop(0, rows_all, layer_one, 0)

    def dense_rows(part):
        start = D + (part - 1) * FREQ if part else 0
        return turned_ref[:, start : start + (FREQ if part else D)].T

    proj0, proj1 = tall6_weight(doubled(dense_rows(0)))
    locals6 = [tall6_weight(doubled(dense_rows(part))) for part in (1, 2, 3)]
    locals4 = [tall4_weight(doubled(dense_rows(part).T)) for part in (1, 2, 3)]
    own = lax.broadcasted_iota(jnp.int32, (2 * count * MODES, MODES * D), 1) // D == lax.rem(
        lax.broadcasted_iota(jnp.int32, (2 * count * MODES, MODES * D), 0), MODES
    )

    def mode_rows(coef):
        cosine, sine = coef[:MODES], coef[MODES:]
        c = [cosine[:, s * FREQ : (s + 1) * FREQ] for s in range(count)]
        d = [sine[:, s * FREQ : (s + 1) * FREQ] for s in range(count)]
        return above(
            *[beside(c[s], d[s]) for s in range(count)], *[beside(d[s], -c[s]) for s in range(count)]
        )

    def spread_rows(rows):
        return jnp.where(own, beside(*([rows] * MODES)), 0.0)

    def unpack(rows):
        lead = count * MODES
        return above(
            *[beside(*[rows[j * lead + s * MODES : j * lead + (s + 1) * MODES] for s in range(count)]) for j in (0, 1)]
        )

    def pack(value):
        return above(
            *[
                value[j * MODES : (j + 1) * MODES, s * FREQ : (s + 1) * FREQ]
                for j in (0, 1)
                for s in range(count)
            ]
        )

    def set_stack(value):
        high, middle, low = thirds(value)
        stack_ref[...] = above(
            high, high, middle, middle, low, high, jnp.zeros((4 * MODES, D), BF16)
        )

    def take_coef(index, high, low):
        coef_acc[...] += dot(trow_ref[index], beside(high, low))

    def mix_forward(layer):
        coef = quarters(coef_acc[...]) * (1.0 / math.sqrt(points))
        coef_acc[...] = jnp.zeros_like(coef_acc)
        rows = mode_rows(coef)
        coef_keep[layer] = rows
        set_stack(unpack(exact(spread_rows(rows), spec_ref[layer])) * (1.0 / math.sqrt(MODES)))

    def mix_back(layer):
        cot = pack(quarters(coef_acc[...])) * (1.0 / math.sqrt(MODES))
        coef_acc[...] = jnp.zeros_like(coef_acc)
        kept_rows = coef_keep[layer]
        padded = beside(cot, jnp.zeros_like(cot))
        for k in range(MODES):
            for r in range(2 * count):
                mode_send[layer * MODES + k, r : r + 1, :] = kept_rows[r * MODES + k : r * MODES + k + 1]
                mode_send[layer * MODES + k, 4 + r : 5 + r, :] = padded[r * MODES + k : r * MODES + k + 1]
        wide = jnp.where(own, exact(cot, spec_ref[layer], 1, 1), 0.0)
        kept = wide[:, :D]
        for k in range(1, MODES):
            kept = kept + wide[:, k * D : (k + 1) * D]
        lead = count * MODES
        first, second = kept[:lead], kept[lead:]
        rows = above(first[:, :FREQ] - second[:, FREQ:], first[:, FREQ:] + second[:, :FREQ])
        set_stack(unpack(rows) * (1.0 / math.sqrt(points)))

    def project_step(index, _):
        where = block(index)
        first = h2_keep[block(index), :]
        second = h2_keep[block(index + steps), :]
        pieces = [beside(first[:, i * D : (i + 1) * D], second[:, i * D : (i + 1) * D]) for i in range(3)]
        field = tall6(pieces, (proj0, proj1)) + vector("proj_bias", 0)
        pieces = thirds(field)
        z_keep[0, where, :] = beside(*pieces)
        take_coef(index, pieces[0], pieces[1])
        return 0

    lax.fori_loop(0, steps, project_step, 0)
    mix_forward(0)

    def fourier_field(layer, where):
        pieces = pieces_of(z_keep.at[layer], where)
        inner = dot(table_ref[where, :], stack_ref[...]) + (
            tall6(pieces, locals6[layer]) + vector("fourier_bias", layer)
        )
        return gelu_pair(inner)

    def fourier_one(index, _):
        where = block(index)
        field, slope = fourier_field(0, where)
        zs_keep[where, :] = slope
        pieces = thirds(field)
        z_keep[1, where, :] = beside(*pieces)
        take_coef(index, pieces[0], pieces[1])
        return 0

    lax.fori_loop(0, steps, fourier_one, 0)
    mix_forward(1)

    lane = lax.broadcasted_iota(jnp.int32, (2 * D, 2 * D), 1)
    row = lax.broadcasted_iota(jnp.int32, (2 * D, 2 * D), 0)
    inner_row = lax.rem(row, D)
    same = row // D == lax.rem(lane, D) // FREQ
    pick_target = (lane < D) & (inner_row >= 15) & (inner_row < 18)
    pick_mask = (lane >= D) & (inner_row == 18)
    spread = jnp.where(same & (pick_target | pick_mask), 1.0, 0.0).astype(BF16)
    out_row = vector("head_out", 0)
    out_column = jnp.sum(eye * out_row, 1, keepdims=True)
    half_blocks = (
        lax.broadcasted_iota(jnp.int32, (D, D), 0) // FREQ == lax.broadcasted_iota(jnp.int32, (D, D), 1) // FREQ
    )
    out_weight = tall6_weight(jnp.where(half_blocks, out_column, 0.0))

    def pair_product(first, second):
        return dot(beside(*first), beside(*second), 0, 0)

    def loss_step(index, _):
        where = block(index)
        field, slope = fourier_field(1, where)
        pieces = thirds(field)
        hidden, hidden_slope = gelu_pair(tall6(pieces, locals6[2]) + vector("head_bias", 0))
        pred = tall6(thirds(hidden), out_weight)
        known = dot(beside(lifted[where, :], lifted[block(index + steps), :]), spread)
        diff = pred - known[:, :D]
        valid = known[:, D:]
        cot = (2.0 * valid) * diff
        b_acc[0:8, :D] += column_sum(valid * diff * diff)
        b_acc[8:16, :D] += column_sum(valid)
        b_acc[16:24, :D] += column_sum(hidden * cot)
        cot = cot * out_row * hidden_slope
        b_acc[24:32, :D] += column_sum(cot)
        split = halves(cot)
        sq_acc[2] += pair_product(pieces[:2], split)
        cot = tall4(split, locals4[2]) * slope
        b_acc[32:40, :D] += column_sum(cot)
        split = halves(cot)
        e_keep[where, :] = beside(*split)
        sq_acc[1] += pair_product(pieces_of(z_keep.at[1], where, 2), split)
        take_coef(index, *split)
        return 0

    lax.fori_loop(0, steps, loss_step, 0)
    mix_back(1)

    def fourier_cot(layer, where):
        return tall4(pieces_of(e_keep, where, 2), locals4[layer]) + dot(table_ref[where, :], stack_ref[...])

    def fourier_back(index, _):
        where = block(index)
        cot = fourier_cot(1, where) * zs_keep[where, :]
        b_acc[40:48, :D] += column_sum(cot)
        split = halves(cot)
        e_keep[where, :] = beside(*split)
        sq_acc[0] += pair_product(pieces_of(z_keep.at[0], where, 2), split)
        take_coef(index, *split)
        return 0

    lax.fori_loop(0, steps, fourier_back, 0)
    mix_back(0)
    mode_land[mine] = mode_send[mine]
    spread_to_all(devices, mine, lambda r: mode_send.at[r], mode_land, mode_sends, mode_recvs, True)
    proj_back = wide4_weight(doubled(turned_ref[:, :D]))

    def project_back(index, _):
        where = block(index)
        later = block(index + steps)
        cot = fourier_cot(0, where)
        b_acc[48:56, :D] += column_sum(cot)
        split = halves(cot)
        first = pieces_of(h2_keep, where, 2)
        second = pieces_of(h2_keep, later, 2)
        p_acc[...] += dot(beside(first[0], second[0], first[1], second[1]), beside(*split), 0, 0)
        rows = wide4(split, proj_back)
        d_keep[where, :] = rows[:, :D]
        d_keep[later, :] = rows[:, D:]
        return 0

    lax.fori_loop(0, steps, project_back, 0)
    spread_to_all(devices, mine, lambda r: mode_send.at[r], mode_land, mode_sends, mode_recvs, False)
    landed = mode_land[...].reshape(devices * 8, D)
    shifted = above(landed[4:], landed[:4])
    row = lax.broadcasted_iota(jnp.int32, landed.shape, 0)
    product = exact(jnp.where(lax.rem(row, 8) < 4, landed, 0.0), shifted[:, :FREQ], 0, 0)
    mode_out[mode_route.area(mode_route.own, FREQ), :] = beside(product[:FREQ], product[FREQ:])
    mode_route.start(4)

    def feed_back(layer, index, cot):
        where = block(index)
        base = 56 + layer * 16
        b_acc[base : base + 8, :D] += column_sum(cot)
        split = halves(cot)
        act = act_keep[layer, where, :]
        w2_acc[layer] += dot(beside(*split), act[:, :FF], 0, 0)
        w2_acc[layer, :D, :] += dot(split[0], act[:, FF:], 0, 0)
        inner = wide4(split, w_outt[layer]) * slope_keep[layer, where, :]
        b_acc[base + 8 : base + 16, :] += column_sum(inner)
        return split, halves(inner)

    def layer_one_back(index, _):
        for number, stage in ((2, 4), (4, 5), (6, 6)):

            @pl.when(index == number)
            def _():
                mode_route.step(stage)

        where = block(index)
        cot = d_keep[where, :]
        _, (high, low) = feed_back(1, index, cot)
        mid = mid_keep[where, :]
        w1_acc[...] += dot(mid, high, 0, 0)
        w1_acc[:D, :] += dot(mid[:, :D], low, 0, 0)
        cot = cot + tall4((high, low), w_int[...])
        d_keep[where, :] = cot
        y_acc[index // steps] += pair_product(pieces_of(h1_keep, where, 2), halves(cot))
        return 0

    lax.fori_loop(0, rows_all, layer_one_back, 0)

    def attend_back(layer, products):
        weight = attn_ref[layer]
        query, outer = weight[:, :D], weight[:, 3 * D :]
        key_gain, value_gain = vector("key_gain", layer), vector("value_gain", layer)
        key_column = jnp.sum(eye * key_gain, 1, keepdims=True)
        key_total = jnp.zeros((D, 1), F32)
        value_total = jnp.zeros((1, D), F32)
        query_grad = jnp.zeros((D, D), F32)
        outer_grad = jnp.zeros((D, D), F32)
        for s in range(count):
            plain, summary, mixed = small_keep[layer, s, 0], small_keep[layer, s, 1], small_keep[layer, s, 2]
            turned = exact(query, products[s], 0, 0)
            outer_grad += exact(summary, turned, 0, 0)
            if layer:
                query_grad += exact(products[s], mixed, 1, 1)
            cot = jnp.where(blocks, exact(turned, outer, 1, 1), 0.0)
            both = cot * plain
            key_total += jnp.sum(both * value_gain, 1, keepdims=True)
            value_total += jnp.sum(both * key_column, 0, keepdims=True)
            scaled = key_column * cot * value_gain * (1.0 / points)
            t_keep[s, 0] = tall4_weight(scaled.T)
            t_keep[s, 1] = tall4_weight(scaled)
        if layer:
            early[5 * D + FREQ : 6 * D + FREQ, :] = query_grad
            early[6 * D + FREQ : 7 * D + FREQ, :] = outer_grad
        else:
            late[6 * D : 7 * D, :] = outer_grad
        return jnp.sum(eye * key_total, 0, keepdims=True), value_total

    mode_route.finish(7)
    for i in range(2):
        half = slice(i * D, (i + 1) * D)
        early[i * D : (i + 1) * D, :] = w1_acc[:D, half] + w1_acc[D:, half]
        early[(2 + i) * D : (3 + i) * D, :] = w2_acc[1, :D, half] + w2_acc[1, D:, half]
    sums = p_acc[...]
    sums = fold(sums[: 2 * D] + sums[2 * D :])
    early[4 * D : 4 * D + FREQ, :] = (sums[:D, :FREQ] + sums[D:, FREQ:]).T
    squares = []
    for part in range(3):
        sums = quarters(sq_acc[part])
        squares.append((sums[:FREQ, :FREQ] + sums[FREQ:, FREQ:]).T)
    early[4 * D + FREQ : 5 * D, :] = beside(squares[0], squares[1])
    early[5 * D : 5 * D + FREQ, :] = beside(squares[2], jnp.zeros_like(squares[2]))
    early[7 * D + FREQ :, :] = jnp.zeros((D // 2, D), F32)
    gains = [None, None]
    gains[1] = attend_back(1, [quarters(y_acc[s]) for s in range(count)])

    def norm_back(index, normal, scale):
        s = index // steps
        key, value = normal[:, :D], normal[:, D:]
        key_cot = tall4(halves(value), t_keep[s, 0])
        value_cot = tall4(halves(key), t_keep[s, 1])
        mean = dot(beside(*halves(key_cot * key)), mean_weight) * (HEADS / D)
        return beside(scale[:, :D] * (key_cot - key * mean), scale[:, D:] * (value_cot - value * mean))

    early_route.start(0)

    def middle_back(index, _):
        for number in range(1, 8):

            @pl.when(index == number)
            def _():
                early_route.step(number - 1)

        where = block(index)
        s = index // steps
        cot = norm_back(index, x_keep[where, :], r_keep[where, :])
        high, low = halves(cot)
        kept = h1_keep[where, : 2 * D]
        kv_acc[...] += dot(kept, high, 0, 0)
        kv_acc[:D, :] += dot(kept[:, :D], low, 0, 0)
        out = d_keep[where, :]
        out = out + tall4(halves(out), nt_keep[s]) + tall4((high, low), w_kvt[...])
        outer, inner = feed_back(0, index, out)
        v_acc[s] += dot(lrows[index], beside(*outer))
        u_acc[s] += dot(lrows[index], beside(*inner))
        return 0

    lax.fori_loop(0, rows_all, middle_back, 0)
    early_route.finish(7)

    def lift_sum(value):
        value = fold(value)
        return above(
            value[0:1] + value[1:2] + value[2:3],
            value[3:4] + value[4:5] + value[5:6],
            value[6:7],
            jnp.zeros((5, value.shape[1]), F32),
        )

    inner_rows = [lift_sum(u_acc[s]) for s in range(count)]
    value_rows = [lift_sum(v_acc[s]) + exact(inner_rows[s], ffn_ref[0, 0], 1, 1) for s in range(count)]
    gains[0] = attend_back(0, [exact(lift_rows, value_rows[s], 0, 0) for s in range(count)])

    query_rows = jnp.zeros((8, D), F32)
    lift_part = jnp.zeros((8, D), F32)
    inner_grad = jnp.zeros((D, FF), F32)
    for s in range(count):
        query_rows += exact(value_rows[s], small_keep[0, s, 2], 1, 1)
        lift_part += value_rows[s] + exact(value_rows[s], n_keep[0, s], 1, 1)
        inner_grad += exact(mid_rows[s], inner_rows[s], 0, 0)
    for i in range(2):
        half = slice(i * D, (i + 1) * D)
        late[i * D : (i + 1) * D, :] = exact(kv_acc[:D, half] + kv_acc[D:, half], centre)
        late[(2 + i) * D : (3 + i) * D, :] = w2_acc[0, :D, half] + w2_acc[0, D:, half]
        late[(4 + i) * D : (5 + i) * D, :] = inner_grad[:, half]

    def bias(slot, width=D):
        return jnp.sum(b_acc[slot * 8 : slot * 8 + 8, :width], 0, keepdims=True)

    rows = [jnp.zeros((3, D), F32)]
    for layer in range(LAYERS):
        inner = bias(8 + 2 * layer, FF)
        rows += [gains[layer][0], gains[layer][1], inner[:, :D], inner[:, D:], bias(7 + 2 * layer)]
    short = [fold(bias(slot)) for slot in (6, 5, 4, 3, 2)]
    rows += [beside(short[0], short[1]), beside(short[2], short[3]), beside(short[4], jnp.zeros((1, FREQ), F32))]
    late[7 * D : 7 * D + 16, :] = above(*rows)
    lanes = lax.broadcasted_iota(jnp.int32, (1, D), 1)
    first = jnp.where(lax.rem(lanes, FREQ) == 0, bias(0), 0.0)
    second = jnp.where(lax.rem(lanes, FREQ) == 0, bias(1), 0.0)
    late[7 * D + 16 : 7 * D + 24, :] = above(first, second, jnp.zeros((6, D), F32))
    late[7 * D + 24 : 7 * D + 32, :] = query_rows
    late[7 * D + 32 : 7 * D + 40, :] = lift_part
    late[7 * D + 40 :, :] = jnp.zeros((D - 40, D), F32)
    late_route.start(0)

    def front_back(index, _):
        for number, stage in ((3, 0), (6, 1)):

            @pl.when(index == number)
            def _():
                late_route.step(stage)

        centred = dot(lifted[block(index), :], w0_kv[...])
        scale = head_scale(centred)
        cot = norm_back(index, centred * scale, scale)
        vt_acc[...] += dot(lrows[index], beside(*halves(cot)))
        return 0

    lax.fori_loop(0, rows_all, front_back, 0)
    turned = lift_sum(vt_acc[...])
    tail_send[...] = above(turned[:4, :D], turned[:4, D:])
    tail_land[mine] = tail_send[...]
    spread_to_all(devices, mine, lambda r: tail_send, tail_land, tail_sends, tail_recvs, True)
    for stage in range(2, 7):
        late_route.step(stage)
    late_route.finish(7)
    spread_to_all(devices, mine, lambda r: tail_send, tail_land, tail_sends, tail_recvs, False)
    summed = jnp.sum(tail_land[...], 0)
    zero = jnp.zeros((4, 2 * D), F32)
    turned = above(beside(summed[:4], summed[4:]), zero)
    joined = exact(lift_rows, turned, 0, 0)
    tail_out[:D, :] = exact(lift_rows, late_out[7 * D + 24 : 7 * D + 32, :], 0, 0)
    tail_out[D : 2 * D, :] = exact(joined[:, :D], centre)
    tail_out[2 * D : 3 * D, :] = exact(joined[:, D:], centre)
    tail_out[3 * D :, :] = late_out[7 * D + 32 : 7 * D + 40, :] + exact(turned, cent_keep[0], 1, 1)


def tables(points):
    order = np.arange(MODES)[:, None]
    angle = (order * np.arange(points)[None, :]) % points * (2.0 * math.pi / points)
    full = np.concatenate([np.cos(angle), np.sin(angle)], 0).astype(np.float32)
    kind = np.dtype(ml_dtypes.bfloat16)
    high = full.astype(kind)
    rest = full - high.astype(np.float32)
    middle = rest.astype(kind)
    low = (rest - middle.astype(np.float32)).astype(kind)
    zero = np.zeros((4 * MODES, points), kind)
    column = np.concatenate([high, middle, high, middle, high, low, zero], 0).T
    row = np.concatenate([high, middle], 0).reshape(4 * MODES, points // ROWS, ROWS).transpose(1, 0, 2)
    return np.ascontiguousarray(column), np.ascontiguousarray(row)


def summed_grads(samples_in, target, mask, attn_w, ffn_w, spec_w, turned_w, vectors):
    parts = samples_in.shape[0] // 2
    count, points = 2, samples_in.shape[2] * parts
    devices = FLAYERS * MODES
    total = count * points
    steps = points // ROWS
    column, row = tables(points)
    vmem = pl.BlockSpec(memory_space=pltpu.VMEM)
    first = [
        ((parts, 8, samples_in.shape[2]), F32),
        ((parts, 8, samples_in.shape[2]), F32),
        ((NVEC_ROWS, D), F32),
        ((8 * D, D), F32),
        ((8 * D, D), F32),
        ((8 * D, D), F32),
        ((8 * D, D), F32),
        ((devices, 8, D), F32),
        ((devices, 8, D), F32),
        ((8, D), F32),
        ((devices, 8, D), F32),
    ]
    numbers = (36, 36, parts - 1, parts - 1, devices - 1, devices - 1, devices - 1, devices - 1)
    scratch = [
        ((total, D), BF16),
        ((total // ROWS, 16, ROWS), BF16),
        ((6 * D, 2 * D), BF16),
        ((4 * D, 2 * D), BF16),
        ((6 * D, FF), BF16),
        ((2 * FF, 2 * D), BF16),
        ((count, D, FF), BF16),
        ((count, 8, D), F32),
        ((LAYERS, 2 * FF, 2 * D), BF16),
        ((LAYERS, 2 * FF, D), BF16),
        ((LAYERS, 4 * D, FF), BF16),
        ((total, 2 * D), F32),
        ((total, 2 * D), F32),
        ((LAYERS, total, FF), F32),
        ((LAYERS, total, 2 * FF), BF16),
        ((total, 2 * D), BF16),
        ((total, 3 * D), BF16),
        ((total, 3 * D), BF16),
        ((FLAYERS, points, 3 * D), BF16),
        ((points, D), F32),
        ((points, 2 * D), BF16),
        ((LAYERS, count, 2 * D, 2 * D), F32),
        ((D, 2 * D), BF16),
        ((count, D, D), BF16),
        ((LAYERS, count, D, D), F32),
        ((LAYERS, count, 3, D, D), F32),
        ((count, 2 * D, 2 * D), BF16),
        ((LAYERS, D, 2 * D), F32),
        ((4 * MODES, 2 * D), F32),
        ((FLAYERS, 2 * count * MODES, D), F32),
        ((2 * D, D), BF16),
        ((3, 2 * D, 2 * D), F32),
        ((4 * D, 2 * D), F32),
        ((count, 2 * D, 2 * D), F32),
        ((LAYERS, 2 * D, FF), F32),
        ((2 * D, FF), F32),
        ((2 * D, 2 * D), F32),
        ((count, 16, 2 * D), F32),
        ((count, 16, 2 * FF), F32),
        ((16, 4 * D), F32),
        ((96, FF), F32),
        ((total, D), F32),
        ((count, 2, 2 * D, 2 * D), BF16),
        ((count, 4 * D, 2 * D), BF16),
    ]
    shapes = [(8 * D, D), (8 * D, D), (devices * FREQ, D), (3 * D + 8, D)]
    return pl.pallas_call(
        step_kernel,
        out_shape=[jax.ShapeDtypeStruct(shape, F32) for shape in shapes],
        in_specs=[vmem] * 10,
        out_specs=[vmem] * 4,
        scratch_shapes=[pltpu.VMEM(*item) for item in first]
        + [pltpu.SemaphoreType.DMA((number,)) for number in numbers]
        + [pltpu.VMEM(*item) for item in scratch],
        compiler_params=pltpu.CompilerParams(
            vmem_limit_bytes=64 * 2**20 - 2**17, collective_id=0, has_side_effects=True
        ),
    )(
        samples_in,
        target,
        mask,
        attn_w,
        ffn_w,
        spec_w,
        turned_w,
        vectors,
        jnp.asarray(column),
        jnp.asarray(row),
    )


def update_kernel(
    early,
    late,
    modes,
    tail,
    vectors,
    vector_m,
    vector_v,
    attn_w,
    ffn_w,
    spec_w,
    turned_w,
    attn_m,
    ffn_m,
    spec_m,
    turned_m,
    attn_v,
    ffn_v,
    spec_v,
    turned_v,
    loss_out,
    count_out,
    weight_out,
    update_out,
    ratio_out,
    vector_m_out,
    vector_v_out,
    vector_w_out,
    vector_low_out,
    *rest,
):
    outs, scratch = rest[:16], rest[16:]
    ins = (attn_w, ffn_w, spec_w, turned_w, attn_m, ffn_m, spec_m, turned_m, attn_v, ffn_v, spec_v, turned_v)
    held, fresh = scratch[:12], scratch[12:28]
    flat, in_sems, out_sems = scratch[28:]

    blocks = [(2, 0), (2, 1), (1, 1), (0, 1), (0, 0), (1, 0), (3, None)]

    def view(ref, part):
        return ref if part is None else ref.at[part]

    def load(slot, kind):
        array, part = blocks[slot]
        number = kind * 4 + array
        return pltpu.make_async_copy(
            view(ins[number], part), view(held[number], part), in_sems.at[slot * 3 + kind]
        )

    def store(slot, kind):
        array, part = blocks[slot]
        number = kind * 4 + array
        return pltpu.make_async_copy(
            view(fresh[number], part), view(outs[number], part), out_sems.at[slot * 4 + kind]
        )

    for slot in range(len(blocks)):
        for kind in range(3):
            load(slot, kind).start()
    misc = late[7 * D + 16 : 7 * D + 24, :]
    loss_out[0] = jnp.sum(misc[0:1])
    valid = jnp.sum(misc[1:2], keepdims=True)
    count_out[0] = jnp.sum(misc[1:2])
    scale = 1.0 / valid

    def moved(weight, grad, first, second):
        first_new = BETA_ONE * first + (1.0 - BETA_ONE) * grad
        second_new = BETA_TWO * second + (1.0 - BETA_TWO) * grad * grad
        update = (
            first_new
            / (1.0 - BETA_ONE**STEP)
            / (jnp.sqrt(second_new / (1.0 - BETA_TWO**STEP)) + ADAM_EPS)
            + DECAY * weight
        )
        return first_new, second_new, update

    def note(slot, weight_sum, update_sum):
        weight_norm, update_norm = jnp.sqrt(weight_sum), jnp.sqrt(update_sum)
        ratio = weight_norm / (update_norm + ADAM_EPS)
        weight_out[slot] = weight_norm[0, 0]
        update_out[slot] = update_norm[0, 0]
        ratio_out[slot] = ratio[0, 0]
        return RATE * ratio

    def total(value):
        return jnp.sum(column_sum(value), keepdims=True)

    for i in range(NVEC_ROWS):
        start = i * D
        size = min(D, flat.shape[0] - start)
        row = tail[3 * D + i : 3 * D + i + 1, :] if i < 3 else late[7 * D + i : 7 * D + i + 1, :]
        flat[start : start + size] = (row * scale)[:, :size].reshape(size)
    weight = vectors[...]
    first_new, second_new, update = moved(weight, flat[...], vector_m[...], vector_v[...])
    vector_m_out[...] = first_new
    vector_v_out[...] = second_new
    rate = note(
        7,
        jnp.sum(weight * weight).reshape(1, 1),
        jnp.sum(update * update).reshape(1, 1),
    )
    flat[...] = jnp.broadcast_to(rate, (1, D)).reshape(D)[0] * update
    weight = weight - flat[...]
    vector_w_out[...] = weight
    vector_low_out[...] = weight.astype(BF16)

    def grad_blocks(array, part):
        if array == 0:
            if part:
                places = [(early, 5 * D + FREQ), (late, 0), (late, D), (early, 6 * D + FREQ)]
            else:
                places = [(tail, 0), (tail, D), (tail, 2 * D), (late, 6 * D)]
            return [
                (ref, start, D, 0, (slice(None), slice(j * D, (j + 1) * D)))
                for j, (ref, start) in enumerate(places)
            ]
        if array == 1:
            ref, starts = (early, (0, 1, 2, 3)) if part else (late, (4, 5, 2, 3))
            return [
                (ref, starts[j] * D, D, 0, (j // 2, slice(None), slice(j % 2 * D, j % 2 * D + D)))
                for j in range(4)
            ]
        if array == 3:
            return [
                (early, 4 * D, FREQ, 0, (slice(None), slice(0, D))),
                (early, 4 * D + FREQ, FREQ, 0, (slice(None), slice(D, 2 * D))),
                (early, 5 * D, FREQ, 0, (slice(None), slice(2 * D, 2 * D + FREQ))),
            ]
        return [
            (modes, (part * MODES + k) * FREQ, FREQ, j * FREQ, (k, j))
            for k in range(MODES)
            for j in range(2)
        ]

    for slot, (array, part) in enumerate(blocks):
        for kind in range(3):
            load(slot, kind).wait()
        weight_ref, first_ref, second_ref = [view(held[kind * 4 + array], part) for kind in range(3)]
        first_out, second_out, weight_new, low_out = [view(fresh[kind * 4 + array], part) for kind in range(4)]
        weight_sum = jnp.zeros((1, 1), F32)
        update_sum = jnp.zeros((1, 1), F32)
        pieces = grad_blocks(array, part)
        for ref, start, rows, lane, where in pieces:
            weight = weight_ref[where]
            width = weight.shape[1]
            grad = ref[start : start + rows, lane : lane + width] * scale
            first_new, second_new, update = moved(weight, grad, first_ref[where], second_ref[where])
            first_out[where] = first_new
            second_out[where] = second_new
            weight_new[where] = update
            weight_sum += total(weight * weight)
            update_sum += total(update * update)
        store(slot, 0).start()
        store(slot, 1).start()
        place = (0 + part if array == 0 else 2 + part if array == 1 else 4 + part) if part is not None else 6
        rate = note(place, weight_sum, update_sum)
        for ref, start, rows, lane, where in pieces:
            weight = weight_ref[where] - rate * weight_new[where]
            weight_new[where] = weight
            low_out[where] = weight.astype(BF16)
        store(slot, 2).start()
        store(slot, 3).start()
    for slot in range(len(blocks)):
        for kind in range(4):
            store(slot, kind).wait()


def fast_body(samples_in, target, mask, attn_w, ffn_w, spec_w, dense_w, vectors, *moments):
    flat_spec = spec_w.reshape(FLAYERS, MODES * 2 * FREQ, FREQ)
    grads = summed_grads(samples_in, target, mask, attn_w, ffn_w, flat_spec, dense_w.T, vectors)
    sets = [
        (attn_w, ffn_w, spec_w, dense_w.T),
        (moments[0], moments[1], moments[2], moments[3].T),
        (moments[5], moments[6], moments[7], moments[8].T),
    ]
    vmem = pl.BlockSpec(memory_space=pltpu.VMEM)
    smem = pl.BlockSpec(memory_space=pltpu.SMEM)
    anywhere = pl.BlockSpec(memory_space=pl.ANY)
    shapes = [item.shape for item in sets[0]]
    kinds = (F32, F32, F32, BF16)
    scalar = [jax.ShapeDtypeStruct((1,), F32)] * 2 + [jax.ShapeDtypeStruct((8,), F32)] * 3
    line = [jax.ShapeDtypeStruct(vectors.shape, kind) for kind in kinds]
    arrays = [jax.ShapeDtypeStruct(shape, kind) for kind in kinds for shape in shapes]
    out = pl.pallas_call(
        update_kernel,
        out_shape=scalar + line + arrays,
        in_specs=[vmem] * 7 + [anywhere] * 12,
        out_specs=[smem] * 5 + [vmem] * 4 + [anywhere] * 16,
        scratch_shapes=[pltpu.VMEM(shape, F32) for _ in range(3) for shape in shapes]
        + [pltpu.VMEM(shape, kind) for kind in kinds for shape in shapes]
        + [pltpu.VMEM(vectors.shape, F32), pltpu.SemaphoreType.DMA((21,)), pltpu.SemaphoreType.DMA((28,))],
        compiler_params=pltpu.CompilerParams(vmem_limit_bytes=60 * 2**20),
    )(*grads, vectors, moments[4], moments[9], *sets[0], *sets[1], *sets[2])
    loss_sum, valid_count, weight_norms, update_norms, ratios = out[:5]
    line, arrays = out[5:9], out[9:]
    results = [loss_sum.reshape(()), valid_count.reshape(())]
    for array in range(4):
        for kind in range(4):
            item = arrays[kind * 4 + array]
            results.append(item.T if array == 3 else item)
    return tuple(results + list(line) + [weight_norms, update_norms, ratios])


def choose_body(*arrays):
    samples_in = arrays[0]
    dp, parts = lax.axis_size("dp"), lax.axis_size("pts")
    fits = dp * parts == FLAYERS * MODES and dp == 4 and samples_in.shape[0] == 2 * parts
    return (fast_body if fits and samples_in.shape[2] * parts % ROWS == 0 else body)(*arrays)


def solution(mesh):
    placed = (
        P("dp", None, "pts"),
        P("dp", "pts"),
        P("dp", "pts"),
        P(),
        P(),
        P(),
        P(),
        P(),
        P(),
        P(),
        P(),
        P(),
        P(),
        P(),
        P(),
        P(),
        P(),
        P(),
    )
    return jax.shard_map(
        choose_body,
        mesh=mesh,
        in_specs=placed,
        out_specs=(
            P(),
            P(),
            P(),
            P(),
            P(),
            P(),
            P(),
            P(),
            P(),
            P(),
            P(),
            P(),
            P(),
            P(),
            P(),
            P(),
            P(),
            P(),
            P(),
            P(),
            P(),
            P(),
            P(),
            P(),
            P(),
        ),
        check_vma=False,
    )
```

```python
import math

import jax
import jax.numpy as jnp
import ml_dtypes
import numpy as np
from jax import lax
from jax.experimental import pallas as pl
from jax.experimental.pallas import tpu as pltpu
from jax.sharding import PartitionSpec as P

D = 128
HEADS = 4
FF = 256
FREQ = 64
MODES = 16
LAYERS = 2
FLAYERS = 2
STEP = 5


HIGH = lax.Precision.HIGHEST
NORM_EPS = 1e-05
BETA_ONE = 0.5
BETA_TWO = 0.5
RATE = 0.2
DECAY = 0.01
ADAM_EPS = 1e-06


def vector_table():
    entries = [("lift_value", 0, D), ("lift_coord", 0, D), ("lift_bias", 0, D)]
    for layer in range(LAYERS):
        entries = entries + [
            ("key_gain", layer, D),
            ("value_gain", layer, D),
            ("inner_bias", layer, FF),
            ("outer_bias", layer, D),
        ]
    entries = entries + [("proj_bias", 0, FREQ)]
    for layer in range(FLAYERS):
        entries = entries + [("fourier_bias", layer, FREQ)]
    entries = entries + [("head_bias", 0, FREQ), ("head_out", 0, FREQ)]
    offsets = {}
    start = 0
    for label, layer, length in entries:
        offsets[label, layer] = (start, length)
        start = start + length
    return offsets


def pick(vectors, label, layer):
    start, length = vector_table()[label, layer]
    return vectors[start : start + length]


def head_norm(values, gain):
    centred = values - jnp.mean(values, -1, keepdims=True)
    scaled = centred * lax.rsqrt(jnp.mean(centred * centred, -1, keepdims=True) + NORM_EPS)
    return scaled * gain.reshape(HEADS, D // HEADS)


def lift(params, inputs):
    vectors = params[4]
    value = inputs[..., 0, :, None]
    coord = inputs[..., 1, :, None]
    return (
        value * pick(vectors, "lift_value", 0)
        + coord * pick(vectors, "lift_coord", 0)
        + pick(vectors, "lift_bias", 0)
    )


def attn_front(params, rows, layer, points):
    weight = params[0][layer]
    vectors = params[4]
    mixed = jnp.einsum("...d,de->...e", rows, weight[:, : 3 * D], precision=HIGH)
    shape = rows.shape[:-1] + (HEADS, D // HEADS)
    query = mixed[..., :D].reshape(shape)
    keys = head_norm(mixed[..., D : 2 * D].reshape(shape), pick(vectors, "key_gain", layer))
    values = head_norm(mixed[..., 2 * D :].reshape(shape), pick(vectors, "value_gain", layer))
    partial_sum = jnp.einsum("...phe,...phf->...hef", keys, values, precision=HIGH) / points
    return (query, partial_sum)


def attn_rear(params, rows, query, summary, layer):
    weight = params[0][layer]
    attended = jnp.einsum("...phe,...hef->...phf", query, summary, precision=HIGH).reshape(
        rows.shape
    )
    return rows + jnp.einsum("...d,de->...e", attended, weight[:, 3 * D :], precision=HIGH)


def ffn_block(params, rows, layer):
    weight = params[1][layer]
    vectors = params[4]
    inner = jnp.einsum("...d,df->...f", rows, weight[0], precision=HIGH) + pick(
        vectors, "inner_bias", layer
    )
    outer = jnp.einsum("...f,df->...d", jax.nn.gelu(inner), weight[1], precision=HIGH)
    return rows + outer + pick(vectors, "outer_bias", layer)


def project(params, rows):
    return jnp.einsum("...d,df->...f", rows, params[3][:D], precision=HIGH) + pick(
        params[4], "proj_bias", 0
    )


def mode_table(count, total):
    position = jnp.arange(count, dtype=jnp.int32)
    orders = jnp.arange(MODES, dtype=jnp.int32)
    phase = orders[:, None] * position[None, :] % total
    angle = phase.astype(jnp.float32) * (2.0 * math.pi / total)
    return jnp.concatenate([jnp.cos(angle), jnp.sin(angle)], 0)


def spectral_mix(coef, spec, first, width):
    columns = lax.dynamic_slice_in_dim(spec, first, width, 3)
    cosine = coef[..., :MODES, :]
    sine = coef[..., MODES:, :]
    real_part = columns[:, 0]
    imag_part = columns[:, 1]
    mixed_cos = jnp.einsum("...mf,mfg->...mg", cosine, real_part, precision=HIGH) + jnp.einsum(
        "...mf,mfg->...mg", sine, imag_part, precision=HIGH
    )
    mixed_sin = jnp.einsum("...mf,mfg->...mg", sine, real_part, precision=HIGH) - jnp.einsum(
        "...mf,mfg->...mg", cosine, imag_part, precision=HIGH
    )
    return jnp.concatenate([mixed_cos, mixed_sin], -2)


def fourier_end(params, back, rows, layer):
    local = params[3][D + layer * FREQ : D + (layer + 1) * FREQ]
    inner = back + jnp.einsum("...f,fg->...g", rows, local, precision=HIGH)
    return jax.nn.gelu(inner + pick(params[4], "fourier_bias", layer))


def head_loss(params, rows, target, mask_f):
    start = D + FLAYERS * FREQ
    hidden = jax.nn.gelu(
        jnp.einsum("...f,fg->...g", rows, params[3][start : start + FREQ], precision=HIGH)
        + pick(params[4], "head_bias", 0)
    )
    pred = jnp.einsum("...f,f->...", hidden, pick(params[4], "head_out", 0), precision=HIGH)
    diff = pred - target
    return jnp.sum(mask_f * diff * diff)


def add_all(first, second):
    return jax.tree.map(jnp.add, first, second)


def spectral_setup(points, parts):
    width = FREQ // parts
    return (mode_table(points, points), lax.axis_index("pts") * width, width, points)


def fourier_mix(spec, field, setup):
    grid, column, width, points = setup
    channel_rows = lax.all_to_all(field, "pts", split_axis=2, concat_axis=1, tiled=True)
    own_coef = jnp.einsum("kp,spc->skc", grid, channel_rows, precision=HIGH) / math.sqrt(points)
    full = lax.all_gather(own_coef, "pts", axis=2, tiled=True)
    mixed = spectral_mix(full, spec, column, width)
    spread = jnp.einsum("kp,skc->spc", grid, mixed, precision=HIGH) / math.sqrt(MODES)
    back = lax.all_to_all(spread, "pts", split_axis=1, concat_axis=2, tiled=True)
    return (back, full)


def fourier_back(params, grad_out, kept_item, layer, setup):
    field, full, back = kept_item
    grid, column, width, points = setup
    _, end_pull = jax.vjp(
        lambda weights, spread, inner: fourier_end(weights, spread, inner, layer),
        params,
        back,
        field,
    )
    grads, grad_back, grad_field = end_pull(grad_out)
    _, mix_pull = jax.vjp(
        lambda coef, weight: spectral_mix(coef, weight, column, width), full, params[2][layer]
    )
    grad_rows = lax.all_to_all(grad_back, "pts", split_axis=2, concat_axis=1, tiled=True)
    grad_mixed = jnp.einsum("kp,spc->skc", grid, grad_rows, precision=HIGH) / math.sqrt(MODES)
    grad_full, grad_spec = mix_pull(grad_mixed)
    grad_coef = lax.psum_scatter(grad_full, "pts", scatter_dimension=2, tiled=True)
    grad_chan = jnp.einsum("kp,skc->spc", grid, grad_coef, precision=HIGH) / math.sqrt(points)
    grad_field = grad_field + lax.all_to_all(
        grad_chan, "pts", split_axis=1, concat_axis=2, tiled=True
    )
    grads = (grads[0], grads[1], grads[2].at[layer].add(grad_spec), grads[3], grads[4])
    return (grads, grad_field)


def attention_back(params, grad_rows, kept_item, layer, points):
    rows, summary = kept_item
    (query, partial_sum), front_pull = jax.vjp(
        lambda weights, inner: attn_front(weights, inner, layer, points), params, rows
    )
    summary = lax.psum(partial_sum, "pts")
    middle, rear_pull = jax.vjp(
        lambda weights, inner, asked, summed: attn_rear(weights, inner, asked, summed, layer),
        params,
        rows,
        query,
        summary,
    )
    _, ffn_pull = jax.vjp(lambda weights, inner: ffn_block(weights, inner, layer), params, middle)
    ffn_grads, grad_middle = ffn_pull(grad_rows)
    rear_grads, grad_direct, grad_query, grad_summary = rear_pull(grad_middle)
    grad_summary = lax.psum(grad_summary, "pts")
    front_grads, grad_front = front_pull((grad_query, grad_summary))
    return (add_all(add_all(ffn_grads, rear_grads), front_grads), grad_direct + grad_front)


def lamb(weight, grad, first, second):
    first_new = BETA_ONE * first + (1.0 - BETA_ONE) * grad
    second_new = BETA_TWO * second + (1.0 - BETA_TWO) * grad * grad
    update = (
        first_new
        / (1.0 - BETA_ONE**STEP)
        / (jnp.sqrt(second_new / (1.0 - BETA_TWO**STEP)) + ADAM_EPS)
        + DECAY * weight
    )
    return (first_new, second_new, update)


def trust_step(weight, update, stacked):
    axes = tuple(range(1, weight.ndim)) if stacked else tuple(range(weight.ndim))
    weight_norm = jnp.sqrt(jnp.sum(weight * weight, axes))
    update_norm = jnp.sqrt(jnp.sum(update * update, axes))
    ratio = weight_norm / (update_norm + ADAM_EPS)
    scale = ratio.reshape(ratio.shape + (1,) * (weight.ndim - ratio.ndim))
    return (
        weight - RATE * scale * update,
        jnp.atleast_1d(weight_norm),
        jnp.atleast_1d(update_norm),
        jnp.atleast_1d(ratio),
    )


def finish(loss_sum, valid_count, params, grads, firsts, seconds):
    results = [loss_sum, valid_count]
    weight_norms, update_norms, ratios = ([], [], [])
    for weight, grad, first, second, stacked in zip(
        params, grads, firsts, seconds, (True, True, True, False, False)
    ):
        first_new, second_new, update = lamb(weight, grad, first, second)
        fresh, weight_norm, update_norm, ratio = trust_step(weight, update, stacked)
        results = results + [first_new, second_new, fresh, fresh.astype(jnp.bfloat16)]
        weight_norms.append(weight_norm)
        update_norms.append(update_norm)
        ratios.append(ratio)
    return results + [
        jnp.concatenate(weight_norms),
        jnp.concatenate(update_norms),
        jnp.concatenate(ratios),
    ]


def body(
    samples_in,
    target,
    mask,
    attn_w,
    ffn_w,
    spec_w,
    dense_w,
    vectors,
    attn_m,
    ffn_m,
    spec_m,
    dense_m,
    vector_m,
    attn_v,
    ffn_v,
    spec_v,
    dense_v,
    vector_v,
):
    params = (attn_w, ffn_w, spec_w, dense_w, vectors)
    parts = lax.axis_size("pts")
    local_pts = samples_in.shape[2]
    points = local_pts * parts
    mask_f = mask.astype(jnp.float32)
    valid_count = lax.psum(jnp.sum(mask_f), ("dp", "pts"))
    setup = spectral_setup(points, parts)
    rows, lift_pull = jax.vjp(lambda weights: lift(weights, samples_in), params)
    kept = []
    for layer in range(LAYERS):
        query, partial_sum = attn_front(params, rows, layer, points)
        summary = lax.psum(partial_sum, "pts")
        kept.append((rows, summary))
        rows = ffn_block(params, attn_rear(params, rows, query, summary, layer), layer)
    field, proj_pull = jax.vjp(project, params, rows)
    spectral_kept = []
    for layer in range(FLAYERS):
        back, full = fourier_mix(params[2][layer], field, setup)
        spectral_kept.append((field, full, back))
        field = fourier_end(params, back, field, layer)
    loss_part, head_pull = jax.vjp(
        lambda weights, inner: head_loss(weights, inner, target, mask_f), params, field
    )
    grads, grad_field = head_pull(1.0 / valid_count)
    for layer in reversed(range(FLAYERS)):
        layer_grads, grad_field = fourier_back(
            params, grad_field, spectral_kept[layer], layer, setup
        )
        grads = add_all(grads, layer_grads)
    proj_grads, grad_rows = proj_pull(grad_field)
    grads = add_all(grads, proj_grads)
    for layer in reversed(range(LAYERS)):
        layer_grads, grad_rows = attention_back(params, grad_rows, kept[layer], layer, points)
        grads = add_all(grads, layer_grads)
    grads = add_all(grads, lift_pull(grad_rows)[0])
    summed = lax.psum((grads[0], grads[1], grads[2], grads[3], grads[4], loss_part), ("dp", "pts"))
    out = finish(
        summed[5],
        valid_count,
        params,
        summed[:5],
        (attn_m, ffn_m, spec_m, dense_m, vector_m),
        (attn_v, ffn_v, spec_v, dense_v, vector_v),
    )
    return (
        out[0],
        out[1],
        out[2],
        out[3],
        out[4],
        out[5],
        out[6],
        out[7],
        out[8],
        out[9],
        out[10],
        out[11],
        out[12],
        out[13],
        out[14],
        out[15],
        out[16],
        out[17],
        out[18],
        out[19],
        out[20],
        out[21],
        out[22],
        out[23],
        out[24],
    )


F32 = jnp.float32
BF16 = jnp.bfloat16
ROWS = 1024
NVEC_ROWS = 16


def dot(first, second, left=1, right=0, precision=None):
    return lax.dot_general(
        first,
        second,
        (((left,), (right,)), ((), ())),
        precision=precision,
        preferred_element_type=F32,
    )


def exact(first, second, left=1, right=0):
    return dot(first, second, left, right, HIGH)


def halves(value):
    high = value.astype(BF16)
    return high, (value - high.astype(F32)).astype(BF16)


def thirds(value):
    high = value.astype(BF16)
    rest = value - high.astype(F32)
    middle = rest.astype(BF16)
    return high, middle, (rest - middle.astype(F32)).astype(BF16)


def beside(*pieces):
    return jnp.concatenate(pieces, 1)


def above(*pieces):
    return jnp.concatenate(pieces, 0)


def fold(value):
    half = value.shape[1] // 2
    return value[:, :half] + value[:, half:]


def column_sum(value):
    rows, width = value.shape
    return jnp.sum(value.reshape(rows // 8, 8, width), 0)


def gelu_pair(inner):
    scale = math.sqrt(2.0 / math.pi)
    square = inner * inner
    bend = jnp.tanh(inner * (scale + (scale * 0.044715) * square))
    half = 0.5 + 0.5 * bend
    slope = half + (0.5 * inner) * (1.0 - bend * bend) * (scale + (3.0 * scale * 0.044715) * square)
    return inner * half, slope


def wide6_weight(weight):
    high, middle, low = thirds(weight)
    return above(high, high, middle, middle, low, high)


def wide6(pieces, weight):
    high, middle, low = pieces
    return dot(beside(high, middle, high, middle, high, low), weight)


def tall6_weight(weight):
    high, middle, low = thirds(weight)
    pair = beside(high, middle)
    return above(pair, pair), above(low, high)


def tall6(pieces, weights):
    high, middle, low = pieces
    return fold(dot(beside(high, middle), weights[0])) + dot(beside(high, low), weights[1])


def head_blocks(width):
    row = lax.broadcasted_iota(jnp.int32, (width, width), 0)
    column = lax.broadcasted_iota(jnp.int32, (width, width), 1)
    return row // (D // HEADS) == column // (D // HEADS)


def doubled(weight):
    zero = jnp.zeros_like(weight)
    return above(beside(weight, zero), beside(zero, weight))


MESH = pl.DeviceIdType.MESH


def position():
    dp, pts = lax.axis_index("dp"), lax.axis_index("pts")
    x, core, z, y = dp // 2, dp % 2, pts // 2, pts % 2
    return x, core, z, y


def device_of(x, core, z, y):
    return (2 * x + core, 2 * z + y)


def device_at(number):
    core, a, b, z = number // 16, number // 8 % 2, number // 4 % 2, number % 4
    x = (1 - core) * a + core * b
    y = (1 - core) * b + core * a
    return device_of(x, core, z, y)


class Route:
    def __init__(self, rows, full, flat, landing, sends, receives, first):
        x, core, z, y = position()
        self.core, self.group = core, FLAYERS * MODES // 2
        self.place = 8 * ((1 - core) * x + core * y) + 4 * ((1 - core) * y + core * x) + z
        self.rows, self.full, self.flat, self.landing = rows, full, flat, landing
        self.sends, self.receives, self.first = sends, receives, first
        self.peer = device_of(x, 1 - core, z, y)
        self.half, self.least = rows // 2, rows // (2 * self.group)
        self.own = core * self.half + self.place * self.least

    def area(self, start, size):
        return pl.ds(pl.multiple_of(start, self.least), size)

    def link(self, source, target, slot, device):
        return pltpu.make_async_remote_copy(
            src_ref=source,
            dst_ref=target,
            send_sem=self.sends.at[self.first + slot],
            recv_sem=self.receives.at[self.first + slot],
            device_id=device,
            device_id_type=MESH,
        )

    def each(self, stage, start):
        half, least, core, group = self.half, self.least, self.core, self.group
        if stage in (0, 3):
            if stage:
                source = self.full.at[self.area(core * half, half)]
                target = source if start else self.full.at[self.area((1 - core) * half, half)]
            else:
                source, target = self.flat.at[self.area((1 - core) * half, half)], self.landing.at[pl.ds(0, half)]
            copy = self.link(source, target, 2 * group - 2 if stage else 2 * group - 1, self.peer)
            if start:
                copy.start()
            else:
                copy.wait()
            return

        def one(i, _):
            other = lax.rem(self.place + 1 + i, group)
            sender = lax.rem(self.place + group - 1 - i, group)
            if stage == 1:
                source = self.flat.at[self.area(core * half + other * least, least)]
                target = self.landing.at[self.area(half + i * least, least)]
            else:
                source = self.full.at[self.area(self.own, least)]
                target = source if start else self.full.at[self.area(core * half + sender * least, least)]
            copy = self.link(source, target, (stage - 1) * (group - 1) + i, device_at(core * group + other))
            if start:
                copy.start()
            else:
                copy.wait()
            return 0

        lax.fori_loop(0, group - 1, one, 0)

    def start(self, stage):
        if stage == 2 and self.flat is not None:
            self.full[self.area(self.own, self.least), :] = self.flat[self.area(self.own, self.least), :]
        self.each(stage, True)

    def finish(self, stage):
        self.each(stage, False)
        if stage == 0:
            self.flat[self.area(self.core * self.half, self.half), :] += self.landing[: self.half, :]
        if stage == 1:
            mine = self.area(self.own, self.least)
            total = self.flat[mine, :]
            for i in range(self.group - 1):
                start = self.half + i * self.least
                total = total + self.landing[start : start + self.least, :]
            self.flat[mine, :] = total

    def step(self, stage):
        self.finish(stage)
        self.start(stage + 1)


def spread_to_all(devices, mine, source_of, target, sends, receives, start):
    def one(i, _):
        other = lax.rem(mine + 1 + i, devices)
        sender = lax.rem(mine + devices - 1 - i, devices)
        copy = pltpu.make_async_remote_copy(
            src_ref=source_of(other),
            dst_ref=target.at[mine if start else sender],
            send_sem=sends.at[i],
            recv_sem=receives.at[i],
            device_id=device_at(other),
            device_id_type=MESH,
        )
        if start:
            copy.start()
        else:
            copy.wait()
        return 0

    lax.fori_loop(0, devices - 1, one, 0)


def step_kernel(
    samples_ref,
    target_ref,
    mask_ref,
    attn_ref,
    ffn_ref,
    spec_ref,
    turned_ref,
    vectors_ref,
    table_ref,
    trow_ref,
    early_out,
    late_out,
    mode_out,
    tail_out,
    outgoing,
    incoming,
    vec_ref,
    early,
    early_land,
    late,
    late_land,
    mode_send,
    mode_land,
    tail_send,
    tail_land,
    route_send,
    route_recv,
    point_send,
    point_recv,
    mode_sends,
    mode_recvs,
    tail_sends,
    tail_recvs,
    lifted,
    lrows,
    w_kv,
    w_kvt,
    w_in,
    w_int,
    w0_u,
    mid_rows,
    w_out0,
    w_out1,
    w_outt,
    x_keep,
    r_keep,
    slope_keep,
    act_keep,
    mid_keep,
    h1_keep,
    h2_keep,
    z_keep,
    e_keep,
    s_acc,
    w0_kv,
    w0_g,
    n_keep,
    small_keep,
    nt_keep,
    cent_keep,
    coef_acc,
    coef_keep,
    stack_ref,
    sq_acc,
    p_acc,
    w2_acc,
    w1_acc,
    kv_acc,
    v_acc,
    u_acc,
    vt_acc,
    b_acc,
    d_keep,
    t_keep,
    wz,
):
    parts = samples_ref.shape[0] // 2
    count = 2
    points = samples_ref.shape[2] * parts
    devices = FLAYERS * MODES
    x, core, z, y = position()
    pts = 2 * z + y
    mine = 16 * core + 8 * ((1 - core) * x + core * y) + 4 * ((1 - core) * y + core * x) + z
    early_route = Route(early.shape[0], early_out, early, early_land, route_send, route_recv, 0)
    late_route = Route(late.shape[0], late_out, late, late_land, route_send, route_recv, devices)
    mode_route = Route(mode_out.shape[0], mode_out, None, None, route_send, route_recv, 2 * devices)

    barrier = pltpu.get_barrier_semaphore()

    def greet(i, _):
        pl.semaphore_signal(
            barrier, inc=1, device_id=device_at(lax.rem(mine + 1 + i, devices)), device_id_type=MESH
        )
        return 0

    lax.fori_loop(0, devices - 1, greet, 0)
    for p in range(parts):
        outgoing[p, 0:2, :] = samples_ref[2 * p]
        outgoing[p, 2:4, :] = samples_ref[2 * p + 1]
        outgoing[p, 4:6, :] = target_ref[2 * p : 2 * p + 2, :]
        outgoing[p, 6:8, :] = mask_ref[2 * p : 2 * p + 2, :].astype(F32)
    incoming[pts] = outgoing[pts]
    pl.semaphore_wait(barrier, devices - 1)

    def point_copy(k, start):
        other = lax.rem(pts + k, parts)
        sender = lax.rem(pts + parts - k, parts)
        return pltpu.make_async_remote_copy(
            src_ref=outgoing.at[other],
            dst_ref=incoming.at[pts if start else sender],
            send_sem=point_send.at[k - 1],
            recv_sem=point_recv.at[k - 1],
            device_id=(2 * x + core, other),
            device_id_type=MESH,
        )

    for k in range(1, parts):
        point_copy(k, True).start()
    for i in range(NVEC_ROWS - 1):
        vec_ref[i : i + 1, :] = vectors_ref[i * D : (i + 1) * D].reshape(1, D)
    last = vectors_ref.shape[0] - (NVEC_ROWS - 1) * D
    vec_ref[NVEC_ROWS - 1 :, :last] = vectors_ref[(NVEC_ROWS - 1) * D :].reshape(1, last)
    total = count * points
    steps = points // ROWS
    rows_all = total // ROWS
    blocks = head_blocks(D)
    block_f = jnp.where(blocks, 1.0, 0.0).astype(F32)
    block_b = block_f.astype(BF16)
    mean_weight = above(block_b, block_b)
    centre = (
        jnp.where(
            lax.broadcasted_iota(jnp.int32, (D, D), 0) == lax.broadcasted_iota(jnp.int32, (D, D), 1),
            1.0,
            0.0,
        ).astype(F32)
        - block_f * (HEADS / D)
    )
    eye = jnp.where(
        lax.broadcasted_iota(jnp.int32, (D, D), 0) == lax.broadcasted_iota(jnp.int32, (D, D), 1), 1.0, 0.0
    ).astype(F32)

    def vector(label, layer):
        start, length = vector_table()[label, layer]
        if length == 2 * D:
            row = start // D
            return beside(vec_ref[row : row + 1, :], vec_ref[row + 1 : row + 2, :])
        row = start // D
        if length == D:
            return vec_ref[row : row + 1, :]
        offset = start - row * D
        piece = vec_ref[row : row + 1, offset : offset + FREQ]
        return beside(piece, piece)

    def block(index):
        return pl.ds(pl.multiple_of(index * ROWS, ROWS), ROWS)

    lift_rows = above(
        vector("lift_value", 0), vector("lift_coord", 0), vector("lift_bias", 0), jnp.zeros((5, D), F32)
    )

    def lift_weight(mixed):
        high, middle, low = [item.astype(F32) for item in thirds(mixed)]
        parts = []
        for i in range(2):
            hi, mi, lo = high[i : i + 1], middle[i : i + 1], low[i : i + 1]
            parts += [hi, hi, mi, mi, lo, hi]
        parts += [high[2:3], middle[2:3], low[2:3]]
        parts.append(jnp.zeros((D - 15, mixed.shape[1]), F32))
        return above(*parts).astype(BF16)

    for layer in range(LAYERS):
        weight = attn_ref[layer]
        keyed = beside(exact(weight[:, D : 2 * D], centre), exact(weight[:, 2 * D : 3 * D], centre))
        cent_keep[layer] = keyed
        if layer == 0:
            w0_kv[...] = lift_weight(exact(lift_rows, keyed))
        else:
            w_kv[...] = wide6_weight(keyed)
            pair, rest = tall6_weight(keyed.T)
            w_kvt[:, : 2 * D] = pair
            w_kvt[:, 2 * D :] = rest
        first, second = ffn_ref[layer, 0], ffn_ref[layer, 1]
        if layer:
            w_in[...] = wide6_weight(first)
            pair, rest = tall6_weight(first.T)
            w_int[:, : 2 * D] = pair
            w_int[:, 2 * D :] = rest
        pair, rest = tall6_weight(second.T)
        w_out0[layer] = pair
        w_out1[layer] = rest
        w_outt[layer] = wide6_weight(second)

    s_acc[...] = jnp.zeros_like(s_acc)
    coef_acc[...] = jnp.zeros_like(coef_acc)
    sq_acc[...] = jnp.zeros_like(sq_acc)
    p_acc[...] = jnp.zeros_like(p_acc)
    w2_acc[...] = jnp.zeros_like(w2_acc)
    w1_acc[...] = jnp.zeros_like(w1_acc)
    kv_acc[...] = jnp.zeros_like(kv_acc)
    v_acc[...] = jnp.zeros_like(v_acc)
    u_acc[...] = jnp.zeros_like(u_acc)
    vt_acc[...] = jnp.zeros_like(vt_acc)
    b_acc[...] = jnp.zeros_like(b_acc)

    for k in range(1, parts):
        point_copy(k, False).wait()
    whole = beside(*[incoming[p] for p in range(parts)])
    for s in range(count):
        value, coord = whole[2 * s : 2 * s + 1], whole[2 * s + 1 : 2 * s + 2]
        target, valid = whole[4 + s : 5 + s], whole[6 + s : 7 + s]
        one = jnp.ones_like(value)
        vh, vm, vl = [item.astype(F32) for item in thirds(value)]
        ch, cm, cl = [item.astype(F32) for item in thirds(coord)]
        th, tm, tl = [item.astype(F32) for item in thirds(target)]
        zero = jnp.zeros((D - 19, points), F32)
        stack = above(vh, vm, vh, vm, vh, vl, ch, cm, ch, cm, ch, cl, one, one, one, th, tm, tl, valid, zero)
        lifted[s * points : (s + 1) * points, :] = stack.T.astype(BF16)
        short = above(vh, vm, vl, ch, cm, cl, one, jnp.zeros((9, points), F32)).astype(BF16)
        for i in range(steps):
            lrows[s * steps + i] = short[:, i * ROWS : (i + 1) * ROWS]

    def head_scale(centred):
        high, low = halves(centred * centred)
        var = beside(
            dot(beside(high[:, :D], low[:, :D]), mean_weight), dot(beside(high[:, D:], low[:, D:]), mean_weight)
        )
        return lax.rsqrt(var * (HEADS / D) + NORM_EPS)

    def normalise(layer, index, centred):
        scale = head_scale(centred)
        normal = centred * scale
        if layer:
            where = block(index)
            x_keep[where, :] = normal
            r_keep[where, :] = scale
        high, low = halves(normal)
        s_acc[index // steps] += dot(
            beside(high[:, :D], low[:, :D]), beside(high[:, D:], low[:, D:]), 0, 0
        )

    def quarters(value):
        half_row, half_col = value.shape[0] // 2, value.shape[1] // 2
        return (
            value[:half_row, :half_col]
            + value[half_row:, :half_col]
            + (value[:half_row, half_col:] + value[half_row:, half_col:])
        )

    def summarise(layer):
        weight = attn_ref[layer]
        key_gain = vector("key_gain", layer).reshape(1, D)
        value_gain = vector("value_gain", layer).reshape(1, D)
        key_column = jnp.sum(eye * key_gain, 1, keepdims=True)
        for s in range(count):
            plain = jnp.where(blocks, quarters(s_acc[s]), 0.0) * (1.0 / points)
            summary = key_column * plain * value_gain
            mixed = exact(summary, weight[:, 3 * D :])
            both = exact(weight[:, :D], mixed)
            n_keep[layer, s] = both
            small_keep[layer, s, 0] = plain
            small_keep[layer, s, 1] = summary
            small_keep[layer, s, 2] = mixed
            if layer == 0:
                rows = exact(lift_rows, eye + both)
                mid_rows[s] = rows
                w0_g[s] = lift_weight(rows)
                w0_u[s] = lift_weight(exact(rows, ffn_ref[0, 0]))
            else:
                pair, rest = tall6_weight(both)
                wz[s, : 2 * D, :] = pair
                wz[s, 2 * D :, :D] = rest
                pair, rest = tall6_weight(both.T)
                nt_keep[s, :, : 2 * D] = pair
                nt_keep[s, :, 2 * D :] = rest

    def feed(layer, index, mid, inner):
        where = block(index)
        act, slope = gelu_pair(inner + vector("inner_bias", layer))
        slope_keep[layer, where, :] = slope
        pieces = thirds(act)
        act_keep[layer, where, :] = beside(pieces[0], pieces[1])
        return mid + tall6(pieces, (w_out0[layer], w_out1[layer])) + vector("outer_bias", layer)

    def front_zero(index, _):
        normalise(0, index, dot(lifted[block(index), :], w0_kv[...]))
        return 0

    lax.fori_loop(0, rows_all, front_zero, 0)
    summarise(0)
    s_acc[...] = jnp.zeros_like(s_acc)

    def layer_zero(index, _):
        where = block(index)
        s = index // steps
        data = lifted[where, :]
        out = feed(0, index, dot(data, w0_g[s]), dot(data, w0_u[s]))
        d_keep[where, :] = out
        pieces = thirds(out)
        h1_keep[where, :] = beside(pieces[0], pieces[1])
        h2_keep[where, 2 * D :] = pieces[2]
        normalise(1, index, wide6(pieces, w_kv[...]))
        return 0

    lax.fori_loop(0, rows_all, layer_zero, 0)
    summarise(1)
    s_acc[...] = jnp.zeros_like(s_acc)

    def pieces_of(ref, where, number=3):
        value = ref[where, : number * D]
        return [value[:, i * D : (i + 1) * D] for i in range(number)]

    def layer_one(index, _):
        where = block(index)
        s = index // steps
        pieces = pieces_of(h1_keep, where, 2) + [h2_keep[where, 2 * D :]]
        mid = d_keep[where, :] + tall6(pieces, (wz[s, : 2 * D, :], wz[s, 2 * D :, :D]))
        pieces = thirds(mid)
        mid_keep[where, :] = beside(pieces[0], pieces[1])
        out = feed(1, index, mid, wide6(pieces, w_in[...]))
        h2_keep[where, :] = beside(*thirds(out))
        return 0

    lax.fori_loop(0, rows_all, layer_one, 0)

    def dense_rows(part):
        start = D + (part - 1) * FREQ if part else 0
        return turned_ref[:, start : start + (FREQ if part else D)].T

    proj0, proj1 = tall6_weight(doubled(dense_rows(0)))
    locals6 = [tall6_weight(doubled(dense_rows(part))) for part in (1, 2, 3)]
    turned6 = [tall6_weight(doubled(dense_rows(part).T)) for part in (1, 2, 3)]
    own = lax.broadcasted_iota(jnp.int32, (2 * count * MODES, MODES * D), 1) // D == lax.rem(
        lax.broadcasted_iota(jnp.int32, (2 * count * MODES, MODES * D), 0), MODES
    )

    def mode_rows(coef):
        cosine, sine = coef[:MODES], coef[MODES:]
        c = [cosine[:, s * FREQ : (s + 1) * FREQ] for s in range(count)]
        d = [sine[:, s * FREQ : (s + 1) * FREQ] for s in range(count)]
        return above(
            *[beside(c[s], d[s]) for s in range(count)], *[beside(d[s], -c[s]) for s in range(count)]
        )

    def spread_rows(rows):
        return jnp.where(own, beside(*([rows] * MODES)), 0.0)

    def unpack(rows):
        lead = count * MODES
        return above(
            *[beside(*[rows[j * lead + s * MODES : j * lead + (s + 1) * MODES] for s in range(count)]) for j in (0, 1)]
        )

    def pack(value):
        return above(
            *[
                value[j * MODES : (j + 1) * MODES, s * FREQ : (s + 1) * FREQ]
                for j in (0, 1)
                for s in range(count)
            ]
        )

    def set_stack(value):
        high, middle, low = thirds(value)
        stack_ref[...] = above(
            high, high, middle, middle, low, high, jnp.zeros((4 * MODES, D), BF16)
        )

    def take_coef(index, high, low):
        coef_acc[...] += dot(trow_ref[index], beside(high, low))

    def mix_forward(layer):
        coef = quarters(coef_acc[...]) * (1.0 / math.sqrt(points))
        coef_acc[...] = jnp.zeros_like(coef_acc)
        rows = mode_rows(coef)
        coef_keep[layer] = rows
        set_stack(unpack(exact(spread_rows(rows), spec_ref[layer])) * (1.0 / math.sqrt(MODES)))

    def mix_back(layer):
        cot = pack(quarters(coef_acc[...])) * (1.0 / math.sqrt(MODES))
        coef_acc[...] = jnp.zeros_like(coef_acc)
        kept_rows = coef_keep[layer]
        padded = beside(cot, jnp.zeros_like(cot))
        for k in range(MODES):
            for r in range(2 * count):
                mode_send[layer * MODES + k, r : r + 1, :] = kept_rows[r * MODES + k : r * MODES + k + 1]
                mode_send[layer * MODES + k, 4 + r : 5 + r, :] = padded[r * MODES + k : r * MODES + k + 1]
        wide = jnp.where(own, exact(cot, spec_ref[layer], 1, 1), 0.0)
        kept = wide[:, :D]
        for k in range(1, MODES):
            kept = kept + wide[:, k * D : (k + 1) * D]
        lead = count * MODES
        first, second = kept[:lead], kept[lead:]
        rows = above(first[:, :FREQ] - second[:, FREQ:], first[:, FREQ:] + second[:, :FREQ])
        set_stack(unpack(rows) * (1.0 / math.sqrt(points)))

    def project_step(index, _):
        where = block(index)
        first = h2_keep[block(index), :]
        second = h2_keep[block(index + steps), :]
        pieces = [beside(first[:, i * D : (i + 1) * D], second[:, i * D : (i + 1) * D]) for i in range(3)]
        field = tall6(pieces, (proj0, proj1)) + vector("proj_bias", 0)
        pieces = thirds(field)
        z_keep[0, where, :] = beside(*pieces)
        take_coef(index, pieces[0], pieces[1])
        return 0

    lax.fori_loop(0, steps, project_step, 0)
    mix_forward(0)

    def fourier_field(layer, where):
        pieces = pieces_of(z_keep.at[layer], where)
        inner = dot(table_ref[where, :], stack_ref[...]) + (
            tall6(pieces, locals6[layer]) + vector("fourier_bias", layer)
        )
        return gelu_pair(inner)

    def fourier_one(index, _):
        where = block(index)
        field, slope = fourier_field(0, where)
        d_keep[where, :] = slope
        pieces = thirds(field)
        z_keep[1, where, :] = beside(*pieces)
        take_coef(index, pieces[0], pieces[1])
        return 0

    lax.fori_loop(0, steps, fourier_one, 0)
    mix_forward(1)

    lane = lax.broadcasted_iota(jnp.int32, (2 * D, 2 * D), 1)
    row = lax.broadcasted_iota(jnp.int32, (2 * D, 2 * D), 0)
    inner_row = lax.rem(row, D)
    same = row // D == lax.rem(lane, D) // FREQ
    pick_target = (lane < D) & (inner_row >= 15) & (inner_row < 18)
    pick_mask = (lane >= D) & (inner_row == 18)
    spread = jnp.where(same & (pick_target | pick_mask), 1.0, 0.0).astype(BF16)
    out_row = vector("head_out", 0)
    out_column = jnp.sum(eye * out_row, 1, keepdims=True)
    half_blocks = (
        lax.broadcasted_iota(jnp.int32, (D, D), 0) // FREQ == lax.broadcasted_iota(jnp.int32, (D, D), 1) // FREQ
    )
    out_weight = tall6_weight(jnp.where(half_blocks, out_column, 0.0))

    def pair_product(first, second):
        return dot(beside(*first), beside(*second), 0, 0)

    def loss_step(index, _):
        where = block(index)
        field, slope = fourier_field(1, where)
        pieces = thirds(field)
        hidden, hidden_slope = gelu_pair(tall6(pieces, locals6[2]) + vector("head_bias", 0))
        pred = tall6(thirds(hidden), out_weight)
        known = dot(beside(lifted[where, :], lifted[block(index + steps), :]), spread)
        diff = pred - known[:, :D]
        valid = known[:, D:]
        cot = (2.0 * valid) * diff
        b_acc[0:8, :D] += column_sum(valid * diff * diff)
        b_acc[8:16, :D] += column_sum(valid)
        b_acc[16:24, :D] += column_sum(hidden * cot)
        cot = cot * out_row * hidden_slope
        b_acc[24:32, :D] += column_sum(cot)
        split = thirds(cot)
        sq_acc[2] += pair_product(pieces[:2], split[:2])
        cot = tall6(split, turned6[2]) * slope
        b_acc[32:40, :D] += column_sum(cot)
        split = thirds(cot)
        e_keep[where, :] = beside(*split)
        sq_acc[1] += pair_product(pieces_of(z_keep.at[1], where, 2), split[:2])
        take_coef(index, *split[:2])
        return 0

    lax.fori_loop(0, steps, loss_step, 0)
    mix_back(1)

    def fourier_cot(layer, where):
        return tall6(pieces_of(e_keep, where), turned6[layer]) + dot(table_ref[where, :], stack_ref[...])

    def fourier_back(index, _):
        where = block(index)
        cot = fourier_cot(1, where) * d_keep[where, :]
        b_acc[40:48, :D] += column_sum(cot)
        split = thirds(cot)
        e_keep[where, :] = beside(*split)
        sq_acc[0] += pair_product(pieces_of(z_keep.at[0], where, 2), split[:2])
        take_coef(index, *split[:2])
        return 0

    lax.fori_loop(0, steps, fourier_back, 0)
    mix_back(0)
    mode_land[mine] = mode_send[mine]
    spread_to_all(devices, mine, lambda r: mode_send.at[r], mode_land, mode_sends, mode_recvs, True)
    proj_back = wide6_weight(doubled(turned_ref[:, :D]))

    def project_back(index, _):
        where = block(index)
        later = block(index + steps)
        cot = fourier_cot(0, where)
        b_acc[48:56, :D] += column_sum(cot)
        split = thirds(cot)
        first = pieces_of(h2_keep, where, 2)
        second = pieces_of(h2_keep, later, 2)
        p_acc[...] += dot(beside(first[0], second[0], first[1], second[1]), beside(*split[:2]), 0, 0)
        rows = wide6(split, proj_back)
        d_keep[where, :] = rows[:, :D]
        d_keep[later, :] = rows[:, D:]
        return 0

    lax.fori_loop(0, steps, project_back, 0)
    spread_to_all(devices, mine, lambda r: mode_send.at[r], mode_land, mode_sends, mode_recvs, False)
    landed = mode_land[...].reshape(devices * 8, D)
    shifted = above(landed[4:], landed[:4])
    row = lax.broadcasted_iota(jnp.int32, landed.shape, 0)
    product = exact(jnp.where(lax.rem(row, 8) < 4, landed, 0.0), shifted[:, :FREQ], 0, 0)
    mode_out[mode_route.area(mode_route.own, FREQ), :] = beside(product[:FREQ], product[FREQ:])
    mode_route.start(2)

    def feed_back(layer, index, cot):
        where = block(index)
        base = 56 + layer * 16
        b_acc[base : base + 8, :D] += column_sum(cot)
        split = thirds(cot)
        act = act_keep[layer, where, :]
        w2_acc[layer] += dot(beside(*split[:2]), act[:, :FF], 0, 0)
        w2_acc[layer, :D, :] += dot(split[0], act[:, FF:], 0, 0)
        inner = wide6(split, w_outt[layer]) * slope_keep[layer, where, :]
        b_acc[base + 8 : base + 16, :] += column_sum(inner)
        return split, thirds(inner)

    def layer_one_back(index, _):
        where = block(index)
        cot = d_keep[where, :]
        _, pieces = feed_back(1, index, cot)
        high, low = pieces[:2]
        mid = mid_keep[where, :]
        w1_acc[...] += dot(mid, high, 0, 0)
        w1_acc[:D, :] += dot(mid[:, :D], low, 0, 0)
        cot = cot + tall6(pieces, (w_int[:, : 2 * D], w_int[:, 2 * D :]))
        d_keep[where, :] = cot
        s_acc[index // steps] += pair_product(pieces_of(h1_keep, where, 2), halves(cot))
        return 0

    lax.fori_loop(0, rows_all, layer_one_back, 0)

    def attend_back(layer, products):
        weight = attn_ref[layer]
        query, outer = weight[:, :D], weight[:, 3 * D :]
        key_gain, value_gain = vector("key_gain", layer), vector("value_gain", layer)
        key_column = jnp.sum(eye * key_gain, 1, keepdims=True)
        key_total = jnp.zeros((D, 1), F32)
        value_total = jnp.zeros((1, D), F32)
        query_grad = jnp.zeros((D, D), F32)
        outer_grad = jnp.zeros((D, D), F32)
        for s in range(count):
            plain, summary, mixed = small_keep[layer, s, 0], small_keep[layer, s, 1], small_keep[layer, s, 2]
            turned = exact(query, products[s], 0, 0)
            outer_grad += exact(summary, turned, 0, 0)
            if layer:
                query_grad += exact(products[s], mixed, 1, 1)
            cot = jnp.where(blocks, exact(turned, outer, 1, 1), 0.0)
            both = cot * plain
            key_total += jnp.sum(both * value_gain, 1, keepdims=True)
            value_total += jnp.sum(both * key_column, 0, keepdims=True)
            scaled = key_column * cot * value_gain * (1.0 / points)
            for i, item in enumerate((scaled.T, scaled)):
                pair, rest = tall6_weight(item)
                t_keep[s, i, :, : 2 * D] = pair
                t_keep[s, i, :, 2 * D :] = rest
        if layer:
            early[5 * D + FREQ : 6 * D + FREQ, :] = query_grad
            early[6 * D + FREQ : 7 * D + FREQ, :] = outer_grad
        else:
            late[6 * D : 7 * D, :] = outer_grad
        return jnp.sum(eye * key_total, 0, keepdims=True), value_total

    for i in range(2):
        half = slice(i * D, (i + 1) * D)
        early[i * D : (i + 1) * D, :] = w1_acc[:D, half] + w1_acc[D:, half]
        early[(2 + i) * D : (3 + i) * D, :] = w2_acc[1, :D, half] + w2_acc[1, D:, half]
    sums = p_acc[...]
    sums = fold(sums[: 2 * D] + sums[2 * D :])
    early[4 * D : 4 * D + FREQ, :] = (sums[:D, :FREQ] + sums[D:, FREQ:]).T
    squares = []
    for part in range(3):
        sums = quarters(sq_acc[part])
        squares.append((sums[:FREQ, :FREQ] + sums[FREQ:, FREQ:]).T)
    early[4 * D + FREQ : 5 * D, :] = beside(squares[0], squares[1])
    early[5 * D : 5 * D + FREQ, :] = beside(squares[2], jnp.zeros_like(squares[2]))
    early[7 * D + FREQ :, :] = jnp.zeros((D // 2, D), F32)
    gains = [None, None]
    gains[1] = attend_back(1, [quarters(s_acc[s]) for s in range(count)])

    def norm_back(index, normal, scale):
        s = index // steps
        key, value = normal[:, :D], normal[:, D:]
        key_cot = tall6(thirds(value), (t_keep[s, 0, :, : 2 * D], t_keep[s, 0, :, 2 * D :]))
        value_cot = tall6(thirds(key), (t_keep[s, 1, :, : 2 * D], t_keep[s, 1, :, 2 * D :]))
        mean = dot(beside(*halves(key_cot * key)), mean_weight) * (HEADS / D)
        return beside(scale[:, :D] * (key_cot - key * mean), scale[:, D:] * (value_cot - value * mean))

    early_route.start(0)

    def middle_back(index, _):
        @pl.when(index == 1)
        def _():
            mode_route.step(2)
            early_route.step(0)

        where = block(index)
        s = index // steps
        cot = norm_back(index, x_keep[where, :], r_keep[where, :])
        pieces = thirds(cot)
        high, low = pieces[:2]
        kept = h1_keep[where, :]
        kv_acc[...] += dot(kept, high, 0, 0)
        kv_acc[:D, :] += dot(kept[:, :D], low, 0, 0)
        out = d_keep[where, :]
        out = (
            out
            + tall6(thirds(out), (nt_keep[s, :, : 2 * D], nt_keep[s, :, 2 * D :]))
            + tall6(pieces, (w_kvt[:, : 2 * D], w_kvt[:, 2 * D :]))
        )
        outer, inner = feed_back(0, index, out)
        v_acc[s] += dot(lrows[index], beside(*outer[:2]))
        u_acc[s] += dot(lrows[index], beside(*inner[:2]))
        return 0

    lax.fori_loop(0, rows_all, middle_back, 0)
    mode_route.finish(3)
    early_route.step(1)

    def lift_sum(value):
        value = fold(value)
        return above(
            value[0:1] + value[1:2] + value[2:3],
            value[3:4] + value[4:5] + value[5:6],
            value[6:7],
            jnp.zeros((5, value.shape[1]), F32),
        )

    inner_rows = [lift_sum(u_acc[s]) for s in range(count)]
    value_rows = [lift_sum(v_acc[s]) + exact(inner_rows[s], ffn_ref[0, 0], 1, 1) for s in range(count)]
    gains[0] = attend_back(0, [exact(lift_rows, value_rows[s], 0, 0) for s in range(count)])

    query_rows = jnp.zeros((8, D), F32)
    lift_part = jnp.zeros((8, D), F32)
    inner_grad = jnp.zeros((D, FF), F32)
    for s in range(count):
        query_rows += exact(value_rows[s], small_keep[0, s, 2], 1, 1)
        lift_part += value_rows[s] + exact(value_rows[s], n_keep[0, s], 1, 1)
        inner_grad += exact(mid_rows[s], inner_rows[s], 0, 0)
    for i in range(2):
        half = slice(i * D, (i + 1) * D)
        late[i * D : (i + 1) * D, :] = exact(kv_acc[:D, half] + kv_acc[D:, half], centre)
        late[(2 + i) * D : (3 + i) * D, :] = w2_acc[0, :D, half] + w2_acc[0, D:, half]
        late[(4 + i) * D : (5 + i) * D, :] = inner_grad[:, half]

    def bias(slot, width=D):
        return jnp.sum(b_acc[slot * 8 : slot * 8 + 8, :width], 0, keepdims=True)

    rows = [jnp.zeros((3, D), F32)]
    for layer in range(LAYERS):
        inner = bias(8 + 2 * layer, FF)
        rows += [gains[layer][0], gains[layer][1], inner[:, :D], inner[:, D:], bias(7 + 2 * layer)]
    short = [fold(bias(slot)) for slot in (6, 5, 4, 3, 2)]
    rows += [beside(short[0], short[1]), beside(short[2], short[3]), beside(short[4], jnp.zeros((1, FREQ), F32))]
    late[7 * D : 7 * D + 16, :] = above(*rows)
    lanes = lax.broadcasted_iota(jnp.int32, (1, D), 1)
    first = jnp.where(lax.rem(lanes, FREQ) == 0, bias(0), 0.0)
    second = jnp.where(lax.rem(lanes, FREQ) == 0, bias(1), 0.0)
    late[7 * D + 16 : 7 * D + 24, :] = above(first, second, jnp.zeros((6, D), F32))
    late[7 * D + 24 : 7 * D + 32, :] = query_rows
    late[7 * D + 32 : 7 * D + 40, :] = lift_part
    late[7 * D + 40 :, :] = jnp.zeros((D - 40, D), F32)
    late_route.start(0)

    def front_back(index, _):
        @pl.when(index == 1)
        def _():
            late_route.step(0)

        centred = dot(lifted[block(index), :], w0_kv[...])
        scale = head_scale(centred)
        cot = norm_back(index, centred * scale, scale)
        vt_acc[...] += dot(lrows[index], beside(*halves(cot)))
        return 0

    lax.fori_loop(0, rows_all, front_back, 0)
    turned = lift_sum(vt_acc[...])
    tail_send[...] = above(turned[:4, :D], turned[:4, D:])
    tail_land[mine] = tail_send[...]
    spread_to_all(devices, mine, lambda r: tail_send, tail_land, tail_sends, tail_recvs, True)
    early_route.step(2)
    late_route.step(1)
    early_route.finish(3)
    late_route.step(2)
    spread_to_all(devices, mine, lambda r: tail_send, tail_land, tail_sends, tail_recvs, False)
    late_route.finish(3)
    summed = jnp.sum(tail_land[...], 0)
    zero = jnp.zeros((4, 2 * D), F32)
    turned = above(beside(summed[:4], summed[4:]), zero)
    joined = exact(lift_rows, turned, 0, 0)
    tail_out[:D, :] = exact(lift_rows, late_out[7 * D + 24 : 7 * D + 32, :], 0, 0)
    tail_out[D : 2 * D, :] = exact(joined[:, :D], centre)
    tail_out[2 * D : 3 * D, :] = exact(joined[:, D:], centre)
    tail_out[3 * D :, :] = late_out[7 * D + 32 : 7 * D + 40, :] + exact(turned, cent_keep[0], 1, 1)


def tables(points):
    order = np.arange(MODES)[:, None]
    angle = (order * np.arange(points)[None, :]) % points * (2.0 * math.pi / points)
    full = np.concatenate([np.cos(angle), np.sin(angle)], 0).astype(np.float32)
    kind = np.dtype(ml_dtypes.bfloat16)
    high = full.astype(kind)
    rest = full - high.astype(np.float32)
    middle = rest.astype(kind)
    low = (rest - middle.astype(np.float32)).astype(kind)
    zero = np.zeros((4 * MODES, points), kind)
    column = np.concatenate([high, middle, high, middle, high, low, zero], 0).T
    row = np.concatenate([high, middle], 0).reshape(4 * MODES, points // ROWS, ROWS).transpose(1, 0, 2)
    return np.ascontiguousarray(column), np.ascontiguousarray(row)


def summed_grads(samples_in, target, mask, attn_w, ffn_w, spec_w, turned_w, vectors):
    parts = samples_in.shape[0] // 2
    count, points = 2, samples_in.shape[2] * parts
    devices = FLAYERS * MODES
    total = count * points
    steps = points // ROWS
    column, row = tables(points)
    vmem = pl.BlockSpec(memory_space=pltpu.VMEM)
    first = [
        ((parts, 8, samples_in.shape[2]), F32),
        ((parts, 8, samples_in.shape[2]), F32),
        ((NVEC_ROWS, D), F32),
        ((8 * D, D), F32),
        ((8 * D, D), F32),
        ((8 * D, D), F32),
        ((8 * D, D), F32),
        ((devices, 8, D), F32),
        ((devices, 8, D), F32),
        ((8, D), F32),
        ((devices, 8, D), F32),
    ]
    numbers = (3 * devices, 3 * devices, parts - 1, parts - 1, devices - 1, devices - 1, devices - 1, devices - 1)
    scratch = [
        ((total, D), BF16),
        ((total // ROWS, 16, ROWS), BF16),
        ((6 * D, 2 * D), BF16),
        ((4 * D, 3 * D), BF16),
        ((6 * D, FF), BF16),
        ((2 * FF, 3 * D), BF16),
        ((count, D, FF), BF16),
        ((count, 8, D), F32),
        ((LAYERS, 2 * FF, 2 * D), BF16),
        ((LAYERS, 2 * FF, D), BF16),
        ((LAYERS, 6 * D, FF), BF16),
        ((total, 2 * D), F32),
        ((total, 2 * D), F32),
        ((LAYERS, total, FF), F32),
        ((LAYERS, total, 2 * FF), BF16),
        ((total, 2 * D), BF16),
        ((total, 2 * D), BF16),
        ((total, 3 * D), BF16),
        ((FLAYERS, points, 3 * D), BF16),
        ((points, 3 * D), BF16),
        ((count, 2 * D, 2 * D), F32),
        ((D, 2 * D), BF16),
        ((count, D, D), BF16),
        ((LAYERS, count, D, D), F32),
        ((LAYERS, count, 3, D, D), F32),
        ((count, 2 * D, 3 * D), BF16),
        ((LAYERS, D, 2 * D), F32),
        ((4 * MODES, 2 * D), F32),
        ((FLAYERS, 2 * count * MODES, D), F32),
        ((2 * D, D), BF16),
        ((3, 2 * D, 2 * D), F32),
        ((4 * D, 2 * D), F32),
        ((LAYERS, 2 * D, FF), F32),
        ((2 * D, FF), F32),
        ((2 * D, 2 * D), F32),
        ((count, 16, 2 * D), F32),
        ((count, 16, 2 * FF), F32),
        ((16, 4 * D), F32),
        ((96, FF), F32),
        ((total, D), F32),
        ((count, 2, 2 * D, 3 * D), BF16),
        ((count, 4 * D, 2 * D), BF16),
    ]
    shapes = [(8 * D, D), (8 * D, D), (devices * FREQ, D), (3 * D + 8, D)]
    return pl.pallas_call(
        step_kernel,
        out_shape=[jax.ShapeDtypeStruct(shape, F32) for shape in shapes],
        in_specs=[vmem] * 10,
        out_specs=[vmem] * 4,
        scratch_shapes=[pltpu.VMEM(*item) for item in first]
        + [pltpu.SemaphoreType.DMA((number,)) for number in numbers]
        + [pltpu.VMEM(*item) for item in scratch],
        compiler_params=pltpu.CompilerParams(
            vmem_limit_bytes=64 * 2**20 - 2**17, collective_id=0, has_side_effects=True
        ),
    )(
        samples_in,
        target,
        mask,
        attn_w,
        ffn_w,
        spec_w,
        turned_w,
        vectors,
        jnp.asarray(column),
        jnp.asarray(row),
    )


def update_kernel(
    early,
    late,
    modes,
    tail,
    vectors,
    vector_m,
    vector_v,
    attn_w,
    ffn_w,
    spec_w,
    turned_w,
    attn_m,
    ffn_m,
    spec_m,
    turned_m,
    attn_v,
    ffn_v,
    spec_v,
    turned_v,
    loss_out,
    count_out,
    weight_out,
    update_out,
    ratio_out,
    vector_m_out,
    vector_v_out,
    vector_w_out,
    vector_low_out,
    *rest,
):
    outs, scratch = rest[:16], rest[16:]
    ins = (attn_w, ffn_w, spec_w, turned_w, attn_m, ffn_m, spec_m, turned_m, attn_v, ffn_v, spec_v, turned_v)
    held, fresh = scratch[:12], scratch[12:28]
    flat, in_sems, out_sems = scratch[28:]

    blocks = [(2, 0), (2, 1), (1, 1), (0, 1), (0, 0), (1, 0), (3, None)]

    def view(ref, part):
        return ref if part is None else ref.at[part]

    def load(slot, kind):
        array, part = blocks[slot]
        number = kind * 4 + array
        return pltpu.make_async_copy(
            view(ins[number], part), view(held[number], part), in_sems.at[slot * 3 + kind]
        )

    def store(slot, kind):
        array, part = blocks[slot]
        number = kind * 4 + array
        return pltpu.make_async_copy(
            view(fresh[number], part), view(outs[number], part), out_sems.at[slot * 4 + kind]
        )

    for slot in range(len(blocks)):
        for kind in range(3):
            load(slot, kind).start()
    misc = late[7 * D + 16 : 7 * D + 24, :]
    loss_out[0] = jnp.sum(misc[0:1])
    valid = jnp.sum(misc[1:2], keepdims=True)
    count_out[0] = jnp.sum(misc[1:2])
    scale = 1.0 / valid

    def moved(weight, grad, first, second):
        first_new = BETA_ONE * first + (1.0 - BETA_ONE) * grad
        second_new = BETA_TWO * second + (1.0 - BETA_TWO) * grad * grad
        update = (
            first_new
            / (1.0 - BETA_ONE**STEP)
            / (jnp.sqrt(second_new / (1.0 - BETA_TWO**STEP)) + ADAM_EPS)
            + DECAY * weight
        )
        return first_new, second_new, update

    def note(slot, weight_sum, update_sum):
        weight_norm, update_norm = jnp.sqrt(weight_sum), jnp.sqrt(update_sum)
        ratio = weight_norm / (update_norm + ADAM_EPS)
        weight_out[slot] = weight_norm[0, 0]
        update_out[slot] = update_norm[0, 0]
        ratio_out[slot] = ratio[0, 0]
        return RATE * ratio

    def total(value):
        return jnp.sum(column_sum(value), keepdims=True)

    for i in range(NVEC_ROWS):
        start = i * D
        size = min(D, flat.shape[0] - start)
        row = tail[3 * D + i : 3 * D + i + 1, :] if i < 3 else late[7 * D + i : 7 * D + i + 1, :]
        flat[start : start + size] = (row * scale)[:, :size].reshape(size)
    weight = vectors[...]
    first_new, second_new, update = moved(weight, flat[...], vector_m[...], vector_v[...])
    vector_m_out[...] = first_new
    vector_v_out[...] = second_new
    rate = note(
        7,
        jnp.sum(weight * weight).reshape(1, 1),
        jnp.sum(update * update).reshape(1, 1),
    )
    flat[...] = jnp.broadcast_to(rate, (1, D)).reshape(D)[0] * update
    weight = weight - flat[...]
    vector_w_out[...] = weight
    vector_low_out[...] = weight.astype(BF16)

    def grad_blocks(array, part):
        if array == 0:
            if part:
                places = [(early, 5 * D + FREQ), (late, 0), (late, D), (early, 6 * D + FREQ)]
            else:
                places = [(tail, 0), (tail, D), (tail, 2 * D), (late, 6 * D)]
            return [
                (ref, start, D, 0, (slice(None), slice(j * D, (j + 1) * D)))
                for j, (ref, start) in enumerate(places)
            ]
        if array == 1:
            ref, starts = (early, (0, 1, 2, 3)) if part else (late, (4, 5, 2, 3))
            return [
                (ref, starts[j] * D, D, 0, (j // 2, slice(None), slice(j % 2 * D, j % 2 * D + D)))
                for j in range(4)
            ]
        if array == 3:
            return [
                (early, 4 * D, FREQ, 0, (slice(None), slice(0, D))),
                (early, 4 * D + FREQ, FREQ, 0, (slice(None), slice(D, 2 * D))),
                (early, 5 * D, FREQ, 0, (slice(None), slice(2 * D, 2 * D + FREQ))),
            ]
        return [
            (modes, (part * MODES + k) * FREQ, FREQ, j * FREQ, (k, j))
            for k in range(MODES)
            for j in range(2)
        ]

    for slot, (array, part) in enumerate(blocks):
        for kind in range(3):
            load(slot, kind).wait()
        weight_ref, first_ref, second_ref = [view(held[kind * 4 + array], part) for kind in range(3)]
        first_out, second_out, weight_new, low_out = [view(fresh[kind * 4 + array], part) for kind in range(4)]
        weight_sum = jnp.zeros((1, 1), F32)
        update_sum = jnp.zeros((1, 1), F32)
        pieces = grad_blocks(array, part)
        for ref, start, rows, lane, where in pieces:
            weight = weight_ref[where]
            width = weight.shape[1]
            grad = ref[start : start + rows, lane : lane + width] * scale
            first_new, second_new, update = moved(weight, grad, first_ref[where], second_ref[where])
            first_out[where] = first_new
            second_out[where] = second_new
            weight_new[where] = update
            weight_sum += total(weight * weight)
            update_sum += total(update * update)
        store(slot, 0).start()
        store(slot, 1).start()
        place = (0 + part if array == 0 else 2 + part if array == 1 else 4 + part) if part is not None else 6
        rate = note(place, weight_sum, update_sum)
        for ref, start, rows, lane, where in pieces:
            weight = weight_ref[where] - rate * weight_new[where]
            weight_new[where] = weight
            low_out[where] = weight.astype(BF16)
        store(slot, 2).start()
        store(slot, 3).start()
    for slot in range(len(blocks)):
        for kind in range(4):
            store(slot, kind).wait()


def fast_body(samples_in, target, mask, attn_w, ffn_w, spec_w, dense_w, vectors, *moments):
    flat_spec = spec_w.reshape(FLAYERS, MODES * 2 * FREQ, FREQ)
    grads = summed_grads(samples_in, target, mask, attn_w, ffn_w, flat_spec, dense_w.T, vectors)
    sets = [
        (attn_w, ffn_w, spec_w, dense_w.T),
        (moments[0], moments[1], moments[2], moments[3].T),
        (moments[5], moments[6], moments[7], moments[8].T),
    ]
    vmem = pl.BlockSpec(memory_space=pltpu.VMEM)
    smem = pl.BlockSpec(memory_space=pltpu.SMEM)
    anywhere = pl.BlockSpec(memory_space=pl.ANY)
    shapes = [item.shape for item in sets[0]]
    kinds = (F32, F32, F32, BF16)
    scalar = [jax.ShapeDtypeStruct((1,), F32)] * 2 + [jax.ShapeDtypeStruct((8,), F32)] * 3
    line = [jax.ShapeDtypeStruct(vectors.shape, kind) for kind in kinds]
    arrays = [jax.ShapeDtypeStruct(shape, kind) for kind in kinds for shape in shapes]
    out = pl.pallas_call(
        update_kernel,
        out_shape=scalar + line + arrays,
        in_specs=[vmem] * 7 + [anywhere] * 12,
        out_specs=[smem] * 5 + [vmem] * 4 + [anywhere] * 16,
        scratch_shapes=[pltpu.VMEM(shape, F32) for _ in range(3) for shape in shapes]
        + [pltpu.VMEM(shape, kind) for kind in kinds for shape in shapes]
        + [pltpu.VMEM(vectors.shape, F32), pltpu.SemaphoreType.DMA((21,)), pltpu.SemaphoreType.DMA((28,))],
        compiler_params=pltpu.CompilerParams(vmem_limit_bytes=60 * 2**20),
    )(*grads, vectors, moments[4], moments[9], *sets[0], *sets[1], *sets[2])
    loss_sum, valid_count, weight_norms, update_norms, ratios = out[:5]
    line, arrays = out[5:9], out[9:]
    results = [loss_sum.reshape(()), valid_count.reshape(())]
    for array in range(4):
        for kind in range(4):
            item = arrays[kind * 4 + array]
            results.append(item.T if array == 3 else item)
    return tuple(results + list(line) + [weight_norms, update_norms, ratios])


def choose_body(*arrays):
    samples_in = arrays[0]
    dp, parts = lax.axis_size("dp"), lax.axis_size("pts")
    fits = dp * parts == FLAYERS * MODES and dp == 4 and samples_in.shape[0] == 2 * parts
    return (fast_body if fits and samples_in.shape[2] * parts % ROWS == 0 else body)(*arrays)


def solution(mesh):
    placed = (
        P("dp", None, "pts"),
        P("dp", "pts"),
        P("dp", "pts"),
        P(),
        P(),
        P(),
        P(),
        P(),
        P(),
        P(),
        P(),
        P(),
        P(),
        P(),
        P(),
        P(),
        P(),
        P(),
    )
    return jax.shard_map(
        choose_body,
        mesh=mesh,
        in_specs=placed,
        out_specs=(
            P(),
            P(),
            P(),
            P(),
            P(),
            P(),
            P(),
            P(),
            P(),
            P(),
            P(),
            P(),
            P(),
            P(),
            P(),
            P(),
            P(),
            P(),
            P(),
            P(),
            P(),
            P(),
            P(),
            P(),
            P(),
        ),
        check_vma=False,
    )
```

```python
import math

import jax
import jax.numpy as jnp
import ml_dtypes
import numpy as np
from jax import lax
from jax.experimental import pallas as pl
from jax.experimental.pallas import tpu as pltpu
from jax.sharding import PartitionSpec as P

D = 128
HEADS = 4
FF = 256
FREQ = 64
MODES = 16
LAYERS = 2
FLAYERS = 2
STEP = 5


HIGH = lax.Precision.HIGHEST
NORM_EPS = 1e-05
BETA_ONE = 0.5
BETA_TWO = 0.5
RATE = 0.2
DECAY = 0.01
ADAM_EPS = 1e-06


def vector_table():
    entries = [("lift_value", 0, D), ("lift_coord", 0, D), ("lift_bias", 0, D)]
    for layer in range(LAYERS):
        entries = entries + [
            ("key_gain", layer, D),
            ("value_gain", layer, D),
            ("inner_bias", layer, FF),
            ("outer_bias", layer, D),
        ]
    entries = entries + [("proj_bias", 0, FREQ)]
    for layer in range(FLAYERS):
        entries = entries + [("fourier_bias", layer, FREQ)]
    entries = entries + [("head_bias", 0, FREQ), ("head_out", 0, FREQ)]
    offsets = {}
    start = 0
    for label, layer, length in entries:
        offsets[label, layer] = (start, length)
        start = start + length
    return offsets


def pick(vectors, label, layer):
    start, length = vector_table()[label, layer]
    return vectors[start : start + length]


def head_norm(values, gain):
    centred = values - jnp.mean(values, -1, keepdims=True)
    scaled = centred * lax.rsqrt(jnp.mean(centred * centred, -1, keepdims=True) + NORM_EPS)
    return scaled * gain.reshape(HEADS, D // HEADS)


def lift(params, inputs):
    vectors = params[4]
    value = inputs[..., 0, :, None]
    coord = inputs[..., 1, :, None]
    return (
        value * pick(vectors, "lift_value", 0)
        + coord * pick(vectors, "lift_coord", 0)
        + pick(vectors, "lift_bias", 0)
    )


def attn_front(params, rows, layer, points):
    weight = params[0][layer]
    vectors = params[4]
    mixed = jnp.einsum("...d,de->...e", rows, weight[:, : 3 * D], precision=HIGH)
    shape = rows.shape[:-1] + (HEADS, D // HEADS)
    query = mixed[..., :D].reshape(shape)
    keys = head_norm(mixed[..., D : 2 * D].reshape(shape), pick(vectors, "key_gain", layer))
    values = head_norm(mixed[..., 2 * D :].reshape(shape), pick(vectors, "value_gain", layer))
    partial_sum = jnp.einsum("...phe,...phf->...hef", keys, values, precision=HIGH) / points
    return (query, partial_sum)


def attn_rear(params, rows, query, summary, layer):
    weight = params[0][layer]
    attended = jnp.einsum("...phe,...hef->...phf", query, summary, precision=HIGH).reshape(
        rows.shape
    )
    return rows + jnp.einsum("...d,de->...e", attended, weight[:, 3 * D :], precision=HIGH)


def ffn_block(params, rows, layer):
    weight = params[1][layer]
    vectors = params[4]
    inner = jnp.einsum("...d,df->...f", rows, weight[0], precision=HIGH) + pick(
        vectors, "inner_bias", layer
    )
    outer = jnp.einsum("...f,df->...d", jax.nn.gelu(inner), weight[1], precision=HIGH)
    return rows + outer + pick(vectors, "outer_bias", layer)


def project(params, rows):
    return jnp.einsum("...d,df->...f", rows, params[3][:D], precision=HIGH) + pick(
        params[4], "proj_bias", 0
    )


def mode_table(count, total):
    position = jnp.arange(count, dtype=jnp.int32)
    orders = jnp.arange(MODES, dtype=jnp.int32)
    phase = orders[:, None] * position[None, :] % total
    angle = phase.astype(jnp.float32) * (2.0 * math.pi / total)
    return jnp.concatenate([jnp.cos(angle), jnp.sin(angle)], 0)


def spectral_mix(coef, spec, first, width):
    columns = lax.dynamic_slice_in_dim(spec, first, width, 3)
    cosine = coef[..., :MODES, :]
    sine = coef[..., MODES:, :]
    real_part = columns[:, 0]
    imag_part = columns[:, 1]
    mixed_cos = jnp.einsum("...mf,mfg->...mg", cosine, real_part, precision=HIGH) + jnp.einsum(
        "...mf,mfg->...mg", sine, imag_part, precision=HIGH
    )
    mixed_sin = jnp.einsum("...mf,mfg->...mg", sine, real_part, precision=HIGH) - jnp.einsum(
        "...mf,mfg->...mg", cosine, imag_part, precision=HIGH
    )
    return jnp.concatenate([mixed_cos, mixed_sin], -2)


def fourier_end(params, back, rows, layer):
    local = params[3][D + layer * FREQ : D + (layer + 1) * FREQ]
    inner = back + jnp.einsum("...f,fg->...g", rows, local, precision=HIGH)
    return jax.nn.gelu(inner + pick(params[4], "fourier_bias", layer))


def head_loss(params, rows, target, mask_f):
    start = D + FLAYERS * FREQ
    hidden = jax.nn.gelu(
        jnp.einsum("...f,fg->...g", rows, params[3][start : start + FREQ], precision=HIGH)
        + pick(params[4], "head_bias", 0)
    )
    pred = jnp.einsum("...f,f->...", hidden, pick(params[4], "head_out", 0), precision=HIGH)
    diff = pred - target
    return jnp.sum(mask_f * diff * diff)


def add_all(first, second):
    return jax.tree.map(jnp.add, first, second)


def spectral_setup(points, parts):
    width = FREQ // parts
    return (mode_table(points, points), lax.axis_index("pts") * width, width, points)


def fourier_mix(spec, field, setup):
    grid, column, width, points = setup
    channel_rows = lax.all_to_all(field, "pts", split_axis=2, concat_axis=1, tiled=True)
    own_coef = jnp.einsum("kp,spc->skc", grid, channel_rows, precision=HIGH) / math.sqrt(points)
    full = lax.all_gather(own_coef, "pts", axis=2, tiled=True)
    mixed = spectral_mix(full, spec, column, width)
    spread = jnp.einsum("kp,skc->spc", grid, mixed, precision=HIGH) / math.sqrt(MODES)
    back = lax.all_to_all(spread, "pts", split_axis=1, concat_axis=2, tiled=True)
    return (back, full)


def fourier_back(params, grad_out, kept_item, layer, setup):
    field, full, back = kept_item
    grid, column, width, points = setup
    _, end_pull = jax.vjp(
        lambda weights, spread, inner: fourier_end(weights, spread, inner, layer),
        params,
        back,
        field,
    )
    grads, grad_back, grad_field = end_pull(grad_out)
    _, mix_pull = jax.vjp(
        lambda coef, weight: spectral_mix(coef, weight, column, width), full, params[2][layer]
    )
    grad_rows = lax.all_to_all(grad_back, "pts", split_axis=2, concat_axis=1, tiled=True)
    grad_mixed = jnp.einsum("kp,spc->skc", grid, grad_rows, precision=HIGH) / math.sqrt(MODES)
    grad_full, grad_spec = mix_pull(grad_mixed)
    grad_coef = lax.psum_scatter(grad_full, "pts", scatter_dimension=2, tiled=True)
    grad_chan = jnp.einsum("kp,skc->spc", grid, grad_coef, precision=HIGH) / math.sqrt(points)
    grad_field = grad_field + lax.all_to_all(
        grad_chan, "pts", split_axis=1, concat_axis=2, tiled=True
    )
    grads = (grads[0], grads[1], grads[2].at[layer].add(grad_spec), grads[3], grads[4])
    return (grads, grad_field)


def attention_back(params, grad_rows, kept_item, layer, points):
    rows, summary = kept_item
    (query, partial_sum), front_pull = jax.vjp(
        lambda weights, inner: attn_front(weights, inner, layer, points), params, rows
    )
    summary = lax.psum(partial_sum, "pts")
    middle, rear_pull = jax.vjp(
        lambda weights, inner, asked, summed: attn_rear(weights, inner, asked, summed, layer),
        params,
        rows,
        query,
        summary,
    )
    _, ffn_pull = jax.vjp(lambda weights, inner: ffn_block(weights, inner, layer), params, middle)
    ffn_grads, grad_middle = ffn_pull(grad_rows)
    rear_grads, grad_direct, grad_query, grad_summary = rear_pull(grad_middle)
    grad_summary = lax.psum(grad_summary, "pts")
    front_grads, grad_front = front_pull((grad_query, grad_summary))
    return (add_all(add_all(ffn_grads, rear_grads), front_grads), grad_direct + grad_front)


def lamb(weight, grad, first, second):
    first_new = BETA_ONE * first + (1.0 - BETA_ONE) * grad
    second_new = BETA_TWO * second + (1.0 - BETA_TWO) * grad * grad
    update = (
        first_new
        / (1.0 - BETA_ONE**STEP)
        / (jnp.sqrt(second_new / (1.0 - BETA_TWO**STEP)) + ADAM_EPS)
        + DECAY * weight
    )
    return (first_new, second_new, update)


def trust_step(weight, update, stacked):
    axes = tuple(range(1, weight.ndim)) if stacked else tuple(range(weight.ndim))
    weight_norm = jnp.sqrt(jnp.sum(weight * weight, axes))
    update_norm = jnp.sqrt(jnp.sum(update * update, axes))
    ratio = weight_norm / (update_norm + ADAM_EPS)
    scale = ratio.reshape(ratio.shape + (1,) * (weight.ndim - ratio.ndim))
    return (
        weight - RATE * scale * update,
        jnp.atleast_1d(weight_norm),
        jnp.atleast_1d(update_norm),
        jnp.atleast_1d(ratio),
    )


def finish(loss_sum, valid_count, params, grads, firsts, seconds):
    results = [loss_sum, valid_count]
    weight_norms, update_norms, ratios = ([], [], [])
    for weight, grad, first, second, stacked in zip(
        params, grads, firsts, seconds, (True, True, True, False, False)
    ):
        first_new, second_new, update = lamb(weight, grad, first, second)
        fresh, weight_norm, update_norm, ratio = trust_step(weight, update, stacked)
        results = results + [first_new, second_new, fresh, fresh.astype(jnp.bfloat16)]
        weight_norms.append(weight_norm)
        update_norms.append(update_norm)
        ratios.append(ratio)
    return results + [
        jnp.concatenate(weight_norms),
        jnp.concatenate(update_norms),
        jnp.concatenate(ratios),
    ]


def body(
    samples_in,
    target,
    mask,
    attn_w,
    ffn_w,
    spec_w,
    dense_w,
    vectors,
    attn_m,
    ffn_m,
    spec_m,
    dense_m,
    vector_m,
    attn_v,
    ffn_v,
    spec_v,
    dense_v,
    vector_v,
):
    params = (attn_w, ffn_w, spec_w, dense_w, vectors)
    parts = lax.axis_size("pts")
    local_pts = samples_in.shape[2]
    points = local_pts * parts
    mask_f = mask.astype(jnp.float32)
    valid_count = lax.psum(jnp.sum(mask_f), ("dp", "pts"))
    setup = spectral_setup(points, parts)
    rows, lift_pull = jax.vjp(lambda weights: lift(weights, samples_in), params)
    kept = []
    for layer in range(LAYERS):
        query, partial_sum = attn_front(params, rows, layer, points)
        summary = lax.psum(partial_sum, "pts")
        kept.append((rows, summary))
        rows = ffn_block(params, attn_rear(params, rows, query, summary, layer), layer)
    field, proj_pull = jax.vjp(project, params, rows)
    spectral_kept = []
    for layer in range(FLAYERS):
        back, full = fourier_mix(params[2][layer], field, setup)
        spectral_kept.append((field, full, back))
        field = fourier_end(params, back, field, layer)
    loss_part, head_pull = jax.vjp(
        lambda weights, inner: head_loss(weights, inner, target, mask_f), params, field
    )
    grads, grad_field = head_pull(1.0 / valid_count)
    for layer in reversed(range(FLAYERS)):
        layer_grads, grad_field = fourier_back(
            params, grad_field, spectral_kept[layer], layer, setup
        )
        grads = add_all(grads, layer_grads)
    proj_grads, grad_rows = proj_pull(grad_field)
    grads = add_all(grads, proj_grads)
    for layer in reversed(range(LAYERS)):
        layer_grads, grad_rows = attention_back(params, grad_rows, kept[layer], layer, points)
        grads = add_all(grads, layer_grads)
    grads = add_all(grads, lift_pull(grad_rows)[0])
    summed = lax.psum((grads[0], grads[1], grads[2], grads[3], grads[4], loss_part), ("dp", "pts"))
    out = finish(
        summed[5],
        valid_count,
        params,
        summed[:5],
        (attn_m, ffn_m, spec_m, dense_m, vector_m),
        (attn_v, ffn_v, spec_v, dense_v, vector_v),
    )
    return (
        out[0],
        out[1],
        out[2],
        out[3],
        out[4],
        out[5],
        out[6],
        out[7],
        out[8],
        out[9],
        out[10],
        out[11],
        out[12],
        out[13],
        out[14],
        out[15],
        out[16],
        out[17],
        out[18],
        out[19],
        out[20],
        out[21],
        out[22],
        out[23],
        out[24],
    )


F32 = jnp.float32
BF16 = jnp.bfloat16
ROWS = 1024
WIDE = 2048
NVEC_ROWS = 16


def dot(first, second, left=1, right=0, precision=None):
    return lax.dot_general(
        first,
        second,
        (((left,), (right,)), ((), ())),
        precision=precision,
        preferred_element_type=F32,
    )


def exact(first, second, left=1, right=0):
    return dot(first, second, left, right, HIGH)


def halves(value):
    high = value.astype(BF16)
    return high, (value - high.astype(F32)).astype(BF16)


def thirds(value):
    high = value.astype(BF16)
    rest = value - high.astype(F32)
    middle = rest.astype(BF16)
    return high, middle, (rest - middle.astype(F32)).astype(BF16)


def beside(*pieces):
    return jnp.concatenate(pieces, 1)


def above(*pieces):
    return jnp.concatenate(pieces, 0)


def fold(value):
    half = value.shape[1] // 2
    return value[:, :half] + value[:, half:]


def column_sum(value):
    rows, width = value.shape
    return jnp.sum(value.reshape(rows // 8, 8, width), 0)


def gelu_pair(inner):
    scale = math.sqrt(2.0 / math.pi)
    square = inner * inner
    bend = jnp.tanh(inner * (scale + (scale * 0.044715) * square))
    half = 0.5 + 0.5 * bend
    slope = half + (0.5 * inner) * (1.0 - bend * bend) * (scale + (3.0 * scale * 0.044715) * square)
    return inner * half, slope


def wide6_weight(weight):
    high, middle, low = thirds(weight)
    return above(high, high, middle, middle, low, high)


def wide6(pieces, weight):
    high, middle, low = pieces
    return dot(beside(high, middle, high, middle, high, low), weight)


def tall6_weight(weight):
    high, middle, low = thirds(weight)
    pair = beside(high, middle)
    return above(pair, pair), above(low, high)


def tall6(pieces, weights):
    high, middle, low = pieces
    return fold(dot(beside(high, middle), weights[0])) + dot(beside(high, low), weights[1])


def even4_weight(weight):
    high, low = halves(weight)
    pair = beside(high, low)
    return above(pair, pair)


def even4(pieces, weight):
    return fold(dot(beside(*pieces), weight))


def head_blocks(width):
    row = lax.broadcasted_iota(jnp.int32, (width, width), 0)
    column = lax.broadcasted_iota(jnp.int32, (width, width), 1)
    return row // (D // HEADS) == column // (D // HEADS)


def doubled(weight):
    zero = jnp.zeros_like(weight)
    return above(beside(weight, zero), beside(zero, weight))


MESH = pl.DeviceIdType.MESH


def position():
    dp, pts = lax.axis_index("dp"), lax.axis_index("pts")
    x, core, z, y = dp // 2, dp % 2, pts // 2, pts % 2
    return x, core, z, y


def device_of(x, core, z, y):
    return (2 * x + core, 2 * z + y)


def others(both_cores):
    x, core, z, y = position()
    xs, ys, cores = (x, 1 - x), (y, 1 - y), (core, 1 - core)
    zs = [lax.rem(z + k, 4) for k in range(4)]
    found = []
    for c in cores if both_cores else cores[:1]:
        for i in range(16):
            place = (xs[i // 8], ys[i // 4 % 2], zs[i % 4])
            number = 16 * c + 8 * place[0] + 4 * place[1] + place[2]
            found.append((number, device_of(place[0], c, place[2], place[1])))
    return found[1:]


class Route:
    def __init__(self, rows, full, flat, landing, sends, receives, first):
        x, core, z, y = position()
        self.core, self.group = core, FLAYERS * MODES // 2
        self.rows, self.full, self.flat, self.landing = rows, full, flat, landing
        self.sends, self.receives, self.first = sends, receives, first
        self.peer = device_of(x, 1 - core, z, y)
        self.half, self.least = rows // 2, rows // (2 * self.group)
        self.own = (16 * core + 8 * x + 4 * y + z) * self.least
        self.group_others = others(False)

    def area(self, start, size):
        return pl.ds(pl.multiple_of(start, self.least), size)

    def link(self, source, target, slot, device):
        return pltpu.make_async_remote_copy(
            src_ref=source,
            dst_ref=target,
            send_sem=self.sends.at[self.first + slot],
            recv_sem=self.receives.at[self.first + slot],
            device_id=device,
            device_id_type=MESH,
        )

    def copies(self, stage, start):
        half, least, core, group = self.half, self.least, self.core, self.group
        mine, yours = self.area(core * half, half), self.area((1 - core) * half, half)
        if stage == 0:
            return [self.link(self.flat.at[yours], self.landing.at[pl.ds(0, half)], 2 * group - 1, self.peer)]
        if stage == 3:
            return [self.link(self.full.at[mine], self.full.at[mine if start else yours], 2 * group - 2, self.peer)]
        found = []
        for i, (number, device) in enumerate(self.group_others):
            if stage == 1:
                source = self.flat.at[self.area(number * least, least)]
                target = self.landing.at[pl.ds(half + i * least, least)]
            else:
                start_row = self.own if start else self.group_others[back_of(i)][0] * least
                source = self.full.at[self.area(self.own, least)]
                target = self.full.at[self.area(start_row, least)]
            found.append(self.link(source, target, (stage - 1) * (group - 1) + i, device))
        return found

    def start(self, stage):
        if stage == 2 and self.flat is not None:
            self.full[self.area(self.own, self.least), :] = self.flat[self.area(self.own, self.least), :]
        for copy in self.copies(stage, True):
            copy.start()

    def finish(self, stage):
        for copy in self.copies(stage, False):
            copy.wait()
        if stage == 0:
            self.flat[self.area(self.core * self.half, self.half), :] += self.landing[: self.half, :]
        if stage == 1:
            mine = self.area(self.own, self.least)
            total = self.flat[mine, :]
            for i in range(self.group - 1):
                start = self.half + i * self.least
                total = total + self.landing[start : start + self.least, :]
            self.flat[mine, :] = total

    def step(self, stage):
        self.finish(stage)
        self.start(stage + 1)


def back_of(i):
    group, rest = (i + 1) // 4 * 4, (i + 1) % 4
    return group + (4 - rest) % 4 - 1


def to_each(source_of, target, slot_of, mine, sends, receives, both_cores, start):
    found = others(both_cores)
    for i, (number, device) in enumerate(found):
        sender = found[back_of(i)][0]
        copy = pltpu.make_async_remote_copy(
            src_ref=source_of(number),
            dst_ref=target.at[slot_of(mine if start else sender)],
            send_sem=sends.at[i],
            recv_sem=receives.at[i],
            device_id=device,
            device_id_type=MESH,
        )
        if start:
            copy.start()
        else:
            copy.wait()


def step_kernel(
    samples_ref,
    target_ref,
    mask_ref,
    attn_ref,
    ffn_ref,
    spec_any,
    turned_ref,
    vectors_ref,
    table_any,
    trow_any,
    early_any,
    late_out,
    mode_any,
    tail_out,
    spec_ref,
    table_ref,
    trow_ref,
    early_out,
    mode_out,
    local_sems,
    outgoing,
    incoming,
    vec_ref,
    early,
    early_land,
    late,
    late_land,
    mode_send,
    mode_land,
    tail_send,
    tail_swap,
    tail_pair,
    tail_land,
    route_send,
    route_recv,
    point_send,
    point_recv,
    mode_sends,
    mode_recvs,
    tail_sends,
    tail_recvs,
    lifted,
    lrows,
    w_kv,
    w_kvt,
    w_in,
    w_int,
    w0_u,
    mid_rows,
    w_out0,
    w_out1,
    w_outt,
    x_keep,
    r_keep,
    slope_keep,
    act_keep,
    mid_keep,
    h1_keep,
    h2_keep,
    z_keep,
    e_keep,
    s_acc,
    w0_kv,
    w0_g,
    n_keep,
    small_keep,
    nt_keep,
    cent_keep,
    coef_acc,
    coef_keep,
    stack_ref,
    sq_acc,
    p_acc,
    w2_acc,
    w1_acc,
    kv_acc,
    v_acc,
    u_acc,
    vt_acc,
    b_acc,
    d_keep,
    t_keep,
    wz,
):
    parts = samples_ref.shape[0] // 2
    count = 2
    points = samples_ref.shape[2] * parts
    devices = FLAYERS * MODES
    x, core, z, y = position()
    pts = 2 * z + y
    place = 8 * x + 4 * y + z
    mine = 16 * core + place
    early_route = Route(early.shape[0], early_out, early, early_land, route_send, route_recv, 0)
    late_route = Route(late.shape[0], late_out, late, late_land, route_send, route_recv, devices)
    mode_route = Route(mode_out.shape[0], mode_out, None, None, route_send, route_recv, 2 * devices)

    barrier = pltpu.get_barrier_semaphore()
    take = [
        pltpu.make_async_copy(source, target, local_sems.at[i])
        for i, (source, target) in enumerate(((trow_any, trow_ref), (spec_any, spec_ref), (table_any, table_ref)))
    ]
    put_mode = pltpu.make_async_copy(mode_out, mode_any, local_sems.at[3])
    put_early = pltpu.make_async_copy(early_out, early_any, local_sems.at[4])
    for copy in take:
        copy.start()

    for _, device in others(True):
        pl.semaphore_signal(barrier, inc=1, device_id=device, device_id_type=MESH)
    for p in range(parts):
        outgoing[p, 0:2, :] = samples_ref[2 * p]
        outgoing[p, 2:4, :] = samples_ref[2 * p + 1]
        outgoing[p, 4:6, :] = target_ref[2 * p : 2 * p + 2, :]
        outgoing[p, 6:8, :] = mask_ref[2 * p : 2 * p + 2, :].astype(F32)
    incoming[pts] = outgoing[pts]
    for i in range(NVEC_ROWS - 1):
        vec_ref[i : i + 1, :] = vectors_ref[i * D : (i + 1) * D].reshape(1, D)
    last = vectors_ref.shape[0] - (NVEC_ROWS - 1) * D
    vec_ref[NVEC_ROWS - 1 :, :last] = vectors_ref[(NVEC_ROWS - 1) * D :].reshape(1, last)
    total = count * points
    steps = points // ROWS
    rows_all = total // ROWS
    blocks = head_blocks(D)
    block_f = jnp.where(blocks, 1.0, 0.0).astype(F32)
    block_b = block_f.astype(BF16)
    mean_weight = above(block_b, block_b)
    centre = (
        jnp.where(
            lax.broadcasted_iota(jnp.int32, (D, D), 0) == lax.broadcasted_iota(jnp.int32, (D, D), 1),
            1.0,
            0.0,
        ).astype(F32)
        - block_f * (HEADS / D)
    )
    eye = jnp.where(
        lax.broadcasted_iota(jnp.int32, (D, D), 0) == lax.broadcasted_iota(jnp.int32, (D, D), 1), 1.0, 0.0
    ).astype(F32)

    def vector(label, layer):
        start, length = vector_table()[label, layer]
        if length == 2 * D:
            row = start // D
            return beside(vec_ref[row : row + 1, :], vec_ref[row + 1 : row + 2, :])
        row = start // D
        if length == D:
            return vec_ref[row : row + 1, :]
        offset = start - row * D
        piece = vec_ref[row : row + 1, offset : offset + FREQ]
        return beside(piece, piece)

    def block(index):
        return pl.ds(pl.multiple_of(index * ROWS, ROWS), ROWS)

    wide_steps = points // WIDE

    def wide_block(index):
        return pl.ds(pl.multiple_of(index * WIDE, WIDE), WIDE)

    lift_rows = above(
        vector("lift_value", 0), vector("lift_coord", 0), vector("lift_bias", 0), jnp.zeros((5, D), F32)
    )

    def lift_weight(mixed):
        high, middle, low = [item.astype(F32) for item in thirds(mixed)]
        parts = []
        for i in range(2):
            hi, mi, lo = high[i : i + 1], middle[i : i + 1], low[i : i + 1]
            parts += [hi, hi, mi, mi, lo, hi]
        parts += [high[2:3], middle[2:3], low[2:3]]
        parts.append(jnp.zeros((D - 15, mixed.shape[1]), F32))
        return above(*parts).astype(BF16)

    def point_copy(k, start):
        other = lax.rem(pts + k, parts)
        sender = lax.rem(pts + parts - k, parts)
        return pltpu.make_async_remote_copy(
            src_ref=outgoing.at[other],
            dst_ref=incoming.at[pts if start else sender],
            send_sem=point_send.at[k - 1],
            recv_sem=point_recv.at[k - 1],
            device_id=(2 * x + core, other),
            device_id_type=MESH,
        )

    for layer in range(LAYERS):
        if layer == 1:
            pl.semaphore_wait(barrier, devices - 1)
            for k in range(1, parts):
                point_copy(k, True).start()
        weight = attn_ref[layer]
        keyed = beside(exact(weight[:, D : 2 * D], centre), exact(weight[:, 2 * D : 3 * D], centre))
        cent_keep[layer] = keyed
        if layer == 0:
            w0_kv[...] = lift_weight(exact(lift_rows, keyed))
        else:
            w_kv[...] = wide6_weight(keyed)
            pair, rest = tall6_weight(keyed.T)
            w_kvt[:, : 2 * D] = pair
            w_kvt[:, 2 * D :] = rest
        first, second = ffn_ref[layer, 0], ffn_ref[layer, 1]
        if layer:
            w_in[...] = wide6_weight(first)
            pair, rest = tall6_weight(first.T)
            w_int[:, : 2 * D] = pair
            w_int[:, 2 * D :] = rest
        pair, rest = tall6_weight(second.T)
        w_out0[layer] = pair
        w_out1[layer] = rest
        w_outt[layer] = wide6_weight(second)

    s_acc[...] = jnp.zeros_like(s_acc)
    coef_acc[...] = jnp.zeros_like(coef_acc)
    sq_acc[...] = jnp.zeros_like(sq_acc)
    p_acc[...] = jnp.zeros_like(p_acc)
    w2_acc[...] = jnp.zeros_like(w2_acc)
    w1_acc[...] = jnp.zeros_like(w1_acc)
    kv_acc[...] = jnp.zeros_like(kv_acc)
    v_acc[...] = jnp.zeros_like(v_acc)
    u_acc[...] = jnp.zeros_like(u_acc)
    vt_acc[...] = jnp.zeros_like(vt_acc)
    b_acc[...] = jnp.zeros_like(b_acc)

    for k in range(1, parts):
        point_copy(k, False).wait()
    whole = beside(*[incoming[p] for p in range(parts)])
    for s in range(count):
        value, coord = whole[2 * s : 2 * s + 1], whole[2 * s + 1 : 2 * s + 2]
        target, valid = whole[4 + s : 5 + s], whole[6 + s : 7 + s]
        one = jnp.ones_like(value)
        vh, vm, vl = [item.astype(F32) for item in thirds(value)]
        ch, cm, cl = [item.astype(F32) for item in thirds(coord)]
        th, tm, tl = [item.astype(F32) for item in thirds(target)]
        zero = jnp.zeros((D - 19, points), F32)
        stack = above(vh, vm, vh, vm, vh, vl, ch, cm, ch, cm, ch, cl, one, one, one, th, tm, tl, valid, zero)
        lifted[s * points : (s + 1) * points, :] = stack.T.astype(BF16)
        short = above(vh, vm, vl, ch, cm, cl, one, jnp.zeros((9, points), F32)).astype(BF16)
        for i in range(steps):
            lrows[s * steps + i] = short[:, i * ROWS : (i + 1) * ROWS]

    def head_scale(centred):
        high, low = halves(centred * centred)
        var = beside(
            dot(beside(high[:, :D], low[:, :D]), mean_weight), dot(beside(high[:, D:], low[:, D:]), mean_weight)
        )
        return lax.rsqrt(var * (HEADS / D) + NORM_EPS)

    def normalise(layer, where, s, centred):
        scale = head_scale(centred)
        normal = centred * scale
        if layer:
            x_keep[where, :] = normal
            r_keep[where, :] = scale
        high, low = halves(normal)
        s_acc[s] += dot(
            beside(high[:, :D], low[:, :D]), beside(high[:, D:], low[:, D:]), 0, 0
        )

    def quarters(value):
        half_row, half_col = value.shape[0] // 2, value.shape[1] // 2
        return (
            value[:half_row, :half_col]
            + value[half_row:, :half_col]
            + (value[:half_row, half_col:] + value[half_row:, half_col:])
        )

    def summarise(layer):
        weight = attn_ref[layer]
        key_gain = vector("key_gain", layer).reshape(1, D)
        value_gain = vector("value_gain", layer).reshape(1, D)
        key_column = jnp.sum(eye * key_gain, 1, keepdims=True)
        for s in range(count):
            plain = jnp.where(blocks, quarters(s_acc[s]), 0.0) * (1.0 / points)
            summary = key_column * plain * value_gain
            mixed = exact(summary, weight[:, 3 * D :])
            both = exact(weight[:, :D], mixed)
            n_keep[layer, s] = both
            small_keep[layer, s, 0] = plain
            small_keep[layer, s, 1] = summary
            small_keep[layer, s, 2] = mixed
            if layer == 0:
                rows = exact(lift_rows, eye + both)
                mid_rows[s] = rows
                w0_g[s] = lift_weight(rows)
                w0_u[s] = lift_weight(exact(rows, ffn_ref[0, 0]))
            else:
                pair, rest = tall6_weight(both)
                wz[s, : 2 * D, :] = pair
                wz[s, 2 * D :, :D] = rest
                nt_keep[s] = even4_weight(both.T)

    def feed(layer, index, mid, inner):
        where = block(index)
        act, slope = gelu_pair(inner + vector("inner_bias", layer))
        slope_keep[layer, where, :] = slope
        pieces = thirds(act)
        act_keep[layer, where, :] = beside(pieces[0], pieces[1])
        return mid + tall6(pieces, (w_out0[layer], w_out1[layer])) + vector("outer_bias", layer)

    def front_zero(index, _):
        where = wide_block(index)
        normalise(0, where, index // wide_steps, dot(lifted[where, :], w0_kv[...]))
        return 0

    lax.fori_loop(0, count * wide_steps, front_zero, 0)
    summarise(0)
    s_acc[...] = jnp.zeros_like(s_acc)

    def layer_zero(index, _):
        where = block(index)
        s = index // steps
        data = lifted[where, :]
        out = feed(0, index, dot(data, w0_g[s]), dot(data, w0_u[s]))
        d_keep[where, :] = out
        pieces = thirds(out)
        h1_keep[where, :] = beside(pieces[0], pieces[1])
        h2_keep[where, 2 * D :] = pieces[2]
        normalise(1, where, s, wide6(pieces, w_kv[...]))
        return 0

    lax.fori_loop(0, rows_all, layer_zero, 0)
    summarise(1)
    s_acc[...] = jnp.zeros_like(s_acc)

    def pieces_of(ref, where, number=3):
        value = ref[where, : number * D]
        return [value[:, i * D : (i + 1) * D] for i in range(number)]

    def layer_one(index, _):
        where = block(index)
        s = index // steps
        pieces = pieces_of(h1_keep, where, 2) + [h2_keep[where, 2 * D :]]
        mid = d_keep[where, :] + tall6(pieces, (wz[s, : 2 * D, :], wz[s, 2 * D :, :D]))
        pieces = thirds(mid)
        mid_keep[where, :] = beside(pieces[0], pieces[1])
        out = feed(1, index, mid, wide6(pieces, w_in[...]))
        h2_keep[where, :] = beside(*thirds(out))
        return 0

    lax.fori_loop(0, rows_all, layer_one, 0)

    def dense_rows(part):
        start = D + (part - 1) * FREQ if part else 0
        return turned_ref[:, start : start + (FREQ if part else D)].T

    proj0, proj1 = tall6_weight(doubled(dense_rows(0)))
    locals6 = [tall6_weight(doubled(dense_rows(part))) for part in (1, 2, 3)]
    turned6 = [tall6_weight(doubled(dense_rows(part).T)) for part in (1, 2, 3)]
    own = lax.broadcasted_iota(jnp.int32, (2 * count * MODES, MODES * D), 1) // D == lax.rem(
        lax.broadcasted_iota(jnp.int32, (2 * count * MODES, MODES * D), 0), MODES
    )

    def mode_rows(coef):
        cosine, sine = coef[:MODES], coef[MODES:]
        c = [cosine[:, s * FREQ : (s + 1) * FREQ] for s in range(count)]
        d = [sine[:, s * FREQ : (s + 1) * FREQ] for s in range(count)]
        return above(
            *[beside(c[s], d[s]) for s in range(count)], *[beside(d[s], -c[s]) for s in range(count)]
        )

    def spread_rows(rows):
        return jnp.where(own, beside(*([rows] * MODES)), 0.0)

    def unpack(rows):
        lead = count * MODES
        return above(
            *[beside(*[rows[j * lead + s * MODES : j * lead + (s + 1) * MODES] for s in range(count)]) for j in (0, 1)]
        )

    def pack(value):
        return above(
            *[
                value[j * MODES : (j + 1) * MODES, s * FREQ : (s + 1) * FREQ]
                for j in (0, 1)
                for s in range(count)
            ]
        )

    def set_stack(value):
        high, middle, low = thirds(value)
        stack_ref[...] = above(
            high, high, middle, middle, low, high, jnp.zeros((4 * MODES, D), BF16)
        )

    def take_coef(index, high, low):
        both = beside(high, low)
        each = both.shape[0] // ROWS
        for i in range(each):
            coef_acc[...] += dot(trow_ref[index * each + i], both[i * ROWS : (i + 1) * ROWS])

    def mix_forward(layer):
        coef = quarters(coef_acc[...]) * (1.0 / math.sqrt(points))
        coef_acc[...] = jnp.zeros_like(coef_acc)
        rows = mode_rows(coef)
        coef_keep[layer] = rows
        set_stack(unpack(exact(spread_rows(rows), spec_ref[layer])) * (1.0 / math.sqrt(MODES)))

    def mix_back(layer):
        cot = pack(quarters(coef_acc[...])) * (1.0 / math.sqrt(MODES))
        coef_acc[...] = jnp.zeros_like(coef_acc)
        kept_rows = coef_keep[layer]
        padded = beside(cot, jnp.zeros_like(cot))
        for k in range(MODES):
            for r in range(2 * count):
                mode_send[layer * MODES + k, r : r + 1, :] = kept_rows[r * MODES + k : r * MODES + k + 1]
                mode_send[layer * MODES + k, 4 + r : 5 + r, :] = padded[r * MODES + k : r * MODES + k + 1]
        wide = jnp.where(own, exact(cot, spec_ref[layer], 1, 1), 0.0)
        kept = wide[:, :D]
        for k in range(1, MODES):
            kept = kept + wide[:, k * D : (k + 1) * D]
        lead = count * MODES
        first, second = kept[:lead], kept[lead:]
        rows = above(first[:, :FREQ] - second[:, FREQ:], first[:, FREQ:] + second[:, :FREQ])
        set_stack(unpack(rows) * (1.0 / math.sqrt(points)))

    def project_step(index, _):
        where = wide_block(index)
        first = h2_keep[wide_block(index), :]
        second = h2_keep[wide_block(index + wide_steps), :]
        pieces = [beside(first[:, i * D : (i + 1) * D], second[:, i * D : (i + 1) * D]) for i in range(3)]
        field = tall6(pieces, (proj0, proj1)) + vector("proj_bias", 0)
        pieces = thirds(field)
        z_keep[0, where, :] = beside(*pieces)
        take_coef(index, pieces[0], pieces[1])
        return 0

    for copy in take:
        copy.wait()
    lax.fori_loop(0, wide_steps, project_step, 0)
    mix_forward(0)

    def fourier_field(layer, where):
        pieces = pieces_of(z_keep.at[layer], where)
        inner = dot(table_ref[where, :], stack_ref[...]) + (
            tall6(pieces, locals6[layer]) + vector("fourier_bias", layer)
        )
        return gelu_pair(inner)

    def fourier_one(index, _):
        where = wide_block(index)
        field, slope = fourier_field(0, where)
        d_keep[where, :] = slope
        pieces = thirds(field)
        z_keep[1, where, :] = beside(*pieces)
        take_coef(index, pieces[0], pieces[1])
        return 0

    lax.fori_loop(0, wide_steps, fourier_one, 0)
    mix_forward(1)

    lane = lax.broadcasted_iota(jnp.int32, (2 * D, 2 * D), 1)
    row = lax.broadcasted_iota(jnp.int32, (2 * D, 2 * D), 0)
    inner_row = lax.rem(row, D)
    same = row // D == lax.rem(lane, D) // FREQ
    pick_target = (lane < D) & (inner_row >= 15) & (inner_row < 18)
    pick_mask = (lane >= D) & (inner_row == 18)
    spread = jnp.where(same & (pick_target | pick_mask), 1.0, 0.0).astype(BF16)
    out_row = vector("head_out", 0)
    out_column = jnp.sum(eye * out_row, 1, keepdims=True)
    half_blocks = (
        lax.broadcasted_iota(jnp.int32, (D, D), 0) // FREQ == lax.broadcasted_iota(jnp.int32, (D, D), 1) // FREQ
    )
    out_weight = tall6_weight(jnp.where(half_blocks, out_column, 0.0))

    def pair_product(first, second):
        return dot(beside(*first), beside(*second), 0, 0)

    def loss_step(index, _):
        where = block(index)
        field, slope = fourier_field(1, where)
        pieces = thirds(field)
        hidden, hidden_slope = gelu_pair(tall6(pieces, locals6[2]) + vector("head_bias", 0))
        pred = tall6(thirds(hidden), out_weight)
        known = dot(beside(lifted[where, :], lifted[block(index + steps), :]), spread)
        diff = pred - known[:, :D]
        valid = known[:, D:]
        cot = (2.0 * valid) * diff
        b_acc[0:8, :D] += column_sum(valid * diff * diff)
        b_acc[8:16, :D] += column_sum(valid)
        b_acc[16:24, :D] += column_sum(hidden * cot)
        cot = cot * out_row * hidden_slope
        b_acc[24:32, :D] += column_sum(cot)
        split = thirds(cot)
        sq_acc[2] += pair_product(pieces[:2], split[:2])
        cot = tall6(split, turned6[2]) * slope
        b_acc[32:40, :D] += column_sum(cot)
        split = thirds(cot)
        e_keep[where, :] = beside(*split)
        sq_acc[1] += pair_product(pieces_of(z_keep.at[1], where, 2), split[:2])
        take_coef(index, *split[:2])
        return 0

    lax.fori_loop(0, steps, loss_step, 0)
    mix_back(1)

    def fourier_cot(layer, where):
        return tall6(pieces_of(e_keep, where), turned6[layer]) + dot(table_ref[where, :], stack_ref[...])

    def fourier_back(index, _):
        where = wide_block(index)
        cot = fourier_cot(1, where) * d_keep[where, :]
        b_acc[40:48, :D] += column_sum(cot)
        split = thirds(cot)
        e_keep[where, :] = beside(*split)
        sq_acc[0] += pair_product(pieces_of(z_keep.at[0], where, 2), split[:2])
        take_coef(index, *split[:2])
        return 0

    lax.fori_loop(0, wide_steps, fourier_back, 0)
    mix_back(0)
    mode_land[mine] = mode_send[mine]
    to_each(lambda r: mode_send.at[r], mode_land, lambda r: r, mine, mode_sends, mode_recvs, True, True)
    proj_back = wide6_weight(doubled(turned_ref[:, :D]))

    def project_back(index, _):
        where = wide_block(index)
        later = wide_block(index + wide_steps)
        cot = fourier_cot(0, where)
        b_acc[48:56, :D] += column_sum(cot)
        split = thirds(cot)
        first = pieces_of(h2_keep, where, 2)
        second = pieces_of(h2_keep, later, 2)
        p_acc[...] += dot(beside(first[0], second[0], first[1], second[1]), beside(*split[:2]), 0, 0)
        rows = wide6(split, proj_back)
        d_keep[where, :] = rows[:, :D]
        d_keep[later, :] = rows[:, D:]
        return 0

    lax.fori_loop(0, wide_steps, project_back, 0)

    def feed_back(layer, index, cot):
        where = block(index)
        base = 56 + layer * 16
        b_acc[base : base + 8, :D] += column_sum(cot)
        split = thirds(cot)
        act = act_keep[layer, where, :]
        w2_acc[layer] += dot(beside(*split[:2]), act[:, :FF], 0, 0)
        w2_acc[layer, :D, :] += dot(split[0], act[:, FF:], 0, 0)
        inner = wide6(split, w_outt[layer]) * slope_keep[layer, where, :]
        b_acc[base + 8 : base + 16, :] += column_sum(inner)
        return split, thirds(inner)

    def layer_one_back(index, _):
        @pl.when(index == 1)
        def _():
            to_each(lambda r: mode_send.at[r], mode_land, lambda r: r, mine, mode_sends, mode_recvs, True, False)
            landed = mode_land[...].reshape(devices * 8, D)
            shifted = above(landed[4:], landed[:4])
            row = lax.broadcasted_iota(jnp.int32, landed.shape, 0)
            product = exact(jnp.where(lax.rem(row, 8) < 4, landed, 0.0), shifted[:, :FREQ], 0, 0)
            mode_out[mode_route.area(mode_route.own, FREQ), :] = beside(product[:FREQ], product[FREQ:])
            mode_route.start(2)

        where = block(index)
        cot = d_keep[where, :]
        _, pieces = feed_back(1, index, cot)
        high, low = pieces[:2]
        mid = mid_keep[where, :]
        w1_acc[...] += dot(mid, high, 0, 0)
        w1_acc[:D, :] += dot(mid[:, :D], low, 0, 0)
        cot = cot + tall6(pieces, (w_int[:, : 2 * D], w_int[:, 2 * D :]))
        d_keep[where, :] = cot
        s_acc[index // steps] += pair_product(pieces_of(h1_keep, where, 2), halves(cot))
        return 0

    lax.fori_loop(0, rows_all, layer_one_back, 0)

    def attend_back(layer, products):
        weight = attn_ref[layer]
        query, outer = weight[:, :D], weight[:, 3 * D :]
        key_gain, value_gain = vector("key_gain", layer), vector("value_gain", layer)
        key_column = jnp.sum(eye * key_gain, 1, keepdims=True)
        key_total = jnp.zeros((D, 1), F32)
        value_total = jnp.zeros((1, D), F32)
        query_grad = jnp.zeros((D, D), F32)
        outer_grad = jnp.zeros((D, D), F32)
        for s in range(count):
            plain, summary, mixed = small_keep[layer, s, 0], small_keep[layer, s, 1], small_keep[layer, s, 2]
            turned = exact(query, products[s], 0, 0)
            outer_grad += exact(summary, turned, 0, 0)
            if layer:
                query_grad += exact(products[s], mixed, 1, 1)
            cot = jnp.where(blocks, exact(turned, outer, 1, 1), 0.0)
            both = cot * plain
            key_total += jnp.sum(both * value_gain, 1, keepdims=True)
            value_total += jnp.sum(both * key_column, 0, keepdims=True)
            scaled = key_column * cot * value_gain * (1.0 / points)
            t_keep[s, 0] = even4_weight(scaled.T)
            t_keep[s, 1] = even4_weight(scaled)
        if layer:
            early[5 * D + FREQ : 6 * D + FREQ, :] = query_grad
            early[6 * D + FREQ : 7 * D + FREQ, :] = outer_grad
        else:
            late[6 * D : 7 * D, :] = outer_grad
        return jnp.sum(eye * key_total, 0, keepdims=True), value_total

    for i in range(2):
        half = slice(i * D, (i + 1) * D)
        early[i * D : (i + 1) * D, :] = w1_acc[:D, half] + w1_acc[D:, half]
        early[(2 + i) * D : (3 + i) * D, :] = w2_acc[1, :D, half] + w2_acc[1, D:, half]
    sums = p_acc[...]
    sums = fold(sums[: 2 * D] + sums[2 * D :])
    early[4 * D : 4 * D + FREQ, :] = (sums[:D, :FREQ] + sums[D:, FREQ:]).T
    squares = []
    for part in range(3):
        sums = quarters(sq_acc[part])
        squares.append((sums[:FREQ, :FREQ] + sums[FREQ:, FREQ:]).T)
    early[4 * D + FREQ : 5 * D, :] = beside(squares[0], squares[1])
    early[5 * D : 5 * D + FREQ, :] = beside(squares[2], jnp.zeros_like(squares[2]))
    early[7 * D + FREQ :, :] = jnp.zeros((D // 2, D), F32)
    gains = [None, None]
    gains[1] = attend_back(1, [quarters(s_acc[s]) for s in range(count)])

    def norm_back(s, normal, scale):
        key, value = normal[:, :D], normal[:, D:]
        key_cot = even4(halves(value), t_keep[s, 0])
        value_cot = even4(halves(key), t_keep[s, 1])
        mean = dot(beside(*halves(key_cot * key)), mean_weight) * (HEADS / D)
        return beside(scale[:, :D] * (key_cot - key * mean), scale[:, D:] * (value_cot - value * mean))

    early_route.start(0)

    def middle_back(index, _):
        @pl.when(index == 1)
        def _():
            mode_route.step(2)
            early_route.step(0)

        where = block(index)
        s = index // steps
        cot = norm_back(s, x_keep[where, :], r_keep[where, :])
        pieces = thirds(cot)
        high, low = pieces[:2]
        kept = h1_keep[where, :]
        kv_acc[...] += dot(kept, high, 0, 0)
        kv_acc[:D, :] += dot(kept[:, :D], low, 0, 0)
        out = d_keep[where, :]
        out = (
            out
            + even4(halves(out), nt_keep[s])
            + tall6(pieces, (w_kvt[:, : 2 * D], w_kvt[:, 2 * D :]))
        )
        outer, inner = feed_back(0, index, out)
        v_acc[s] += dot(lrows[index], beside(*outer[:2]))
        u_acc[s] += dot(lrows[index], beside(*inner[:2]))
        return 0

    lax.fori_loop(0, rows_all, middle_back, 0)
    mode_route.finish(3)
    put_mode.start()
    early_route.step(1)

    def lift_sum(value):
        value = fold(value)
        return above(
            value[0:1] + value[1:2] + value[2:3],
            value[3:4] + value[4:5] + value[5:6],
            value[6:7],
            jnp.zeros((5, value.shape[1]), F32),
        )

    inner_rows = [lift_sum(u_acc[s]) for s in range(count)]
    value_rows = [lift_sum(v_acc[s]) + exact(inner_rows[s], ffn_ref[0, 0], 1, 1) for s in range(count)]
    gains[0] = attend_back(0, [exact(lift_rows, value_rows[s], 0, 0) for s in range(count)])

    query_rows = jnp.zeros((8, D), F32)
    lift_part = jnp.zeros((8, D), F32)
    inner_grad = jnp.zeros((D, FF), F32)
    for s in range(count):
        query_rows += exact(value_rows[s], small_keep[0, s, 2], 1, 1)
        lift_part += value_rows[s] + exact(value_rows[s], n_keep[0, s], 1, 1)
        inner_grad += exact(mid_rows[s], inner_rows[s], 0, 0)
    for i in range(2):
        half = slice(i * D, (i + 1) * D)
        late[i * D : (i + 1) * D, :] = exact(kv_acc[:D, half] + kv_acc[D:, half], centre)
        late[(2 + i) * D : (3 + i) * D, :] = w2_acc[0, :D, half] + w2_acc[0, D:, half]
        late[(4 + i) * D : (5 + i) * D, :] = inner_grad[:, half]

    def bias(slot, width=D):
        return jnp.sum(b_acc[slot * 8 : slot * 8 + 8, :width], 0, keepdims=True)

    rows = [jnp.zeros((3, D), F32)]
    for layer in range(LAYERS):
        inner = bias(8 + 2 * layer, FF)
        rows += [gains[layer][0], gains[layer][1], inner[:, :D], inner[:, D:], bias(7 + 2 * layer)]
    short = [fold(bias(slot)) for slot in (6, 5, 4, 3, 2)]
    rows += [beside(short[0], short[1]), beside(short[2], short[3]), beside(short[4], jnp.zeros((1, FREQ), F32))]
    late[7 * D : 7 * D + 16, :] = above(*rows)
    lanes = lax.broadcasted_iota(jnp.int32, (1, D), 1)
    first = jnp.where(lax.rem(lanes, FREQ) == 0, bias(0), 0.0)
    second = jnp.where(lax.rem(lanes, FREQ) == 0, bias(1), 0.0)
    late[7 * D + 16 : 7 * D + 24, :] = above(first, second, jnp.zeros((6, D), F32))
    late[7 * D + 24 : 7 * D + 32, :] = query_rows
    late[7 * D + 32 : 7 * D + 40, :] = lift_part
    late[7 * D + 40 :, :] = jnp.zeros((D - 40, D), F32)
    late_route.start(0)

    def front_back(index, _):
        @pl.when(index == 1)
        def _():
            late_route.step(0)

        centred = dot(lifted[block(index), :], w0_kv[...])
        scale = head_scale(centred)
        cot = norm_back(index // steps, centred * scale, scale)
        vt_acc[...] += dot(lrows[index], beside(*halves(cot)))
        return 0

    lax.fori_loop(0, rows_all, front_back, 0)
    turned = lift_sum(vt_acc[...])
    tail_send[...] = above(turned[:4, :D], turned[:4, D:])
    swap = pltpu.make_async_remote_copy(
        src_ref=tail_send,
        dst_ref=tail_swap,
        send_sem=tail_sends.at[devices // 2 - 1],
        recv_sem=tail_recvs.at[devices // 2 - 1],
        device_id=device_of(x, 1 - core, z, y),
        device_id_type=MESH,
    )
    swap.start()
    late_route.step(1)
    swap.wait()
    tail_pair[...] = tail_send[...] + tail_swap[...]
    tail_land[place] = tail_pair[...]
    to_each(lambda r: tail_pair, tail_land, lambda r: r - 16 * core, mine, tail_sends, tail_recvs, False, True)
    early_route.step(2)
    early_route.finish(3)
    put_early.start()
    to_each(lambda r: tail_pair, tail_land, lambda r: r - 16 * core, mine, tail_sends, tail_recvs, False, False)
    late_route.step(2)
    late_route.finish(3)
    put_mode.wait()
    put_early.wait()
    summed = jnp.sum(tail_land[...], 0)
    zero = jnp.zeros((4, 2 * D), F32)
    turned = above(beside(summed[:4], summed[4:]), zero)
    joined = exact(lift_rows, turned, 0, 0)
    tail_out[:D, :] = exact(lift_rows, late_out[7 * D + 24 : 7 * D + 32, :], 0, 0)
    tail_out[D : 2 * D, :] = exact(joined[:, :D], centre)
    tail_out[2 * D : 3 * D, :] = exact(joined[:, D:], centre)
    tail_out[3 * D :, :] = late_out[7 * D + 32 : 7 * D + 40, :] + exact(turned, cent_keep[0], 1, 1)


def tables(points):
    order = np.arange(MODES)[:, None]
    angle = (order * np.arange(points)[None, :]) % points * (2.0 * math.pi / points)
    full = np.concatenate([np.cos(angle), np.sin(angle)], 0).astype(np.float32)
    kind = np.dtype(ml_dtypes.bfloat16)
    high = full.astype(kind)
    rest = full - high.astype(np.float32)
    middle = rest.astype(kind)
    low = (rest - middle.astype(np.float32)).astype(kind)
    zero = np.zeros((4 * MODES, points), kind)
    column = np.concatenate([high, middle, high, middle, high, low, zero], 0).T
    row = np.concatenate([high, middle], 0).reshape(4 * MODES, points // ROWS, ROWS).transpose(1, 0, 2)
    return np.ascontiguousarray(column), np.ascontiguousarray(row)


def summed_grads(samples_in, target, mask, attn_w, ffn_w, spec_w, turned_w, vectors):
    parts = samples_in.shape[0] // 2
    count, points = 2, samples_in.shape[2] * parts
    devices = FLAYERS * MODES
    total = count * points
    steps = points // ROWS
    column, row = tables(points)
    vmem = pl.BlockSpec(memory_space=pltpu.VMEM)
    anywhere = pl.BlockSpec(memory_space=pl.ANY)
    first = [
        ((parts, 8, samples_in.shape[2]), F32),
        ((parts, 8, samples_in.shape[2]), F32),
        ((NVEC_ROWS, D), F32),
        ((8 * D, D), F32),
        ((8 * D, D), F32),
        ((8 * D, D), F32),
        ((8 * D, D), F32),
        ((devices, 8, D), F32),
        ((devices, 8, D), F32),
        ((8, D), F32),
        ((8, D), F32),
        ((8, D), F32),
        ((devices // 2, 8, D), F32),
    ]
    numbers = (3 * devices, 3 * devices, parts - 1, parts - 1, devices - 1, devices - 1, devices // 2, devices // 2)
    scratch = [
        ((total, D), BF16),
        ((total // ROWS, 16, ROWS), BF16),
        ((6 * D, 2 * D), BF16),
        ((4 * D, 3 * D), BF16),
        ((6 * D, FF), BF16),
        ((2 * FF, 3 * D), BF16),
        ((count, D, FF), BF16),
        ((count, 8, D), F32),
        ((LAYERS, 2 * FF, 2 * D), BF16),
        ((LAYERS, 2 * FF, D), BF16),
        ((LAYERS, 6 * D, FF), BF16),
        ((total, 2 * D), F32),
        ((total, 2 * D), F32),
        ((LAYERS, total, FF), F32),
        ((LAYERS, total, 2 * FF), BF16),
        ((total, 2 * D), BF16),
        ((total, 2 * D), BF16),
        ((total, 3 * D), BF16),
        ((FLAYERS, points, 3 * D), BF16),
        ((points, 3 * D), BF16),
        ((count, 2 * D, 2 * D), F32),
        ((D, 2 * D), BF16),
        ((count, D, D), BF16),
        ((LAYERS, count, D, D), F32),
        ((LAYERS, count, 3, D, D), F32),
        ((count, 2 * D, 2 * D), BF16),
        ((LAYERS, D, 2 * D), F32),
        ((4 * MODES, 2 * D), F32),
        ((FLAYERS, 2 * count * MODES, D), F32),
        ((2 * D, D), BF16),
        ((3, 2 * D, 2 * D), F32),
        ((4 * D, 2 * D), F32),
        ((LAYERS, 2 * D, FF), F32),
        ((2 * D, FF), F32),
        ((2 * D, 2 * D), F32),
        ((count, 16, 2 * D), F32),
        ((count, 16, 2 * FF), F32),
        ((16, 4 * D), F32),
        ((96, FF), F32),
        ((total, D), F32),
        ((count, 2, 2 * D, 2 * D), BF16),
        ((count, 4 * D, 2 * D), BF16),
    ]
    shapes = [(8 * D, D), (8 * D, D), (devices * FREQ, D), (3 * D + 8, D)]
    return pl.pallas_call(
        step_kernel,
        out_shape=[jax.ShapeDtypeStruct(shape, F32) for shape in shapes],
        in_specs=[vmem] * 5 + [anywhere] + [vmem] * 2 + [anywhere] * 2,
        out_specs=[anywhere, vmem, anywhere, vmem],
        scratch_shapes=[
            pltpu.VMEM(spec_w.shape, F32),
            pltpu.VMEM(column.shape, BF16),
            pltpu.VMEM(row.shape, BF16),
            pltpu.VMEM(shapes[0], F32),
            pltpu.VMEM(shapes[2], F32),
            pltpu.SemaphoreType.DMA((5,)),
        ]
        + [pltpu.VMEM(*item) for item in first]
        + [pltpu.SemaphoreType.DMA((number,)) for number in numbers]
        + [pltpu.VMEM(*item) for item in scratch],
        compiler_params=pltpu.CompilerParams(
            vmem_limit_bytes=64 * 2**20 - 2**17, collective_id=0, has_side_effects=True
        ),
    )(
        samples_in,
        target,
        mask,
        attn_w,
        ffn_w,
        spec_w,
        turned_w,
        vectors,
        jnp.asarray(column),
        jnp.asarray(row),
    )


def update_kernel(
    early_any,
    late_any,
    modes_any,
    tail_any,
    vectors,
    vector_m,
    vector_v,
    attn_w,
    ffn_w,
    spec_w,
    turned_w,
    attn_m,
    ffn_m,
    spec_m,
    turned_m,
    attn_v,
    ffn_v,
    spec_v,
    turned_v,
    loss_out,
    count_out,
    weight_out,
    update_out,
    ratio_out,
    vector_m_out,
    vector_v_out,
    vector_w_out,
    vector_low_out,
    *rest,
):
    outs, scratch = rest[:16], rest[16:]
    ins = (attn_w, ffn_w, spec_w, turned_w, attn_m, ffn_m, spec_m, turned_m, attn_v, ffn_v, spec_v, turned_v)
    held, fresh = scratch[:12], scratch[12:28]
    flat, in_sems, out_sems, early, late, modes, tail, grad_sems = scratch[28:]

    blocks = [(2, 0), (2, 1), (1, 1), (1, 0), (0, 1), (0, 0), (3, None)]

    def view(ref, part):
        return ref if part is None else ref.at[part]

    def load(slot, kind):
        array, part = blocks[slot]
        number = kind * 4 + array
        return pltpu.make_async_copy(
            view(ins[number], part), view(held[number], part), in_sems.at[slot * 3 + kind]
        )

    def store(slot, kind):
        array, part = blocks[slot]
        number = kind * 4 + array
        return pltpu.make_async_copy(
            view(fresh[number], part), view(outs[number], part), out_sems.at[slot * 4 + kind]
        )

    grads = [
        pltpu.make_async_copy(source, target, grad_sems.at[i])
        for i, (source, target) in enumerate(
            ((late_any, late), (tail_any, tail), (modes_any, modes), (early_any, early))
        )
    ]
    for copy in grads[:3]:
        copy.start()
    for kind in range(3):
        load(0, kind).start()
    grads[3].start()
    for slot in range(1, len(blocks)):
        for kind in range(3):
            load(slot, kind).start()
    grads[0].wait()
    grads[1].wait()
    misc = late[7 * D + 16 : 7 * D + 24, :]
    loss_out[0] = jnp.sum(misc[0:1])
    valid = jnp.sum(misc[1:2], keepdims=True)
    count_out[0] = jnp.sum(misc[1:2])
    scale = 1.0 / valid

    def moved(weight, grad, first, second):
        first_new = BETA_ONE * first + (1.0 - BETA_ONE) * grad
        second_new = BETA_TWO * second + (1.0 - BETA_TWO) * grad * grad
        update = (
            first_new
            / (1.0 - BETA_ONE**STEP)
            / (jnp.sqrt(second_new / (1.0 - BETA_TWO**STEP)) + ADAM_EPS)
            + DECAY * weight
        )
        return first_new, second_new, update

    def note(slot, weight_sum, update_sum):
        weight_norm, update_norm = jnp.sqrt(weight_sum), jnp.sqrt(update_sum)
        ratio = weight_norm / (update_norm + ADAM_EPS)
        weight_out[slot] = weight_norm[0, 0]
        update_out[slot] = update_norm[0, 0]
        ratio_out[slot] = ratio[0, 0]
        return RATE * ratio

    def total(sums):
        return sum(jnp.sum(value, keepdims=True) for value in sums.values())

    for i in range(NVEC_ROWS):
        start = i * D
        size = min(D, flat.shape[0] - start)
        row = tail[3 * D + i : 3 * D + i + 1, :] if i < 3 else late[7 * D + i : 7 * D + i + 1, :]
        flat[start : start + size] = (row * scale)[:, :size].reshape(size)
    weight = vectors[...]
    first_new, second_new, update = moved(weight, flat[...], vector_m[...], vector_v[...])
    vector_m_out[...] = first_new
    vector_v_out[...] = second_new
    rate = note(
        7,
        jnp.sum(weight * weight).reshape(1, 1),
        jnp.sum(update * update).reshape(1, 1),
    )
    flat[...] = jnp.broadcast_to(rate, (1, D)).reshape(D)[0] * update
    weight = weight - flat[...]
    vector_w_out[...] = weight
    vector_low_out[...] = weight.astype(BF16)

    def grad_blocks(array, part):
        if array == 0:
            if part:
                places = [(early, 5 * D + FREQ), (late, 0), (late, D), (early, 6 * D + FREQ)]
            else:
                places = [(tail, 0), (tail, D), (tail, 2 * D), (late, 6 * D)]
            return [
                (ref, start, D, 0, (slice(None), slice(j * D, (j + 1) * D)))
                for j, (ref, start) in enumerate(places)
            ]
        if array == 1:
            ref, starts = (early, (0, 1, 2, 3)) if part else (late, (4, 5, 2, 3))
            return [
                (ref, starts[j] * D, D, 0, (j // 2, slice(None), slice(j % 2 * D, j % 2 * D + D)))
                for j in range(4)
            ]
        if array == 3:
            return [
                (early, 4 * D, FREQ, 0, (slice(None), slice(0, D))),
                (early, 4 * D + FREQ, FREQ, 0, (slice(None), slice(D, 2 * D))),
                (early, 5 * D, FREQ, 0, (slice(None), slice(2 * D, 2 * D + FREQ))),
            ]
        return [
            (modes, (part * MODES + k) * FREQ, FREQ, j * FREQ, (k, j))
            for k in range(MODES)
            for j in range(2)
        ]

    grads[2].wait()
    grads[3].wait()
    for slot, (array, part) in enumerate(blocks):
        for kind in range(3):
            load(slot, kind).wait()
        weight_ref, first_ref, second_ref = [view(held[kind * 4 + array], part) for kind in range(3)]
        first_out, second_out, weight_new, low_out = [view(fresh[kind * 4 + array], part) for kind in range(4)]
        pieces = grad_blocks(array, part)
        weight_sums, update_sums = {}, {}
        for ref, start, rows, lane, where in pieces:
            weight = weight_ref[where]
            width = weight.shape[1]
            grad = ref[start : start + rows, lane : lane + width] * scale
            first_new, second_new, update = moved(weight, grad, first_ref[where], second_ref[where])
            first_out[where] = first_new
            second_out[where] = second_new
            weight_new[where] = update
            weight_sums[width] = weight_sums.get(width, 0.0) + column_sum(weight * weight)
            update_sums[width] = update_sums.get(width, 0.0) + column_sum(update * update)
        store(slot, 0).start()
        store(slot, 1).start()
        place = (0 + part if array == 0 else 2 + part if array == 1 else 4 + part) if part is not None else 6
        rate = note(place, total(weight_sums), total(update_sums))
        for ref, start, rows, lane, where in pieces:
            weight = weight_ref[where] - rate * weight_new[where]
            weight_new[where] = weight
            low_out[where] = weight.astype(BF16)
        store(slot, 2).start()
        store(slot, 3).start()
    for slot in range(len(blocks)):
        for kind in range(4):
            store(slot, kind).wait()


def fast_body(samples_in, target, mask, attn_w, ffn_w, spec_w, dense_w, vectors, *moments):
    flat_spec = spec_w.reshape(FLAYERS, MODES * 2 * FREQ, FREQ)
    grads = summed_grads(samples_in, target, mask, attn_w, ffn_w, flat_spec, dense_w.T, vectors)
    sets = [
        (attn_w, ffn_w, spec_w, dense_w.T),
        (moments[0], moments[1], moments[2], moments[3].T),
        (moments[5], moments[6], moments[7], moments[8].T),
    ]
    vmem = pl.BlockSpec(memory_space=pltpu.VMEM)
    smem = pl.BlockSpec(memory_space=pltpu.SMEM)
    anywhere = pl.BlockSpec(memory_space=pl.ANY)
    shapes = [item.shape for item in sets[0]]
    kinds = (F32, F32, F32, BF16)
    scalar = [jax.ShapeDtypeStruct((1,), F32)] * 2 + [jax.ShapeDtypeStruct((8,), F32)] * 3
    line = [jax.ShapeDtypeStruct(vectors.shape, kind) for kind in kinds]
    arrays = [jax.ShapeDtypeStruct(shape, kind) for kind in kinds for shape in shapes]
    out = pl.pallas_call(
        update_kernel,
        out_shape=scalar + line + arrays,
        in_specs=[anywhere] * 4 + [vmem] * 3 + [anywhere] * 12,
        out_specs=[smem] * 5 + [vmem] * 4 + [anywhere] * 16,
        scratch_shapes=[pltpu.VMEM(shape, F32) for _ in range(3) for shape in shapes]
        + [pltpu.VMEM(shape, kind) for kind in kinds for shape in shapes]
        + [pltpu.VMEM(vectors.shape, F32), pltpu.SemaphoreType.DMA((21,)), pltpu.SemaphoreType.DMA((28,))]
        + [pltpu.VMEM(grad.shape, F32) for grad in grads]
        + [pltpu.SemaphoreType.DMA((4,))],
        compiler_params=pltpu.CompilerParams(vmem_limit_bytes=60 * 2**20),
    )(*grads, vectors, moments[4], moments[9], *sets[0], *sets[1], *sets[2])
    loss_sum, valid_count, weight_norms, update_norms, ratios = out[:5]
    line, arrays = out[5:9], out[9:]
    results = [loss_sum.reshape(()), valid_count.reshape(())]
    for array in range(4):
        for kind in range(4):
            item = arrays[kind * 4 + array]
            results.append(item.T if array == 3 else item)
    return tuple(results + list(line) + [weight_norms, update_norms, ratios])


def choose_body(*arrays):
    samples_in = arrays[0]
    dp, parts = lax.axis_size("dp"), lax.axis_size("pts")
    fits = dp * parts == FLAYERS * MODES and dp == 4 and samples_in.shape[0] == 2 * parts
    return (fast_body if fits and samples_in.shape[2] * parts % WIDE == 0 else body)(*arrays)


def solution(mesh):
    placed = (
        P("dp", None, "pts"),
        P("dp", "pts"),
        P("dp", "pts"),
        P(),
        P(),
        P(),
        P(),
        P(),
        P(),
        P(),
        P(),
        P(),
        P(),
        P(),
        P(),
        P(),
        P(),
        P(),
    )
    return jax.shard_map(
        choose_body,
        mesh=mesh,
        in_specs=placed,
        out_specs=(
            P(),
            P(),
            P(),
            P(),
            P(),
            P(),
            P(),
            P(),
            P(),
            P(),
            P(),
            P(),
            P(),
            P(),
            P(),
            P(),
            P(),
            P(),
            P(),
            P(),
            P(),
            P(),
            P(),
            P(),
            P(),
        ),
        check_vma=False,
    )
```

```python
import math

import jax
import jax.numpy as jnp
import ml_dtypes
import numpy as np
from jax import lax
from jax.experimental import pallas as pl
from jax.experimental.pallas import tpu as pltpu
from jax.sharding import PartitionSpec as P

D = 128
HEADS = 4
FF = 256
FREQ = 64
MODES = 16
LAYERS = 2
FLAYERS = 2
STEP = 5


HIGH = lax.Precision.HIGHEST
NORM_EPS = 1e-05
BETA_ONE = 0.5
BETA_TWO = 0.5
RATE = 0.2
DECAY = 0.01
ADAM_EPS = 1e-06


def vector_table():
    entries = [("lift_value", 0, D), ("lift_coord", 0, D), ("lift_bias", 0, D)]
    for layer in range(LAYERS):
        entries = entries + [
            ("key_gain", layer, D),
            ("value_gain", layer, D),
            ("inner_bias", layer, FF),
            ("outer_bias", layer, D),
        ]
    entries = entries + [("proj_bias", 0, FREQ)]
    for layer in range(FLAYERS):
        entries = entries + [("fourier_bias", layer, FREQ)]
    entries = entries + [("head_bias", 0, FREQ), ("head_out", 0, FREQ)]
    offsets = {}
    start = 0
    for label, layer, length in entries:
        offsets[label, layer] = (start, length)
        start = start + length
    return offsets


def pick(vectors, label, layer):
    start, length = vector_table()[label, layer]
    return vectors[start : start + length]


def head_norm(values, gain):
    centred = values - jnp.mean(values, -1, keepdims=True)
    scaled = centred * lax.rsqrt(jnp.mean(centred * centred, -1, keepdims=True) + NORM_EPS)
    return scaled * gain.reshape(HEADS, D // HEADS)


def lift(params, inputs):
    vectors = params[4]
    value = inputs[..., 0, :, None]
    coord = inputs[..., 1, :, None]
    return (
        value * pick(vectors, "lift_value", 0)
        + coord * pick(vectors, "lift_coord", 0)
        + pick(vectors, "lift_bias", 0)
    )


def attn_front(params, rows, layer, points):
    weight = params[0][layer]
    vectors = params[4]
    mixed = jnp.einsum("...d,de->...e", rows, weight[:, : 3 * D], precision=HIGH)
    shape = rows.shape[:-1] + (HEADS, D // HEADS)
    query = mixed[..., :D].reshape(shape)
    keys = head_norm(mixed[..., D : 2 * D].reshape(shape), pick(vectors, "key_gain", layer))
    values = head_norm(mixed[..., 2 * D :].reshape(shape), pick(vectors, "value_gain", layer))
    partial_sum = jnp.einsum("...phe,...phf->...hef", keys, values, precision=HIGH) / points
    return (query, partial_sum)


def attn_rear(params, rows, query, summary, layer):
    weight = params[0][layer]
    attended = jnp.einsum("...phe,...hef->...phf", query, summary, precision=HIGH).reshape(
        rows.shape
    )
    return rows + jnp.einsum("...d,de->...e", attended, weight[:, 3 * D :], precision=HIGH)


def ffn_block(params, rows, layer):
    weight = params[1][layer]
    vectors = params[4]
    inner = jnp.einsum("...d,df->...f", rows, weight[0], precision=HIGH) + pick(
        vectors, "inner_bias", layer
    )
    outer = jnp.einsum("...f,df->...d", jax.nn.gelu(inner), weight[1], precision=HIGH)
    return rows + outer + pick(vectors, "outer_bias", layer)


def project(params, rows):
    return jnp.einsum("...d,df->...f", rows, params[3][:D], precision=HIGH) + pick(
        params[4], "proj_bias", 0
    )


def mode_table(count, total):
    position = jnp.arange(count, dtype=jnp.int32)
    orders = jnp.arange(MODES, dtype=jnp.int32)
    phase = orders[:, None] * position[None, :] % total
    angle = phase.astype(jnp.float32) * (2.0 * math.pi / total)
    return jnp.concatenate([jnp.cos(angle), jnp.sin(angle)], 0)


def spectral_mix(coef, spec, first, width):
    columns = lax.dynamic_slice_in_dim(spec, first, width, 3)
    cosine = coef[..., :MODES, :]
    sine = coef[..., MODES:, :]
    real_part = columns[:, 0]
    imag_part = columns[:, 1]
    mixed_cos = jnp.einsum("...mf,mfg->...mg", cosine, real_part, precision=HIGH) + jnp.einsum(
        "...mf,mfg->...mg", sine, imag_part, precision=HIGH
    )
    mixed_sin = jnp.einsum("...mf,mfg->...mg", sine, real_part, precision=HIGH) - jnp.einsum(
        "...mf,mfg->...mg", cosine, imag_part, precision=HIGH
    )
    return jnp.concatenate([mixed_cos, mixed_sin], -2)


def fourier_end(params, back, rows, layer):
    local = params[3][D + layer * FREQ : D + (layer + 1) * FREQ]
    inner = back + jnp.einsum("...f,fg->...g", rows, local, precision=HIGH)
    return jax.nn.gelu(inner + pick(params[4], "fourier_bias", layer))


def head_loss(params, rows, target, mask_f):
    start = D + FLAYERS * FREQ
    hidden = jax.nn.gelu(
        jnp.einsum("...f,fg->...g", rows, params[3][start : start + FREQ], precision=HIGH)
        + pick(params[4], "head_bias", 0)
    )
    pred = jnp.einsum("...f,f->...", hidden, pick(params[4], "head_out", 0), precision=HIGH)
    diff = pred - target
    return jnp.sum(mask_f * diff * diff)


def add_all(first, second):
    return jax.tree.map(jnp.add, first, second)


def spectral_setup(points, parts):
    width = FREQ // parts
    return (mode_table(points, points), lax.axis_index("pts") * width, width, points)


def fourier_mix(spec, field, setup):
    grid, column, width, points = setup
    channel_rows = lax.all_to_all(field, "pts", split_axis=2, concat_axis=1, tiled=True)
    own_coef = jnp.einsum("kp,spc->skc", grid, channel_rows, precision=HIGH) / math.sqrt(points)
    full = lax.all_gather(own_coef, "pts", axis=2, tiled=True)
    mixed = spectral_mix(full, spec, column, width)
    spread = jnp.einsum("kp,skc->spc", grid, mixed, precision=HIGH) / math.sqrt(MODES)
    back = lax.all_to_all(spread, "pts", split_axis=1, concat_axis=2, tiled=True)
    return (back, full)


def fourier_back(params, grad_out, kept_item, layer, setup):
    field, full, back = kept_item
    grid, column, width, points = setup
    _, end_pull = jax.vjp(
        lambda weights, spread, inner: fourier_end(weights, spread, inner, layer),
        params,
        back,
        field,
    )
    grads, grad_back, grad_field = end_pull(grad_out)
    _, mix_pull = jax.vjp(
        lambda coef, weight: spectral_mix(coef, weight, column, width), full, params[2][layer]
    )
    grad_rows = lax.all_to_all(grad_back, "pts", split_axis=2, concat_axis=1, tiled=True)
    grad_mixed = jnp.einsum("kp,spc->skc", grid, grad_rows, precision=HIGH) / math.sqrt(MODES)
    grad_full, grad_spec = mix_pull(grad_mixed)
    grad_coef = lax.psum_scatter(grad_full, "pts", scatter_dimension=2, tiled=True)
    grad_chan = jnp.einsum("kp,skc->spc", grid, grad_coef, precision=HIGH) / math.sqrt(points)
    grad_field = grad_field + lax.all_to_all(
        grad_chan, "pts", split_axis=1, concat_axis=2, tiled=True
    )
    grads = (grads[0], grads[1], grads[2].at[layer].add(grad_spec), grads[3], grads[4])
    return (grads, grad_field)


def attention_back(params, grad_rows, kept_item, layer, points):
    rows, summary = kept_item
    (query, partial_sum), front_pull = jax.vjp(
        lambda weights, inner: attn_front(weights, inner, layer, points), params, rows
    )
    summary = lax.psum(partial_sum, "pts")
    middle, rear_pull = jax.vjp(
        lambda weights, inner, asked, summed: attn_rear(weights, inner, asked, summed, layer),
        params,
        rows,
        query,
        summary,
    )
    _, ffn_pull = jax.vjp(lambda weights, inner: ffn_block(weights, inner, layer), params, middle)
    ffn_grads, grad_middle = ffn_pull(grad_rows)
    rear_grads, grad_direct, grad_query, grad_summary = rear_pull(grad_middle)
    grad_summary = lax.psum(grad_summary, "pts")
    front_grads, grad_front = front_pull((grad_query, grad_summary))
    return (add_all(add_all(ffn_grads, rear_grads), front_grads), grad_direct + grad_front)


def lamb(weight, grad, first, second):
    first_new = BETA_ONE * first + (1.0 - BETA_ONE) * grad
    second_new = BETA_TWO * second + (1.0 - BETA_TWO) * grad * grad
    update = (
        first_new
        / (1.0 - BETA_ONE**STEP)
        / (jnp.sqrt(second_new / (1.0 - BETA_TWO**STEP)) + ADAM_EPS)
        + DECAY * weight
    )
    return (first_new, second_new, update)


def trust_step(weight, update, stacked):
    axes = tuple(range(1, weight.ndim)) if stacked else tuple(range(weight.ndim))
    weight_norm = jnp.sqrt(jnp.sum(weight * weight, axes))
    update_norm = jnp.sqrt(jnp.sum(update * update, axes))
    ratio = weight_norm / (update_norm + ADAM_EPS)
    scale = ratio.reshape(ratio.shape + (1,) * (weight.ndim - ratio.ndim))
    return (
        weight - RATE * scale * update,
        jnp.atleast_1d(weight_norm),
        jnp.atleast_1d(update_norm),
        jnp.atleast_1d(ratio),
    )


def finish(loss_sum, valid_count, params, grads, firsts, seconds):
    results = [loss_sum, valid_count]
    weight_norms, update_norms, ratios = ([], [], [])
    for weight, grad, first, second, stacked in zip(
        params, grads, firsts, seconds, (True, True, True, False, False)
    ):
        first_new, second_new, update = lamb(weight, grad, first, second)
        fresh, weight_norm, update_norm, ratio = trust_step(weight, update, stacked)
        results = results + [first_new, second_new, fresh, fresh.astype(jnp.bfloat16)]
        weight_norms.append(weight_norm)
        update_norms.append(update_norm)
        ratios.append(ratio)
    return results + [
        jnp.concatenate(weight_norms),
        jnp.concatenate(update_norms),
        jnp.concatenate(ratios),
    ]


def body(
    samples_in,
    target,
    mask,
    attn_w,
    ffn_w,
    spec_w,
    dense_w,
    vectors,
    attn_m,
    ffn_m,
    spec_m,
    dense_m,
    vector_m,
    attn_v,
    ffn_v,
    spec_v,
    dense_v,
    vector_v,
):
    params = (attn_w, ffn_w, spec_w, dense_w, vectors)
    parts = lax.axis_size("pts")
    local_pts = samples_in.shape[2]
    points = local_pts * parts
    mask_f = mask.astype(jnp.float32)
    valid_count = lax.psum(jnp.sum(mask_f), ("dp", "pts"))
    setup = spectral_setup(points, parts)
    rows, lift_pull = jax.vjp(lambda weights: lift(weights, samples_in), params)
    kept = []
    for layer in range(LAYERS):
        query, partial_sum = attn_front(params, rows, layer, points)
        summary = lax.psum(partial_sum, "pts")
        kept.append((rows, summary))
        rows = ffn_block(params, attn_rear(params, rows, query, summary, layer), layer)
    field, proj_pull = jax.vjp(project, params, rows)
    spectral_kept = []
    for layer in range(FLAYERS):
        back, full = fourier_mix(params[2][layer], field, setup)
        spectral_kept.append((field, full, back))
        field = fourier_end(params, back, field, layer)
    loss_part, head_pull = jax.vjp(
        lambda weights, inner: head_loss(weights, inner, target, mask_f), params, field
    )
    grads, grad_field = head_pull(1.0 / valid_count)
    for layer in reversed(range(FLAYERS)):
        layer_grads, grad_field = fourier_back(
            params, grad_field, spectral_kept[layer], layer, setup
        )
        grads = add_all(grads, layer_grads)
    proj_grads, grad_rows = proj_pull(grad_field)
    grads = add_all(grads, proj_grads)
    for layer in reversed(range(LAYERS)):
        layer_grads, grad_rows = attention_back(params, grad_rows, kept[layer], layer, points)
        grads = add_all(grads, layer_grads)
    grads = add_all(grads, lift_pull(grad_rows)[0])
    summed = lax.psum((grads[0], grads[1], grads[2], grads[3], grads[4], loss_part), ("dp", "pts"))
    out = finish(
        summed[5],
        valid_count,
        params,
        summed[:5],
        (attn_m, ffn_m, spec_m, dense_m, vector_m),
        (attn_v, ffn_v, spec_v, dense_v, vector_v),
    )
    return (
        out[0],
        out[1],
        out[2],
        out[3],
        out[4],
        out[5],
        out[6],
        out[7],
        out[8],
        out[9],
        out[10],
        out[11],
        out[12],
        out[13],
        out[14],
        out[15],
        out[16],
        out[17],
        out[18],
        out[19],
        out[20],
        out[21],
        out[22],
        out[23],
        out[24],
    )


F32 = jnp.float32
BF16 = jnp.bfloat16
ROWS = 1024
WIDE = 2048
NVEC_ROWS = 16


def dot(first, second, left=1, right=0, precision=None):
    return lax.dot_general(
        first,
        second,
        (((left,), (right,)), ((), ())),
        precision=precision,
        preferred_element_type=F32,
    )


def exact(first, second, left=1, right=0):
    return dot(first, second, left, right, HIGH)


def halves(value):
    high = value.astype(BF16)
    return high, (value - high.astype(F32)).astype(BF16)


def thirds(value):
    high = value.astype(BF16)
    rest = value - high.astype(F32)
    middle = rest.astype(BF16)
    return high, middle, (rest - middle.astype(F32)).astype(BF16)


def beside(*pieces):
    return jnp.concatenate(pieces, 1)


def above(*pieces):
    return jnp.concatenate(pieces, 0)


def fold(value):
    half = value.shape[1] // 2
    return value[:, :half] + value[:, half:]


def column_sum(value):
    rows, width = value.shape
    return jnp.sum(value.reshape(rows // 8, 8, width), 0)


def gelu_pair(inner):
    scale = math.sqrt(2.0 / math.pi)
    square = inner * inner
    bend = jnp.tanh(inner * (scale + (scale * 0.044715) * square))
    half = 0.5 + 0.5 * bend
    slope = half + (0.5 * inner) * (1.0 - bend * bend) * (scale + (3.0 * scale * 0.044715) * square)
    return inner * half, slope


def wide6_weight(weight):
    high, middle, low = thirds(weight)
    return above(high, high, middle, middle, low, high)


def wide6(pieces, weight):
    high, middle, low = pieces
    return dot(beside(high, middle, high, middle, high, low), weight)


def tall6_weight(weight):
    high, middle, low = thirds(weight)
    pair = beside(high, middle)
    return above(pair, pair), above(low, high)


def tall6(pieces, weights):
    high, middle, low = pieces
    return fold(dot(beside(high, middle), weights[0])) + dot(beside(high, low), weights[1])


def even4_weight(weight):
    high, low = halves(weight)
    pair = beside(high, low)
    return above(pair, pair)


def even4(pieces, weight):
    return fold(dot(beside(*pieces), weight))


def head_blocks(width):
    row = lax.broadcasted_iota(jnp.int32, (width, width), 0)
    column = lax.broadcasted_iota(jnp.int32, (width, width), 1)
    return row // (D // HEADS) == column // (D // HEADS)


def doubled(weight):
    zero = jnp.zeros_like(weight)
    return above(beside(weight, zero), beside(zero, weight))


MESH = pl.DeviceIdType.MESH


def position():
    dp, pts = lax.axis_index("dp"), lax.axis_index("pts")
    x, core, z, y = dp // 2, dp % 2, pts // 2, pts % 2
    return x, core, z, y


def device_of(x, core, z, y):
    return (2 * x + core, 2 * z + y)


def other(i):
    x, core, z, y = position()
    step = i + 1
    c = core + lax.div(step, 16) * (1 - 2 * core)
    x = x + lax.rem(lax.div(step, 8), 2) * (1 - 2 * x)
    y = y + lax.rem(lax.div(step, 4), 2) * (1 - 2 * y)
    z = lax.rem(z + lax.rem(step, 4), 4)
    return 16 * c + 8 * x + 4 * y + z, device_of(x, c, z, y)


def back_of(i):
    step = i + 1
    rest = lax.rem(step, 4)
    return step - rest + lax.rem(4 - rest, 4) - 1


def each_of(number, copy_of, start):
    def one(i, _):
        copy = copy_of(i)
        if start:
            copy.start()
        else:
            copy.wait()
        return 0

    lax.fori_loop(0, number, one, 0)


class Route:
    def __init__(self, rows, full, flat, landing, sends, receives, first):
        x, core, z, y = position()
        self.core, self.group = core, FLAYERS * MODES // 2
        self.rows, self.full, self.flat, self.landing = rows, full, flat, landing
        self.sends, self.receives, self.first = sends, receives, first
        self.peer = device_of(x, 1 - core, z, y)
        self.half, self.least = rows // 2, rows // (2 * self.group)
        self.own = (16 * core + 8 * x + 4 * y + z) * self.least

    def area(self, start, size):
        return pl.ds(pl.multiple_of(start, self.least), size)

    def link(self, source, target, slot, device):
        return pltpu.make_async_remote_copy(
            src_ref=source,
            dst_ref=target,
            send_sem=self.sends.at[self.first + slot],
            recv_sem=self.receives.at[self.first + slot],
            device_id=device,
            device_id_type=MESH,
        )

    def run(self, stage, start):
        half, least, core, group = self.half, self.least, self.core, self.group
        mine, yours = self.area(core * half, half), self.area((1 - core) * half, half)

        def copy_of(i):
            if stage == 0:
                return self.link(self.flat.at[yours], self.landing.at[pl.ds(0, half)], 2 * group - 1, self.peer)
            if stage == 3:
                return self.link(self.full.at[mine], self.full.at[mine if start else yours], 2 * group - 2, self.peer)
            number, device = other(i)
            if stage == 1:
                source = self.flat.at[self.area(number * least, least)]
                target = self.landing.at[self.area(half + i * least, least)]
            else:
                start_row = self.own if start else other(back_of(i))[0] * least
                source = self.full.at[self.area(self.own, least)]
                target = self.full.at[self.area(start_row, least)]
            return self.link(source, target, (stage - 1) * (group - 1) + i, device)

        if stage in (1, 2):
            each_of(group - 1, copy_of, start)
        elif start:
            copy_of(0).start()
        else:
            copy_of(0).wait()

    def start(self, stage):
        if stage == 2 and self.flat is not None:
            self.full[self.area(self.own, self.least), :] = self.flat[self.area(self.own, self.least), :]
        self.run(stage, True)

    def finish(self, stage):
        self.run(stage, False)
        if stage == 0:
            self.flat[self.area(self.core * self.half, self.half), :] += self.landing[: self.half, :]
        if stage == 1:
            mine = self.area(self.own, self.least)
            total = self.flat[mine, :]
            for i in range(self.group - 1):
                start = self.half + i * self.least
                total = total + self.landing[start : start + self.least, :]
            self.flat[mine, :] = total

    def step(self, stage):
        self.finish(stage)
        self.start(stage + 1)


def to_each(source_of, target, slot_of, mine, sends, receives, number, start):
    def copy_of(i):
        to, device = other(i)
        return pltpu.make_async_remote_copy(
            src_ref=source_of(to),
            dst_ref=target.at[slot_of(mine if start else other(back_of(i))[0])],
            send_sem=sends.at[i],
            recv_sem=receives.at[i],
            device_id=device,
            device_id_type=MESH,
        )

    each_of(number, copy_of, start)


def step_kernel(
    samples_ref,
    target_ref,
    mask_ref,
    attn_ref,
    ffn_ref,
    spec_any,
    turned_ref,
    vectors_ref,
    table_any,
    trow_any,
    early_any,
    late_out,
    mode_any,
    tail_out,
    spec_ref,
    table_ref,
    trow_ref,
    early_out,
    mode_out,
    local_sems,
    outgoing,
    incoming,
    vec_ref,
    early,
    early_land,
    late,
    late_land,
    mode_send,
    mode_land,
    tail_send,
    tail_swap,
    tail_pair,
    tail_land,
    route_send,
    route_recv,
    point_send,
    point_recv,
    mode_sends,
    mode_recvs,
    tail_sends,
    tail_recvs,
    lifted,
    lrows,
    w_kv,
    w_kvt,
    w_in,
    w_int,
    w0_u,
    mid_rows,
    w_out0,
    w_out1,
    w_outt,
    x_keep,
    r_keep,
    slope_keep,
    act_keep,
    mid_keep,
    h1_keep,
    h2_keep,
    z_keep,
    e_keep,
    s_acc,
    w0_kv,
    w0_g,
    n_keep,
    small_keep,
    nt_keep,
    cent_keep,
    coef_acc,
    coef_keep,
    stack_ref,
    sq_acc,
    p_acc,
    w2_acc,
    w1_acc,
    kv_acc,
    v_acc,
    u_acc,
    vt_acc,
    b_acc,
    d_keep,
    t_keep,
    wz,
):
    parts = samples_ref.shape[0] // 2
    count = 2
    points = samples_ref.shape[2] * parts
    devices = FLAYERS * MODES
    x, core, z, y = position()
    pts = 2 * z + y
    place = 8 * x + 4 * y + z
    mine = 16 * core + place
    early_route = Route(early.shape[0], early_out, early, early_land, route_send, route_recv, 0)
    late_route = Route(late.shape[0], late_out, late, late_land, route_send, route_recv, devices)
    mode_route = Route(mode_out.shape[0], mode_out, None, None, route_send, route_recv, 2 * devices)

    barrier = pltpu.get_barrier_semaphore()
    take = [
        pltpu.make_async_copy(source, target, local_sems.at[i])
        for i, (source, target) in enumerate(((trow_any, trow_ref), (spec_any, spec_ref), (table_any, table_ref)))
    ]
    put_mode = pltpu.make_async_copy(mode_out, mode_any, local_sems.at[3])
    put_early = pltpu.make_async_copy(early_out, early_any, local_sems.at[4])
    for copy in take:
        copy.start()

    def greet(i, _):
        pl.semaphore_signal(barrier, inc=1, device_id=other(i)[1], device_id_type=MESH)
        return 0

    lax.fori_loop(0, devices - 1, greet, 0)
    for p in range(parts):
        outgoing[p, 0:2, :] = samples_ref[2 * p]
        outgoing[p, 2:4, :] = samples_ref[2 * p + 1]
        outgoing[p, 4:6, :] = target_ref[2 * p : 2 * p + 2, :]
        outgoing[p, 6:8, :] = mask_ref[2 * p : 2 * p + 2, :].astype(F32)
    incoming[pts] = outgoing[pts]
    for i in range(NVEC_ROWS - 1):
        vec_ref[i : i + 1, :] = vectors_ref[i * D : (i + 1) * D].reshape(1, D)
    last = vectors_ref.shape[0] - (NVEC_ROWS - 1) * D
    vec_ref[NVEC_ROWS - 1 :, :last] = vectors_ref[(NVEC_ROWS - 1) * D :].reshape(1, last)
    total = count * points
    steps = points // ROWS
    rows_all = total // ROWS
    blocks = head_blocks(D)
    block_f = jnp.where(blocks, 1.0, 0.0).astype(F32)
    block_b = block_f.astype(BF16)
    mean_weight = above(block_b, block_b)
    centre = (
        jnp.where(
            lax.broadcasted_iota(jnp.int32, (D, D), 0) == lax.broadcasted_iota(jnp.int32, (D, D), 1),
            1.0,
            0.0,
        ).astype(F32)
        - block_f * (HEADS / D)
    )
    eye = jnp.where(
        lax.broadcasted_iota(jnp.int32, (D, D), 0) == lax.broadcasted_iota(jnp.int32, (D, D), 1), 1.0, 0.0
    ).astype(F32)

    def vector(label, layer):
        start, length = vector_table()[label, layer]
        if length == 2 * D:
            row = start // D
            return beside(vec_ref[row : row + 1, :], vec_ref[row + 1 : row + 2, :])
        row = start // D
        if length == D:
            return vec_ref[row : row + 1, :]
        offset = start - row * D
        piece = vec_ref[row : row + 1, offset : offset + FREQ]
        return beside(piece, piece)

    def block(index):
        return pl.ds(pl.multiple_of(index * ROWS, ROWS), ROWS)

    wide_steps = points // WIDE

    def wide_block(index):
        return pl.ds(pl.multiple_of(index * WIDE, WIDE), WIDE)

    lift_rows = above(
        vector("lift_value", 0), vector("lift_coord", 0), vector("lift_bias", 0), jnp.zeros((5, D), F32)
    )

    def lift_weight(mixed):
        high, middle, low = [item.astype(F32) for item in thirds(mixed)]
        parts = []
        for i in range(2):
            hi, mi, lo = high[i : i + 1], middle[i : i + 1], low[i : i + 1]
            parts += [hi, hi, mi, mi, lo, hi]
        parts += [high[2:3], middle[2:3], low[2:3]]
        parts.append(jnp.zeros((D - 15, mixed.shape[1]), F32))
        return above(*parts).astype(BF16)

    def point_copy(k, start):
        other = lax.rem(pts + k, parts)
        sender = lax.rem(pts + parts - k, parts)
        return pltpu.make_async_remote_copy(
            src_ref=outgoing.at[other],
            dst_ref=incoming.at[pts if start else sender],
            send_sem=point_send.at[k - 1],
            recv_sem=point_recv.at[k - 1],
            device_id=(2 * x + core, other),
            device_id_type=MESH,
        )

    for layer in range(LAYERS):
        if layer == 1:
            pl.semaphore_wait(barrier, devices - 1)
            for k in range(1, parts):
                point_copy(k, True).start()
        weight = attn_ref[layer]
        keyed = beside(exact(weight[:, D : 2 * D], centre), exact(weight[:, 2 * D : 3 * D], centre))
        cent_keep[layer] = keyed
        if layer == 0:
            w0_kv[...] = lift_weight(exact(lift_rows, keyed))
        else:
            w_kv[...] = wide6_weight(keyed)
            pair, rest = tall6_weight(keyed.T)
            w_kvt[:, : 2 * D] = pair
            w_kvt[:, 2 * D :] = rest
        first, second = ffn_ref[layer, 0], ffn_ref[layer, 1]
        if layer:
            w_in[...] = wide6_weight(first)
            pair, rest = tall6_weight(first.T)
            w_int[:, : 2 * D] = pair
            w_int[:, 2 * D :] = rest
        pair, rest = tall6_weight(second.T)
        w_out0[layer] = pair
        w_out1[layer] = rest
        w_outt[layer] = wide6_weight(second)

    s_acc[...] = jnp.zeros_like(s_acc)
    coef_acc[...] = jnp.zeros_like(coef_acc)
    sq_acc[...] = jnp.zeros_like(sq_acc)
    p_acc[...] = jnp.zeros_like(p_acc)
    w2_acc[...] = jnp.zeros_like(w2_acc)
    w1_acc[...] = jnp.zeros_like(w1_acc)
    kv_acc[...] = jnp.zeros_like(kv_acc)
    v_acc[...] = jnp.zeros_like(v_acc)
    u_acc[...] = jnp.zeros_like(u_acc)
    vt_acc[...] = jnp.zeros_like(vt_acc)
    b_acc[...] = jnp.zeros_like(b_acc)

    for k in range(1, parts):
        point_copy(k, False).wait()
    whole = beside(*[incoming[p] for p in range(parts)])
    for s in range(count):
        value, coord = whole[2 * s : 2 * s + 1], whole[2 * s + 1 : 2 * s + 2]
        target, valid = whole[4 + s : 5 + s], whole[6 + s : 7 + s]
        one = jnp.ones_like(value)
        vh, vm, vl = [item.astype(F32) for item in thirds(value)]
        ch, cm, cl = [item.astype(F32) for item in thirds(coord)]
        th, tm, tl = [item.astype(F32) for item in thirds(target)]
        zero = jnp.zeros((D - 19, points), F32)
        stack = above(vh, vm, vh, vm, vh, vl, ch, cm, ch, cm, ch, cl, one, one, one, th, tm, tl, valid, zero)
        lifted[s * points : (s + 1) * points, :] = stack.T.astype(BF16)
        short = above(vh, vm, vl, ch, cm, cl, one, jnp.zeros((9, points), F32)).astype(BF16)
        for i in range(steps):
            lrows[s * steps + i] = short[:, i * ROWS : (i + 1) * ROWS]

    def head_scale(centred):
        high, low = halves(centred * centred)
        var = beside(
            dot(beside(high[:, :D], low[:, :D]), mean_weight), dot(beside(high[:, D:], low[:, D:]), mean_weight)
        )
        return lax.rsqrt(var * (HEADS / D) + NORM_EPS)

    def normalise(layer, where, s, centred):
        scale = head_scale(centred)
        normal = centred * scale
        if layer:
            x_keep[where, :] = normal
            r_keep[where, :] = scale
        high, low = halves(normal)
        s_acc[s] += dot(
            beside(high[:, :D], low[:, :D]), beside(high[:, D:], low[:, D:]), 0, 0
        )

    def quarters(value):
        half_row, half_col = value.shape[0] // 2, value.shape[1] // 2
        return (
            value[:half_row, :half_col]
            + value[half_row:, :half_col]
            + (value[:half_row, half_col:] + value[half_row:, half_col:])
        )

    def summarise(layer):
        weight = attn_ref[layer]
        key_gain = vector("key_gain", layer).reshape(1, D)
        value_gain = vector("value_gain", layer).reshape(1, D)
        key_column = jnp.sum(eye * key_gain, 1, keepdims=True)
        for s in range(count):
            plain = jnp.where(blocks, quarters(s_acc[s]), 0.0) * (1.0 / points)
            summary = key_column * plain * value_gain
            mixed = exact(summary, weight[:, 3 * D :])
            both = exact(weight[:, :D], mixed)
            n_keep[layer, s] = both
            small_keep[layer, s, 0] = plain
            small_keep[layer, s, 1] = summary
            small_keep[layer, s, 2] = mixed
            if layer == 0:
                rows = exact(lift_rows, eye + both)
                mid_rows[s] = rows
                w0_g[s] = lift_weight(rows)
                w0_u[s] = lift_weight(exact(rows, ffn_ref[0, 0]))
            else:
                pair, rest = tall6_weight(both)
                wz[s, : 2 * D, :] = pair
                wz[s, 2 * D :, :D] = rest
                nt_keep[s] = even4_weight(both.T)

    def feed(layer, index, mid, inner):
        where = block(index)
        act, slope = gelu_pair(inner + vector("inner_bias", layer))
        slope_keep[layer, where, :] = slope
        pieces = thirds(act)
        act_keep[layer, where, :] = beside(pieces[0], pieces[1])
        return mid + tall6(pieces, (w_out0[layer], w_out1[layer])) + vector("outer_bias", layer)

    def front_zero(index, _):
        where = wide_block(index)
        normalise(0, where, index // wide_steps, dot(lifted[where, :], w0_kv[...]))
        return 0

    lax.fori_loop(0, count * wide_steps, front_zero, 0)
    summarise(0)
    s_acc[...] = jnp.zeros_like(s_acc)

    def layer_zero(index, _):
        where = block(index)
        s = index // steps
        data = lifted[where, :]
        out = feed(0, index, dot(data, w0_g[s]), dot(data, w0_u[s]))
        d_keep[where, :] = out
        pieces = thirds(out)
        h1_keep[where, :] = beside(pieces[0], pieces[1])
        h2_keep[where, 2 * D :] = pieces[2]
        normalise(1, where, s, wide6(pieces, w_kv[...]))
        return 0

    lax.fori_loop(0, rows_all, layer_zero, 0)
    summarise(1)
    s_acc[...] = jnp.zeros_like(s_acc)

    def pieces_of(ref, where, number=3):
        value = ref[where, : number * D]
        return [value[:, i * D : (i + 1) * D] for i in range(number)]

    def layer_one(index, _):
        where = block(index)
        s = index // steps
        pieces = pieces_of(h1_keep, where, 2) + [h2_keep[where, 2 * D :]]
        mid = d_keep[where, :] + tall6(pieces, (wz[s, : 2 * D, :], wz[s, 2 * D :, :D]))
        pieces = thirds(mid)
        mid_keep[where, :] = beside(pieces[0], pieces[1])
        out = feed(1, index, mid, wide6(pieces, w_in[...]))
        h2_keep[where, :] = beside(*thirds(out))
        return 0

    lax.fori_loop(0, rows_all, layer_one, 0)

    def dense_rows(part):
        start = D + (part - 1) * FREQ if part else 0
        return turned_ref[:, start : start + (FREQ if part else D)].T

    proj0, proj1 = tall6_weight(doubled(dense_rows(0)))
    locals6 = [tall6_weight(doubled(dense_rows(part))) for part in (1, 2, 3)]
    turned6 = [tall6_weight(doubled(dense_rows(part).T)) for part in (1, 2, 3)]
    own = lax.broadcasted_iota(jnp.int32, (2 * count * MODES, MODES * D), 1) // D == lax.rem(
        lax.broadcasted_iota(jnp.int32, (2 * count * MODES, MODES * D), 0), MODES
    )

    def mode_rows(coef):
        cosine, sine = coef[:MODES], coef[MODES:]
        c = [cosine[:, s * FREQ : (s + 1) * FREQ] for s in range(count)]
        d = [sine[:, s * FREQ : (s + 1) * FREQ] for s in range(count)]
        return above(
            *[beside(c[s], d[s]) for s in range(count)], *[beside(d[s], -c[s]) for s in range(count)]
        )

    def spread_rows(rows):
        return jnp.where(own, beside(*([rows] * MODES)), 0.0)

    def unpack(rows):
        lead = count * MODES
        return above(
            *[beside(*[rows[j * lead + s * MODES : j * lead + (s + 1) * MODES] for s in range(count)]) for j in (0, 1)]
        )

    def pack(value):
        return above(
            *[
                value[j * MODES : (j + 1) * MODES, s * FREQ : (s + 1) * FREQ]
                for j in (0, 1)
                for s in range(count)
            ]
        )

    def set_stack(value):
        high, middle, low = thirds(value)
        stack_ref[...] = above(
            high, high, middle, middle, low, high, jnp.zeros((4 * MODES, D), BF16)
        )

    def take_coef(index, high, low):
        both = beside(high, low)
        each = both.shape[0] // ROWS
        for i in range(each):
            coef_acc[...] += dot(trow_ref[index * each + i], both[i * ROWS : (i + 1) * ROWS])

    def mix_forward(layer):
        coef = quarters(coef_acc[...]) * (1.0 / math.sqrt(points))
        coef_acc[...] = jnp.zeros_like(coef_acc)
        rows = mode_rows(coef)
        coef_keep[layer] = rows
        set_stack(unpack(exact(spread_rows(rows), spec_ref[layer])) * (1.0 / math.sqrt(MODES)))

    def mix_back(layer):
        cot = pack(quarters(coef_acc[...])) * (1.0 / math.sqrt(MODES))
        coef_acc[...] = jnp.zeros_like(coef_acc)
        kept_rows = coef_keep[layer]
        padded = beside(cot, jnp.zeros_like(cot))
        for k in range(MODES):
            for r in range(2 * count):
                mode_send[layer * MODES + k, r : r + 1, :] = kept_rows[r * MODES + k : r * MODES + k + 1]
                mode_send[layer * MODES + k, 4 + r : 5 + r, :] = padded[r * MODES + k : r * MODES + k + 1]
        wide = jnp.where(own, exact(cot, spec_ref[layer], 1, 1), 0.0)
        kept = wide[:, :D]
        for k in range(1, MODES):
            kept = kept + wide[:, k * D : (k + 1) * D]
        lead = count * MODES
        first, second = kept[:lead], kept[lead:]
        rows = above(first[:, :FREQ] - second[:, FREQ:], first[:, FREQ:] + second[:, :FREQ])
        set_stack(unpack(rows) * (1.0 / math.sqrt(points)))

    def project_step(index, _):
        where = wide_block(index)
        first = h2_keep[wide_block(index), :]
        second = h2_keep[wide_block(index + wide_steps), :]
        pieces = [beside(first[:, i * D : (i + 1) * D], second[:, i * D : (i + 1) * D]) for i in range(3)]
        field = tall6(pieces, (proj0, proj1)) + vector("proj_bias", 0)
        pieces = thirds(field)
        z_keep[0, where, :] = beside(*pieces)
        take_coef(index, pieces[0], pieces[1])
        return 0

    for copy in take:
        copy.wait()
    lax.fori_loop(0, wide_steps, project_step, 0)
    mix_forward(0)

    def fourier_field(layer, where):
        pieces = pieces_of(z_keep.at[layer], where)
        inner = dot(table_ref[where, :], stack_ref[...]) + (
            tall6(pieces, locals6[layer]) + vector("fourier_bias", layer)
        )
        return gelu_pair(inner)

    def fourier_one(index, _):
        where = wide_block(index)
        field, slope = fourier_field(0, where)
        d_keep[where, :] = slope
        pieces = thirds(field)
        z_keep[1, where, :] = beside(*pieces)
        take_coef(index, pieces[0], pieces[1])
        return 0

    lax.fori_loop(0, wide_steps, fourier_one, 0)
    mix_forward(1)

    lane = lax.broadcasted_iota(jnp.int32, (2 * D, 2 * D), 1)
    row = lax.broadcasted_iota(jnp.int32, (2 * D, 2 * D), 0)
    inner_row = lax.rem(row, D)
    same = row // D == lax.rem(lane, D) // FREQ
    pick_target = (lane < D) & (inner_row >= 15) & (inner_row < 18)
    pick_mask = (lane >= D) & (inner_row == 18)
    spread = jnp.where(same & (pick_target | pick_mask), 1.0, 0.0).astype(BF16)
    out_row = vector("head_out", 0)
    out_column = jnp.sum(eye * out_row, 1, keepdims=True)
    half_blocks = (
        lax.broadcasted_iota(jnp.int32, (D, D), 0) // FREQ == lax.broadcasted_iota(jnp.int32, (D, D), 1) // FREQ
    )
    out_weight = tall6_weight(jnp.where(half_blocks, out_column, 0.0))

    def pair_product(first, second):
        return dot(beside(*first), beside(*second), 0, 0)

    def loss_step(index, _):
        where = block(index)
        field, slope = fourier_field(1, where)
        pieces = thirds(field)
        hidden, hidden_slope = gelu_pair(tall6(pieces, locals6[2]) + vector("head_bias", 0))
        pred = tall6(thirds(hidden), out_weight)
        known = dot(beside(lifted[where, :], lifted[block(index + steps), :]), spread)
        diff = pred - known[:, :D]
        valid = known[:, D:]
        cot = (2.0 * valid) * diff
        b_acc[0:8, :D] += column_sum(valid * diff * diff)
        b_acc[8:16, :D] += column_sum(valid)
        b_acc[16:24, :D] += column_sum(hidden * cot)
        cot = cot * out_row * hidden_slope
        b_acc[24:32, :D] += column_sum(cot)
        split = thirds(cot)
        sq_acc[2] += pair_product(pieces[:2], split[:2])
        cot = tall6(split, turned6[2]) * slope
        b_acc[32:40, :D] += column_sum(cot)
        split = thirds(cot)
        e_keep[where, :] = beside(*split)
        sq_acc[1] += pair_product(pieces_of(z_keep.at[1], where, 2), split[:2])
        take_coef(index, *split[:2])
        return 0

    lax.fori_loop(0, steps, loss_step, 0)
    mix_back(1)

    def fourier_cot(layer, where):
        return tall6(pieces_of(e_keep, where), turned6[layer]) + dot(table_ref[where, :], stack_ref[...])

    def fourier_back(index, _):
        where = wide_block(index)
        cot = fourier_cot(1, where) * d_keep[where, :]
        b_acc[40:48, :D] += column_sum(cot)
        split = thirds(cot)
        e_keep[where, :] = beside(*split)
        sq_acc[0] += pair_product(pieces_of(z_keep.at[0], where, 2), split[:2])
        take_coef(index, *split[:2])
        return 0

    lax.fori_loop(0, wide_steps, fourier_back, 0)
    mix_back(0)
    mode_land[mine] = mode_send[mine]
    to_each(lambda r: mode_send.at[r], mode_land, lambda r: r, mine, mode_sends, mode_recvs, devices - 1, True)
    proj_back = wide6_weight(doubled(turned_ref[:, :D]))

    def project_back(index, _):
        where = wide_block(index)
        later = wide_block(index + wide_steps)
        cot = fourier_cot(0, where)
        b_acc[48:56, :D] += column_sum(cot)
        split = thirds(cot)
        first = pieces_of(h2_keep, where, 2)
        second = pieces_of(h2_keep, later, 2)
        p_acc[...] += dot(beside(first[0], second[0], first[1], second[1]), beside(*split[:2]), 0, 0)
        rows = wide6(split, proj_back)
        d_keep[where, :] = rows[:, :D]
        d_keep[later, :] = rows[:, D:]
        return 0

    lax.fori_loop(0, wide_steps, project_back, 0)

    def feed_back(layer, index, cot):
        where = block(index)
        base = 56 + layer * 16
        b_acc[base : base + 8, :D] += column_sum(cot)
        split = thirds(cot)
        act = act_keep[layer, where, :]
        w2_acc[layer] += dot(beside(*split[:2]), act[:, :FF], 0, 0)
        w2_acc[layer, :D, :] += dot(split[0], act[:, FF:], 0, 0)
        inner = wide6(split, w_outt[layer]) * slope_keep[layer, where, :]
        b_acc[base + 8 : base + 16, :] += column_sum(inner)
        return split, thirds(inner)

    def layer_one_back(index, _):
        @pl.when(index == 1)
        def _():
            to_each(lambda r: mode_send.at[r], mode_land, lambda r: r, mine, mode_sends, mode_recvs, devices - 1, False)
            landed = mode_land[...].reshape(devices * 8, D)
            shifted = above(landed[4:], landed[:4])
            row = lax.broadcasted_iota(jnp.int32, landed.shape, 0)
            product = exact(jnp.where(lax.rem(row, 8) < 4, landed, 0.0), shifted[:, :FREQ], 0, 0)
            mode_out[mode_route.area(mode_route.own, FREQ), :] = beside(product[:FREQ], product[FREQ:])
            mode_route.start(2)

        where = block(index)
        cot = d_keep[where, :]
        _, pieces = feed_back(1, index, cot)
        high, low = pieces[:2]
        mid = mid_keep[where, :]
        w1_acc[...] += dot(mid, high, 0, 0)
        w1_acc[:D, :] += dot(mid[:, :D], low, 0, 0)
        cot = cot + tall6(pieces, (w_int[:, : 2 * D], w_int[:, 2 * D :]))
        d_keep[where, :] = cot
        s_acc[index // steps] += pair_product(pieces_of(h1_keep, where, 2), halves(cot))
        return 0

    lax.fori_loop(0, rows_all, layer_one_back, 0)

    def attend_back(layer, products):
        weight = attn_ref[layer]
        query, outer = weight[:, :D], weight[:, 3 * D :]
        key_gain, value_gain = vector("key_gain", layer), vector("value_gain", layer)
        key_column = jnp.sum(eye * key_gain, 1, keepdims=True)
        key_total = jnp.zeros((D, 1), F32)
        value_total = jnp.zeros((1, D), F32)
        query_grad = jnp.zeros((D, D), F32)
        outer_grad = jnp.zeros((D, D), F32)
        for s in range(count):
            plain, summary, mixed = small_keep[layer, s, 0], small_keep[layer, s, 1], small_keep[layer, s, 2]
            turned = exact(query, products[s], 0, 0)
            outer_grad += exact(summary, turned, 0, 0)
            if layer:
                query_grad += exact(products[s], mixed, 1, 1)
            cot = jnp.where(blocks, exact(turned, outer, 1, 1), 0.0)
            both = cot * plain
            key_total += jnp.sum(both * value_gain, 1, keepdims=True)
            value_total += jnp.sum(both * key_column, 0, keepdims=True)
            scaled = key_column * cot * value_gain * (1.0 / points)
            t_keep[s, 0] = even4_weight(scaled.T)
            t_keep[s, 1] = even4_weight(scaled)
        if layer:
            early[5 * D + FREQ : 6 * D + FREQ, :] = query_grad
            early[6 * D + FREQ : 7 * D + FREQ, :] = outer_grad
        else:
            late[6 * D : 7 * D, :] = outer_grad
        return jnp.sum(eye * key_total, 0, keepdims=True), value_total

    for i in range(2):
        half = slice(i * D, (i + 1) * D)
        early[i * D : (i + 1) * D, :] = w1_acc[:D, half] + w1_acc[D:, half]
        early[(2 + i) * D : (3 + i) * D, :] = w2_acc[1, :D, half] + w2_acc[1, D:, half]
    sums = p_acc[...]
    sums = fold(sums[: 2 * D] + sums[2 * D :])
    early[4 * D : 4 * D + FREQ, :] = (sums[:D, :FREQ] + sums[D:, FREQ:]).T
    squares = []
    for part in range(3):
        sums = quarters(sq_acc[part])
        squares.append((sums[:FREQ, :FREQ] + sums[FREQ:, FREQ:]).T)
    early[4 * D + FREQ : 5 * D, :] = beside(squares[0], squares[1])
    early[5 * D : 5 * D + FREQ, :] = beside(squares[2], jnp.zeros_like(squares[2]))
    early[7 * D + FREQ :, :] = jnp.zeros((D // 2, D), F32)
    gains = [None, None]
    gains[1] = attend_back(1, [quarters(s_acc[s]) for s in range(count)])

    def norm_back(s, normal, scale):
        key, value = normal[:, :D], normal[:, D:]
        key_cot = even4(halves(value), t_keep[s, 0])
        value_cot = even4(halves(key), t_keep[s, 1])
        mean = dot(beside(*halves(key_cot * key)), mean_weight) * (HEADS / D)
        return beside(scale[:, :D] * (key_cot - key * mean), scale[:, D:] * (value_cot - value * mean))

    early_route.start(0)

    def middle_back(index, _):
        @pl.when(index == 1)
        def _():
            mode_route.step(2)
            early_route.step(0)

        where = block(index)
        s = index // steps
        cot = norm_back(s, x_keep[where, :], r_keep[where, :])
        pieces = thirds(cot)
        high, low = pieces[:2]
        kept = h1_keep[where, :]
        kv_acc[...] += dot(kept, high, 0, 0)
        kv_acc[:D, :] += dot(kept[:, :D], low, 0, 0)
        out = d_keep[where, :]
        out = (
            out
            + even4(halves(out), nt_keep[s])
            + tall6(pieces, (w_kvt[:, : 2 * D], w_kvt[:, 2 * D :]))
        )
        outer, inner = feed_back(0, index, out)
        v_acc[s] += dot(lrows[index], beside(*outer[:2]))
        u_acc[s] += dot(lrows[index], beside(*inner[:2]))
        return 0

    lax.fori_loop(0, rows_all, middle_back, 0)
    mode_route.finish(3)
    put_mode.start()
    early_route.step(1)

    def lift_sum(value):
        value = fold(value)
        return above(
            value[0:1] + value[1:2] + value[2:3],
            value[3:4] + value[4:5] + value[5:6],
            value[6:7],
            jnp.zeros((5, value.shape[1]), F32),
        )

    inner_rows = [lift_sum(u_acc[s]) for s in range(count)]
    value_rows = [lift_sum(v_acc[s]) + exact(inner_rows[s], ffn_ref[0, 0], 1, 1) for s in range(count)]
    gains[0] = attend_back(0, [exact(lift_rows, value_rows[s], 0, 0) for s in range(count)])

    query_rows = jnp.zeros((8, D), F32)
    lift_part = jnp.zeros((8, D), F32)
    inner_grad = jnp.zeros((D, FF), F32)
    for s in range(count):
        query_rows += exact(value_rows[s], small_keep[0, s, 2], 1, 1)
        lift_part += value_rows[s] + exact(value_rows[s], n_keep[0, s], 1, 1)
        inner_grad += exact(mid_rows[s], inner_rows[s], 0, 0)
    for i in range(2):
        half = slice(i * D, (i + 1) * D)
        late[i * D : (i + 1) * D, :] = exact(kv_acc[:D, half] + kv_acc[D:, half], centre)
        late[(2 + i) * D : (3 + i) * D, :] = w2_acc[0, :D, half] + w2_acc[0, D:, half]
        late[(4 + i) * D : (5 + i) * D, :] = inner_grad[:, half]

    def bias(slot, width=D):
        return jnp.sum(b_acc[slot * 8 : slot * 8 + 8, :width], 0, keepdims=True)

    rows = [jnp.zeros((3, D), F32)]
    for layer in range(LAYERS):
        inner = bias(8 + 2 * layer, FF)
        rows += [gains[layer][0], gains[layer][1], inner[:, :D], inner[:, D:], bias(7 + 2 * layer)]
    short = [fold(bias(slot)) for slot in (6, 5, 4, 3, 2)]
    rows += [beside(short[0], short[1]), beside(short[2], short[3]), beside(short[4], jnp.zeros((1, FREQ), F32))]
    late[7 * D : 7 * D + 16, :] = above(*rows)
    lanes = lax.broadcasted_iota(jnp.int32, (1, D), 1)
    first = jnp.where(lax.rem(lanes, FREQ) == 0, bias(0), 0.0)
    second = jnp.where(lax.rem(lanes, FREQ) == 0, bias(1), 0.0)
    late[7 * D + 16 : 7 * D + 24, :] = above(first, second, jnp.zeros((6, D), F32))
    late[7 * D + 24 : 7 * D + 32, :] = query_rows
    late[7 * D + 32 : 7 * D + 40, :] = lift_part
    late[7 * D + 40 :, :] = jnp.zeros((D - 40, D), F32)
    late_route.start(0)

    def front_back(index, _):
        @pl.when(index == 1)
        def _():
            late_route.step(0)

        centred = dot(lifted[block(index), :], w0_kv[...])
        scale = head_scale(centred)
        cot = norm_back(index // steps, centred * scale, scale)
        vt_acc[...] += dot(lrows[index], beside(*halves(cot)))
        return 0

    lax.fori_loop(0, rows_all, front_back, 0)
    turned = lift_sum(vt_acc[...])
    tail_send[...] = above(turned[:4, :D], turned[:4, D:])
    swap = pltpu.make_async_remote_copy(
        src_ref=tail_send,
        dst_ref=tail_swap,
        send_sem=tail_sends.at[devices // 2 - 1],
        recv_sem=tail_recvs.at[devices // 2 - 1],
        device_id=device_of(x, 1 - core, z, y),
        device_id_type=MESH,
    )
    swap.start()
    late_route.step(1)
    swap.wait()
    tail_pair[...] = tail_send[...] + tail_swap[...]
    tail_land[place] = tail_pair[...]
    to_each(lambda r: tail_pair, tail_land, lambda r: r - 16 * core, mine, tail_sends, tail_recvs, devices // 2 - 1, True)
    early_route.step(2)
    early_route.finish(3)
    put_early.start()
    to_each(lambda r: tail_pair, tail_land, lambda r: r - 16 * core, mine, tail_sends, tail_recvs, devices // 2 - 1, False)
    late_route.step(2)
    late_route.finish(3)
    put_mode.wait()
    put_early.wait()
    summed = jnp.sum(tail_land[...], 0)
    zero = jnp.zeros((4, 2 * D), F32)
    turned = above(beside(summed[:4], summed[4:]), zero)
    joined = exact(lift_rows, turned, 0, 0)
    tail_out[:D, :] = exact(lift_rows, late_out[7 * D + 24 : 7 * D + 32, :], 0, 0)
    tail_out[D : 2 * D, :] = exact(joined[:, :D], centre)
    tail_out[2 * D : 3 * D, :] = exact(joined[:, D:], centre)
    tail_out[3 * D :, :] = late_out[7 * D + 32 : 7 * D + 40, :] + exact(turned, cent_keep[0], 1, 1)


def tables(points):
    order = np.arange(MODES)[:, None]
    angle = (order * np.arange(points)[None, :]) % points * (2.0 * math.pi / points)
    full = np.concatenate([np.cos(angle), np.sin(angle)], 0).astype(np.float32)
    kind = np.dtype(ml_dtypes.bfloat16)
    high = full.astype(kind)
    rest = full - high.astype(np.float32)
    middle = rest.astype(kind)
    low = (rest - middle.astype(np.float32)).astype(kind)
    zero = np.zeros((4 * MODES, points), kind)
    column = np.concatenate([high, middle, high, middle, high, low, zero], 0).T
    row = np.concatenate([high, middle], 0).reshape(4 * MODES, points // ROWS, ROWS).transpose(1, 0, 2)
    return np.ascontiguousarray(column), np.ascontiguousarray(row)


def summed_grads(samples_in, target, mask, attn_w, ffn_w, spec_w, turned_w, vectors):
    parts = samples_in.shape[0] // 2
    count, points = 2, samples_in.shape[2] * parts
    devices = FLAYERS * MODES
    total = count * points
    steps = points // ROWS
    column, row = tables(points)
    vmem = pl.BlockSpec(memory_space=pltpu.VMEM)
    anywhere = pl.BlockSpec(memory_space=pl.ANY)
    first = [
        ((parts, 8, samples_in.shape[2]), F32),
        ((parts, 8, samples_in.shape[2]), F32),
        ((NVEC_ROWS, D), F32),
        ((8 * D, D), F32),
        ((8 * D, D), F32),
        ((8 * D, D), F32),
        ((8 * D, D), F32),
        ((devices, 8, D), F32),
        ((devices, 8, D), F32),
        ((8, D), F32),
        ((8, D), F32),
        ((8, D), F32),
        ((devices // 2, 8, D), F32),
    ]
    numbers = (3 * devices, 3 * devices, parts - 1, parts - 1, devices - 1, devices - 1, devices // 2, devices // 2)
    scratch = [
        ((total, D), BF16),
        ((total // ROWS, 16, ROWS), BF16),
        ((6 * D, 2 * D), BF16),
        ((4 * D, 3 * D), BF16),
        ((6 * D, FF), BF16),
        ((2 * FF, 3 * D), BF16),
        ((count, D, FF), BF16),
        ((count, 8, D), F32),
        ((LAYERS, 2 * FF, 2 * D), BF16),
        ((LAYERS, 2 * FF, D), BF16),
        ((LAYERS, 6 * D, FF), BF16),
        ((total, 2 * D), F32),
        ((total, 2 * D), F32),
        ((LAYERS, total, FF), F32),
        ((LAYERS, total, 2 * FF), BF16),
        ((total, 2 * D), BF16),
        ((total, 2 * D), BF16),
        ((total, 3 * D), BF16),
        ((FLAYERS, points, 3 * D), BF16),
        ((points, 3 * D), BF16),
        ((count, 2 * D, 2 * D), F32),
        ((D, 2 * D), BF16),
        ((count, D, D), BF16),
        ((LAYERS, count, D, D), F32),
        ((LAYERS, count, 3, D, D), F32),
        ((count, 2 * D, 2 * D), BF16),
        ((LAYERS, D, 2 * D), F32),
        ((4 * MODES, 2 * D), F32),
        ((FLAYERS, 2 * count * MODES, D), F32),
        ((2 * D, D), BF16),
        ((3, 2 * D, 2 * D), F32),
        ((4 * D, 2 * D), F32),
        ((LAYERS, 2 * D, FF), F32),
        ((2 * D, FF), F32),
        ((2 * D, 2 * D), F32),
        ((count, 16, 2 * D), F32),
        ((count, 16, 2 * FF), F32),
        ((16, 4 * D), F32),
        ((96, FF), F32),
        ((total, D), F32),
        ((count, 2, 2 * D, 2 * D), BF16),
        ((count, 4 * D, 2 * D), BF16),
    ]
    shapes = [(8 * D, D), (8 * D, D), (devices * FREQ, D), (3 * D + 8, D)]
    return pl.pallas_call(
        step_kernel,
        out_shape=[jax.ShapeDtypeStruct(shape, F32) for shape in shapes],
        in_specs=[vmem] * 5 + [anywhere] + [vmem] * 2 + [anywhere] * 2,
        out_specs=[anywhere, vmem, anywhere, vmem],
        scratch_shapes=[
            pltpu.VMEM(spec_w.shape, F32),
            pltpu.VMEM(column.shape, BF16),
            pltpu.VMEM(row.shape, BF16),
            pltpu.VMEM(shapes[0], F32),
            pltpu.VMEM(shapes[2], F32),
            pltpu.SemaphoreType.DMA((5,)),
        ]
        + [pltpu.VMEM(*item) for item in first]
        + [pltpu.SemaphoreType.DMA((number,)) for number in numbers]
        + [pltpu.VMEM(*item) for item in scratch],
        compiler_params=pltpu.CompilerParams(
            vmem_limit_bytes=64 * 2**20 - 2**17, collective_id=0, has_side_effects=True
        ),
    )(
        samples_in,
        target,
        mask,
        attn_w,
        ffn_w,
        spec_w,
        turned_w,
        vectors,
        jnp.asarray(column),
        jnp.asarray(row),
    )


def update_kernel(
    early_any,
    late_any,
    modes_any,
    tail_any,
    vectors,
    vector_m,
    vector_v,
    attn_w,
    ffn_w,
    spec_w,
    turned_w,
    attn_m,
    ffn_m,
    spec_m,
    turned_m,
    attn_v,
    ffn_v,
    spec_v,
    turned_v,
    loss_out,
    count_out,
    weight_out,
    update_out,
    ratio_out,
    vector_m_out,
    vector_v_out,
    vector_w_out,
    vector_low_out,
    *rest,
):
    outs, scratch = rest[:16], rest[16:]
    ins = (attn_w, ffn_w, spec_w, turned_w, attn_m, ffn_m, spec_m, turned_m, attn_v, ffn_v, spec_v, turned_v)
    held, fresh = scratch[:12], scratch[12:28]
    flat, in_sems, out_sems, early, late, modes, tail, grad_sems = scratch[28:]

    blocks = [(2, 0), (2, 1), (1, 1), (1, 0), (0, 1), (0, 0), (3, None)]

    def view(ref, part):
        return ref if part is None else ref.at[part]

    def load(slot, kind):
        array, part = blocks[slot]
        number = kind * 4 + array
        return pltpu.make_async_copy(
            view(ins[number], part), view(held[number], part), in_sems.at[slot * 3 + kind]
        )

    def store(slot, kind):
        array, part = blocks[slot]
        number = kind * 4 + array
        return pltpu.make_async_copy(
            view(fresh[number], part), view(outs[number], part), out_sems.at[slot * 4 + kind]
        )

    grads = [
        pltpu.make_async_copy(source, target, grad_sems.at[i])
        for i, (source, target) in enumerate(
            ((late_any, late), (tail_any, tail), (modes_any, modes), (early_any, early))
        )
    ]
    for copy in grads[:3]:
        copy.start()
    for kind in range(3):
        load(0, kind).start()
    grads[3].start()
    for slot in range(1, len(blocks)):
        for kind in range(3):
            load(slot, kind).start()
    grads[0].wait()
    grads[1].wait()
    misc = late[7 * D + 16 : 7 * D + 24, :]
    loss_out[0] = jnp.sum(misc[0:1])
    valid = jnp.sum(misc[1:2], keepdims=True)
    count_out[0] = jnp.sum(misc[1:2])
    scale = 1.0 / valid

    def moved(weight, grad, first, second):
        first_new = BETA_ONE * first + (1.0 - BETA_ONE) * grad
        second_new = BETA_TWO * second + (1.0 - BETA_TWO) * grad * grad
        update = (
            first_new
            / (1.0 - BETA_ONE**STEP)
            / (jnp.sqrt(second_new / (1.0 - BETA_TWO**STEP)) + ADAM_EPS)
            + DECAY * weight
        )
        return first_new, second_new, update

    def note(slot, weight_sum, update_sum):
        weight_norm, update_norm = jnp.sqrt(weight_sum), jnp.sqrt(update_sum)
        ratio = weight_norm / (update_norm + ADAM_EPS)
        weight_out[slot] = weight_norm[0, 0]
        update_out[slot] = update_norm[0, 0]
        ratio_out[slot] = ratio[0, 0]
        return RATE * ratio

    def total(sums):
        return sum(jnp.sum(value, keepdims=True) for value in sums.values())

    for i in range(NVEC_ROWS):
        start = i * D
        size = min(D, flat.shape[0] - start)
        row = tail[3 * D + i : 3 * D + i + 1, :] if i < 3 else late[7 * D + i : 7 * D + i + 1, :]
        flat[start : start + size] = (row * scale)[:, :size].reshape(size)
    weight = vectors[...]
    first_new, second_new, update = moved(weight, flat[...], vector_m[...], vector_v[...])
    vector_m_out[...] = first_new
    vector_v_out[...] = second_new
    rate = note(
        7,
        jnp.sum(weight * weight).reshape(1, 1),
        jnp.sum(update * update).reshape(1, 1),
    )
    flat[...] = jnp.broadcast_to(rate, (1, D)).reshape(D)[0] * update
    weight = weight - flat[...]
    vector_w_out[...] = weight
    vector_low_out[...] = weight.astype(BF16)

    def grad_blocks(array, part):
        if array == 0:
            if part:
                places = [(early, 5 * D + FREQ), (late, 0), (late, D), (early, 6 * D + FREQ)]
            else:
                places = [(tail, 0), (tail, D), (tail, 2 * D), (late, 6 * D)]
            return [
                (ref, start, D, 0, (slice(None), slice(j * D, (j + 1) * D)))
                for j, (ref, start) in enumerate(places)
            ]
        if array == 1:
            ref, starts = (early, (0, 1, 2, 3)) if part else (late, (4, 5, 2, 3))
            return [
                (ref, starts[j] * D, D, 0, (j // 2, slice(None), slice(j % 2 * D, j % 2 * D + D)))
                for j in range(4)
            ]
        if array == 3:
            return [
                (early, 4 * D, FREQ, 0, (slice(None), slice(0, D))),
                (early, 4 * D + FREQ, FREQ, 0, (slice(None), slice(D, 2 * D))),
                (early, 5 * D, FREQ, 0, (slice(None), slice(2 * D, 2 * D + FREQ))),
            ]
        return [
            (modes, (part * MODES + k) * FREQ, FREQ, j * FREQ, (k, j))
            for k in range(MODES)
            for j in range(2)
        ]

    grads[2].wait()
    grads[3].wait()
    for slot, (array, part) in enumerate(blocks):
        for kind in range(3):
            load(slot, kind).wait()
        weight_ref, first_ref, second_ref = [view(held[kind * 4 + array], part) for kind in range(3)]
        first_out, second_out, weight_new, low_out = [view(fresh[kind * 4 + array], part) for kind in range(4)]
        pieces = grad_blocks(array, part)
        weight_sums, update_sums = {}, {}
        for ref, start, rows, lane, where in pieces:
            weight = weight_ref[where]
            width = weight.shape[1]
            grad = ref[start : start + rows, lane : lane + width] * scale
            first_new, second_new, update = moved(weight, grad, first_ref[where], second_ref[where])
            first_out[where] = first_new
            second_out[where] = second_new
            weight_new[where] = update
            weight_sums[width] = weight_sums.get(width, 0.0) + column_sum(weight * weight)
            update_sums[width] = update_sums.get(width, 0.0) + column_sum(update * update)
        store(slot, 0).start()
        store(slot, 1).start()
        place = (0 + part if array == 0 else 2 + part if array == 1 else 4 + part) if part is not None else 6
        rate = note(place, total(weight_sums), total(update_sums))
        for ref, start, rows, lane, where in pieces:
            weight = weight_ref[where] - rate * weight_new[where]
            weight_new[where] = weight
            low_out[where] = weight.astype(BF16)
        store(slot, 2).start()
        store(slot, 3).start()
    for slot in range(len(blocks)):
        for kind in range(4):
            store(slot, kind).wait()


def fast_body(samples_in, target, mask, attn_w, ffn_w, spec_w, dense_w, vectors, *moments):
    flat_spec = spec_w.reshape(FLAYERS, MODES * 2 * FREQ, FREQ)
    grads = summed_grads(samples_in, target, mask, attn_w, ffn_w, flat_spec, dense_w.T, vectors)
    sets = [
        (attn_w, ffn_w, spec_w, dense_w.T),
        (moments[0], moments[1], moments[2], moments[3].T),
        (moments[5], moments[6], moments[7], moments[8].T),
    ]
    vmem = pl.BlockSpec(memory_space=pltpu.VMEM)
    smem = pl.BlockSpec(memory_space=pltpu.SMEM)
    anywhere = pl.BlockSpec(memory_space=pl.ANY)
    shapes = [item.shape for item in sets[0]]
    kinds = (F32, F32, F32, BF16)
    scalar = [jax.ShapeDtypeStruct((1,), F32)] * 2 + [jax.ShapeDtypeStruct((8,), F32)] * 3
    line = [jax.ShapeDtypeStruct(vectors.shape, kind) for kind in kinds]
    arrays = [jax.ShapeDtypeStruct(shape, kind) for kind in kinds for shape in shapes]
    out = pl.pallas_call(
        update_kernel,
        out_shape=scalar + line + arrays,
        in_specs=[anywhere] * 4 + [vmem] * 3 + [anywhere] * 12,
        out_specs=[smem] * 5 + [vmem] * 4 + [anywhere] * 16,
        scratch_shapes=[pltpu.VMEM(shape, F32) for _ in range(3) for shape in shapes]
        + [pltpu.VMEM(shape, kind) for kind in kinds for shape in shapes]
        + [pltpu.VMEM(vectors.shape, F32), pltpu.SemaphoreType.DMA((21,)), pltpu.SemaphoreType.DMA((28,))]
        + [pltpu.VMEM(grad.shape, F32) for grad in grads]
        + [pltpu.SemaphoreType.DMA((4,))],
        compiler_params=pltpu.CompilerParams(vmem_limit_bytes=60 * 2**20),
    )(*grads, vectors, moments[4], moments[9], *sets[0], *sets[1], *sets[2])
    loss_sum, valid_count, weight_norms, update_norms, ratios = out[:5]
    line, arrays = out[5:9], out[9:]
    results = [loss_sum.reshape(()), valid_count.reshape(())]
    for array in range(4):
        for kind in range(4):
            item = arrays[kind * 4 + array]
            results.append(item.T if array == 3 else item)
    return tuple(results + list(line) + [weight_norms, update_norms, ratios])


def choose_body(*arrays):
    samples_in = arrays[0]
    dp, parts = lax.axis_size("dp"), lax.axis_size("pts")
    fits = dp * parts == FLAYERS * MODES and dp == 4 and samples_in.shape[0] == 2 * parts
    return (fast_body if fits and samples_in.shape[2] * parts % WIDE == 0 else body)(*arrays)


def solution(mesh):
    placed = (
        P("dp", None, "pts"),
        P("dp", "pts"),
        P("dp", "pts"),
        P(),
        P(),
        P(),
        P(),
        P(),
        P(),
        P(),
        P(),
        P(),
        P(),
        P(),
        P(),
        P(),
        P(),
        P(),
    )
    return jax.shard_map(
        choose_body,
        mesh=mesh,
        in_specs=placed,
        out_specs=(
            P(),
            P(),
            P(),
            P(),
            P(),
            P(),
            P(),
            P(),
            P(),
            P(),
            P(),
            P(),
            P(),
            P(),
            P(),
            P(),
            P(),
            P(),
            P(),
            P(),
            P(),
            P(),
            P(),
            P(),
            P(),
        ),
        check_vma=False,
    )
```

```python
import math

import jax
import jax.numpy as jnp
import ml_dtypes
import numpy as np
from jax import lax
from jax.experimental import pallas as pl
from jax.experimental.pallas import tpu as pltpu
from jax.sharding import PartitionSpec as P

D = 128
HEADS = 4
FF = 256
FREQ = 64
MODES = 16
LAYERS = 2
FLAYERS = 2
STEP = 5


HIGH = lax.Precision.HIGHEST
NORM_EPS = 1e-05
BETA_ONE = 0.5
BETA_TWO = 0.5
RATE = 0.2
DECAY = 0.01
ADAM_EPS = 1e-06


def vector_table():
    entries = [("lift_value", 0, D), ("lift_coord", 0, D), ("lift_bias", 0, D)]
    for layer in range(LAYERS):
        entries = entries + [
            ("key_gain", layer, D),
            ("value_gain", layer, D),
            ("inner_bias", layer, FF),
            ("outer_bias", layer, D),
        ]
    entries = entries + [("proj_bias", 0, FREQ)]
    for layer in range(FLAYERS):
        entries = entries + [("fourier_bias", layer, FREQ)]
    entries = entries + [("head_bias", 0, FREQ), ("head_out", 0, FREQ)]
    offsets = {}
    start = 0
    for label, layer, length in entries:
        offsets[label, layer] = (start, length)
        start = start + length
    return offsets


def pick(vectors, label, layer):
    start, length = vector_table()[label, layer]
    return vectors[start : start + length]


def head_norm(values, gain):
    centred = values - jnp.mean(values, -1, keepdims=True)
    scaled = centred * lax.rsqrt(jnp.mean(centred * centred, -1, keepdims=True) + NORM_EPS)
    return scaled * gain.reshape(HEADS, D // HEADS)


def lift(params, inputs):
    vectors = params[4]
    value = inputs[..., 0, :, None]
    coord = inputs[..., 1, :, None]
    return (
        value * pick(vectors, "lift_value", 0)
        + coord * pick(vectors, "lift_coord", 0)
        + pick(vectors, "lift_bias", 0)
    )


def attn_front(params, rows, layer, points):
    weight = params[0][layer]
    vectors = params[4]
    mixed = jnp.einsum("...d,de->...e", rows, weight[:, : 3 * D], precision=HIGH)
    shape = rows.shape[:-1] + (HEADS, D // HEADS)
    query = mixed[..., :D].reshape(shape)
    keys = head_norm(mixed[..., D : 2 * D].reshape(shape), pick(vectors, "key_gain", layer))
    values = head_norm(mixed[..., 2 * D :].reshape(shape), pick(vectors, "value_gain", layer))
    partial_sum = jnp.einsum("...phe,...phf->...hef", keys, values, precision=HIGH) / points
    return (query, partial_sum)


def attn_rear(params, rows, query, summary, layer):
    weight = params[0][layer]
    attended = jnp.einsum("...phe,...hef->...phf", query, summary, precision=HIGH).reshape(
        rows.shape
    )
    return rows + jnp.einsum("...d,de->...e", attended, weight[:, 3 * D :], precision=HIGH)


def ffn_block(params, rows, layer):
    weight = params[1][layer]
    vectors = params[4]
    inner = jnp.einsum("...d,df->...f", rows, weight[0], precision=HIGH) + pick(
        vectors, "inner_bias", layer
    )
    outer = jnp.einsum("...f,df->...d", jax.nn.gelu(inner), weight[1], precision=HIGH)
    return rows + outer + pick(vectors, "outer_bias", layer)


def project(params, rows):
    return jnp.einsum("...d,df->...f", rows, params[3][:D], precision=HIGH) + pick(
        params[4], "proj_bias", 0
    )


def mode_table(count, total):
    position = jnp.arange(count, dtype=jnp.int32)
    orders = jnp.arange(MODES, dtype=jnp.int32)
    phase = orders[:, None] * position[None, :] % total
    angle = phase.astype(jnp.float32) * (2.0 * math.pi / total)
    return jnp.concatenate([jnp.cos(angle), jnp.sin(angle)], 0)


def spectral_mix(coef, spec, first, width):
    columns = lax.dynamic_slice_in_dim(spec, first, width, 3)
    cosine = coef[..., :MODES, :]
    sine = coef[..., MODES:, :]
    real_part = columns[:, 0]
    imag_part = columns[:, 1]
    mixed_cos = jnp.einsum("...mf,mfg->...mg", cosine, real_part, precision=HIGH) + jnp.einsum(
        "...mf,mfg->...mg", sine, imag_part, precision=HIGH
    )
    mixed_sin = jnp.einsum("...mf,mfg->...mg", sine, real_part, precision=HIGH) - jnp.einsum(
        "...mf,mfg->...mg", cosine, imag_part, precision=HIGH
    )
    return jnp.concatenate([mixed_cos, mixed_sin], -2)


def fourier_end(params, back, rows, layer):
    local = params[3][D + layer * FREQ : D + (layer + 1) * FREQ]
    inner = back + jnp.einsum("...f,fg->...g", rows, local, precision=HIGH)
    return jax.nn.gelu(inner + pick(params[4], "fourier_bias", layer))


def head_loss(params, rows, target, mask_f):
    start = D + FLAYERS * FREQ
    hidden = jax.nn.gelu(
        jnp.einsum("...f,fg->...g", rows, params[3][start : start + FREQ], precision=HIGH)
        + pick(params[4], "head_bias", 0)
    )
    pred = jnp.einsum("...f,f->...", hidden, pick(params[4], "head_out", 0), precision=HIGH)
    diff = pred - target
    return jnp.sum(mask_f * diff * diff)


def add_all(first, second):
    return jax.tree.map(jnp.add, first, second)


def spectral_setup(points, parts):
    width = FREQ // parts
    return (mode_table(points, points), lax.axis_index("pts") * width, width, points)


def fourier_mix(spec, field, setup):
    grid, column, width, points = setup
    channel_rows = lax.all_to_all(field, "pts", split_axis=2, concat_axis=1, tiled=True)
    own_coef = jnp.einsum("kp,spc->skc", grid, channel_rows, precision=HIGH) / math.sqrt(points)
    full = lax.all_gather(own_coef, "pts", axis=2, tiled=True)
    mixed = spectral_mix(full, spec, column, width)
    spread = jnp.einsum("kp,skc->spc", grid, mixed, precision=HIGH) / math.sqrt(MODES)
    back = lax.all_to_all(spread, "pts", split_axis=1, concat_axis=2, tiled=True)
    return (back, full)


def fourier_back(params, grad_out, kept_item, layer, setup):
    field, full, back = kept_item
    grid, column, width, points = setup
    _, end_pull = jax.vjp(
        lambda weights, spread, inner: fourier_end(weights, spread, inner, layer),
        params,
        back,
        field,
    )
    grads, grad_back, grad_field = end_pull(grad_out)
    _, mix_pull = jax.vjp(
        lambda coef, weight: spectral_mix(coef, weight, column, width), full, params[2][layer]
    )
    grad_rows = lax.all_to_all(grad_back, "pts", split_axis=2, concat_axis=1, tiled=True)
    grad_mixed = jnp.einsum("kp,spc->skc", grid, grad_rows, precision=HIGH) / math.sqrt(MODES)
    grad_full, grad_spec = mix_pull(grad_mixed)
    grad_coef = lax.psum_scatter(grad_full, "pts", scatter_dimension=2, tiled=True)
    grad_chan = jnp.einsum("kp,skc->spc", grid, grad_coef, precision=HIGH) / math.sqrt(points)
    grad_field = grad_field + lax.all_to_all(
        grad_chan, "pts", split_axis=1, concat_axis=2, tiled=True
    )
    grads = (grads[0], grads[1], grads[2].at[layer].add(grad_spec), grads[3], grads[4])
    return (grads, grad_field)


def attention_back(params, grad_rows, kept_item, layer, points):
    rows, summary = kept_item
    (query, partial_sum), front_pull = jax.vjp(
        lambda weights, inner: attn_front(weights, inner, layer, points), params, rows
    )
    summary = lax.psum(partial_sum, "pts")
    middle, rear_pull = jax.vjp(
        lambda weights, inner, asked, summed: attn_rear(weights, inner, asked, summed, layer),
        params,
        rows,
        query,
        summary,
    )
    _, ffn_pull = jax.vjp(lambda weights, inner: ffn_block(weights, inner, layer), params, middle)
    ffn_grads, grad_middle = ffn_pull(grad_rows)
    rear_grads, grad_direct, grad_query, grad_summary = rear_pull(grad_middle)
    grad_summary = lax.psum(grad_summary, "pts")
    front_grads, grad_front = front_pull((grad_query, grad_summary))
    return (add_all(add_all(ffn_grads, rear_grads), front_grads), grad_direct + grad_front)


def lamb(weight, grad, first, second):
    first_new = BETA_ONE * first + (1.0 - BETA_ONE) * grad
    second_new = BETA_TWO * second + (1.0 - BETA_TWO) * grad * grad
    update = (
        first_new
        / (1.0 - BETA_ONE**STEP)
        / (jnp.sqrt(second_new / (1.0 - BETA_TWO**STEP)) + ADAM_EPS)
        + DECAY * weight
    )
    return (first_new, second_new, update)


def trust_step(weight, update, stacked):
    axes = tuple(range(1, weight.ndim)) if stacked else tuple(range(weight.ndim))
    weight_norm = jnp.sqrt(jnp.sum(weight * weight, axes))
    update_norm = jnp.sqrt(jnp.sum(update * update, axes))
    ratio = weight_norm / (update_norm + ADAM_EPS)
    scale = ratio.reshape(ratio.shape + (1,) * (weight.ndim - ratio.ndim))
    return (
        weight - RATE * scale * update,
        jnp.atleast_1d(weight_norm),
        jnp.atleast_1d(update_norm),
        jnp.atleast_1d(ratio),
    )


def finish(loss_sum, valid_count, params, grads, firsts, seconds):
    results = [loss_sum, valid_count]
    weight_norms, update_norms, ratios = ([], [], [])
    for weight, grad, first, second, stacked in zip(
        params, grads, firsts, seconds, (True, True, True, False, False)
    ):
        first_new, second_new, update = lamb(weight, grad, first, second)
        fresh, weight_norm, update_norm, ratio = trust_step(weight, update, stacked)
        results = results + [first_new, second_new, fresh, fresh.astype(jnp.bfloat16)]
        weight_norms.append(weight_norm)
        update_norms.append(update_norm)
        ratios.append(ratio)
    return results + [
        jnp.concatenate(weight_norms),
        jnp.concatenate(update_norms),
        jnp.concatenate(ratios),
    ]


def body(
    samples_in,
    target,
    mask,
    attn_w,
    ffn_w,
    spec_w,
    dense_w,
    vectors,
    attn_m,
    ffn_m,
    spec_m,
    dense_m,
    vector_m,
    attn_v,
    ffn_v,
    spec_v,
    dense_v,
    vector_v,
):
    params = (attn_w, ffn_w, spec_w, dense_w, vectors)
    parts = lax.axis_size("pts")
    local_pts = samples_in.shape[2]
    points = local_pts * parts
    mask_f = mask.astype(jnp.float32)
    valid_count = lax.psum(jnp.sum(mask_f), ("dp", "pts"))
    setup = spectral_setup(points, parts)
    rows, lift_pull = jax.vjp(lambda weights: lift(weights, samples_in), params)
    kept = []
    for layer in range(LAYERS):
        query, partial_sum = attn_front(params, rows, layer, points)
        summary = lax.psum(partial_sum, "pts")
        kept.append((rows, summary))
        rows = ffn_block(params, attn_rear(params, rows, query, summary, layer), layer)
    field, proj_pull = jax.vjp(project, params, rows)
    spectral_kept = []
    for layer in range(FLAYERS):
        back, full = fourier_mix(params[2][layer], field, setup)
        spectral_kept.append((field, full, back))
        field = fourier_end(params, back, field, layer)
    loss_part, head_pull = jax.vjp(
        lambda weights, inner: head_loss(weights, inner, target, mask_f), params, field
    )
    grads, grad_field = head_pull(1.0 / valid_count)
    for layer in reversed(range(FLAYERS)):
        layer_grads, grad_field = fourier_back(
            params, grad_field, spectral_kept[layer], layer, setup
        )
        grads = add_all(grads, layer_grads)
    proj_grads, grad_rows = proj_pull(grad_field)
    grads = add_all(grads, proj_grads)
    for layer in reversed(range(LAYERS)):
        layer_grads, grad_rows = attention_back(params, grad_rows, kept[layer], layer, points)
        grads = add_all(grads, layer_grads)
    grads = add_all(grads, lift_pull(grad_rows)[0])
    summed = lax.psum((grads[0], grads[1], grads[2], grads[3], grads[4], loss_part), ("dp", "pts"))
    out = finish(
        summed[5],
        valid_count,
        params,
        summed[:5],
        (attn_m, ffn_m, spec_m, dense_m, vector_m),
        (attn_v, ffn_v, spec_v, dense_v, vector_v),
    )
    return (
        out[0],
        out[1],
        out[2],
        out[3],
        out[4],
        out[5],
        out[6],
        out[7],
        out[8],
        out[9],
        out[10],
        out[11],
        out[12],
        out[13],
        out[14],
        out[15],
        out[16],
        out[17],
        out[18],
        out[19],
        out[20],
        out[21],
        out[22],
        out[23],
        out[24],
    )


F32 = jnp.float32
BF16 = jnp.bfloat16
ROWS = 1024
WIDE = 2048
NVEC_ROWS = 16


def dot(first, second, left=1, right=0, precision=None):
    return lax.dot_general(
        first,
        second,
        (((left,), (right,)), ((), ())),
        precision=precision,
        preferred_element_type=F32,
    )


def exact(first, second, left=1, right=0):
    return dot(first, second, left, right, HIGH)


def halves(value):
    high = value.astype(BF16)
    return high, (value - high.astype(F32)).astype(BF16)


def thirds(value):
    high = value.astype(BF16)
    rest = value - high.astype(F32)
    middle = rest.astype(BF16)
    return high, middle, (rest - middle.astype(F32)).astype(BF16)


def beside(*pieces):
    return jnp.concatenate(pieces, 1)


def above(*pieces):
    return jnp.concatenate(pieces, 0)


def fold(value):
    half = value.shape[1] // 2
    return value[:, :half] + value[:, half:]


def column_sum(value):
    rows, width = value.shape
    return jnp.sum(value.reshape(rows // 8, 8, width), 0)


def gelu_pair(inner):
    scale = math.sqrt(2.0 / math.pi)
    square = inner * inner
    bend = jnp.tanh(inner * (scale + (scale * 0.044715) * square))
    half = 0.5 + 0.5 * bend
    slope = half + (0.5 * inner) * (1.0 - bend * bend) * (scale + (3.0 * scale * 0.044715) * square)
    return inner * half, slope


def wide6_weight(weight):
    high, middle, low = thirds(weight)
    return above(high, high, middle, middle, low, high)


def wide6(pieces, weight):
    high, middle, low = pieces
    return dot(beside(high, middle, high, middle, high, low), weight)


def tall6_weight(weight):
    high, middle, low = thirds(weight)
    pair = beside(high, middle)
    return above(pair, pair), above(low, high)


def tall6(pieces, weights):
    high, middle, low = pieces
    return fold(dot(beside(high, middle), weights[0])) + dot(beside(high, low), weights[1])


def even4_weight(weight):
    high, low = halves(weight)
    pair = beside(high, low)
    return above(pair, pair)


def even4(pieces, weight):
    return fold(dot(beside(*pieces), weight))


def head_blocks(width):
    row = lax.broadcasted_iota(jnp.int32, (width, width), 0)
    column = lax.broadcasted_iota(jnp.int32, (width, width), 1)
    return row // (D // HEADS) == column // (D // HEADS)


def doubled(weight):
    zero = jnp.zeros_like(weight)
    return above(beside(weight, zero), beside(zero, weight))


MESH = pl.DeviceIdType.MESH


def position():
    dp, pts = lax.axis_index("dp"), lax.axis_index("pts")
    x, core, z, y = dp // 2, dp % 2, pts // 2, pts % 2
    return x, core, z, y


def device_of(x, core, z, y):
    return (2 * x + core, 2 * z + y)


def other(i):
    x, core, z, y = position()
    step = i + 1
    c = core + lax.div(step, 16) * (1 - 2 * core)
    x = x + lax.rem(lax.div(step, 8), 2) * (1 - 2 * x)
    y = y + lax.rem(lax.div(step, 4), 2) * (1 - 2 * y)
    z = lax.rem(z + lax.rem(step, 4), 4)
    return 16 * c + 8 * x + 4 * y + z, device_of(x, c, z, y)


def back_of(i):
    step = i + 1
    rest = lax.rem(step, 4)
    return step - rest + lax.rem(4 - rest, 4) - 1


def each_of(number, copy_of, start):
    def one(i, _):
        copy = copy_of(i)
        if start:
            copy.start()
        else:
            copy.wait()
        return 0

    lax.fori_loop(0, number, one, 0)


class Route:
    def __init__(self, rows, full, flat, landing, sends, receives, first):
        x, core, z, y = position()
        self.core, self.group = core, FLAYERS * MODES // 2
        self.rows, self.full, self.flat, self.landing = rows, full, flat, landing
        self.sends, self.receives, self.first = sends, receives, first
        self.peer = device_of(x, 1 - core, z, y)
        self.half, self.least = rows // 2, rows // (2 * self.group)
        self.own = (16 * core + 8 * x + 4 * y + z) * self.least

    def area(self, start, size):
        return pl.ds(pl.multiple_of(start, self.least), size)

    def link(self, source, target, slot, device):
        return pltpu.make_async_remote_copy(
            src_ref=source,
            dst_ref=target,
            send_sem=self.sends.at[self.first + slot],
            recv_sem=self.receives.at[self.first + slot],
            device_id=device,
            device_id_type=MESH,
        )

    def run(self, stage, start):
        half, least, core, group = self.half, self.least, self.core, self.group
        mine, yours = self.area(core * half, half), self.area((1 - core) * half, half)

        def copy_of(i):
            if stage == 0:
                return self.link(self.flat.at[yours], self.landing.at[pl.ds(0, half)], 2 * group - 1, self.peer)
            if stage == 3:
                return self.link(self.full.at[mine], self.full.at[mine if start else yours], 2 * group - 2, self.peer)
            number, device = other(i)
            if stage == 1:
                source = self.flat.at[self.area(number * least, least)]
                target = self.landing.at[self.area(half + i * least, least)]
            else:
                start_row = self.own if start else other(back_of(i))[0] * least
                source = self.full.at[self.area(self.own, least)]
                target = self.full.at[self.area(start_row, least)]
            return self.link(source, target, (stage - 1) * (group - 1) + i, device)

        if stage in (1, 2):
            each_of(group - 1, copy_of, start)
        elif start:
            copy_of(0).start()
        else:
            copy_of(0).wait()

    def start(self, stage):
        if stage == 2 and self.flat is not None:
            self.full[self.area(self.own, self.least), :] = self.flat[self.area(self.own, self.least), :]
        self.run(stage, True)

    def finish(self, stage):
        self.run(stage, False)
        if stage == 0:
            self.flat[self.area(self.core * self.half, self.half), :] += self.landing[: self.half, :]
        if stage == 1:
            mine = self.area(self.own, self.least)
            total = self.flat[mine, :]
            for i in range(self.group - 1):
                start = self.half + i * self.least
                total = total + self.landing[start : start + self.least, :]
            self.flat[mine, :] = total

    def step(self, stage):
        self.finish(stage)
        self.start(stage + 1)


def to_each(source_of, target, slot_of, mine, sends, receives, number, start):
    def copy_of(i):
        to, device = other(i)
        return pltpu.make_async_remote_copy(
            src_ref=source_of(to),
            dst_ref=target.at[slot_of(mine if start else other(back_of(i))[0])],
            send_sem=sends.at[i],
            recv_sem=receives.at[i],
            device_id=device,
            device_id_type=MESH,
        )

    each_of(number, copy_of, start)


def step_kernel(
    samples_ref,
    target_ref,
    mask_ref,
    attn_ref,
    ffn_ref,
    spec_any,
    turned_ref,
    vectors_ref,
    table_any,
    trow_any,
    early_any,
    late_out,
    mode_any,
    tail_out,
    spec_ref,
    table_ref,
    trow_ref,
    early_out,
    mode_out,
    local_sems,
    outgoing,
    incoming,
    vec_ref,
    early,
    early_land,
    late,
    late_land,
    mode_send,
    mode_land,
    tail_send,
    tail_swap,
    tail_pair,
    tail_land,
    route_send,
    route_recv,
    point_send,
    point_recv,
    mode_sends,
    mode_recvs,
    tail_sends,
    tail_recvs,
    lifted,
    lrows,
    w_kv,
    w_kvt,
    w_in,
    w_int,
    w0_u,
    mid_rows,
    w_out0,
    w_out1,
    w_outt,
    x_keep,
    r_keep,
    slope_keep,
    act_keep,
    mid_keep,
    h1_keep,
    h2_keep,
    z_keep,
    e_keep,
    s_acc,
    w0_kv,
    w0_g,
    n_keep,
    small_keep,
    nt_keep,
    cent_keep,
    coef_acc,
    coef_keep,
    stack_ref,
    sq_acc,
    p_acc,
    w2_acc,
    w1_acc,
    kv_acc,
    v_acc,
    u_acc,
    vt_acc,
    b_acc,
    d_keep,
    t_keep,
    wz,
):
    parts = samples_ref.shape[0] // 2
    count = 2
    points = samples_ref.shape[2] * parts
    devices = FLAYERS * MODES
    x, core, z, y = position()
    pts = 2 * z + y
    place = 8 * x + 4 * y + z
    mine = 16 * core + place
    early_route = Route(early.shape[0], early_out, early, early_land, route_send, route_recv, 0)
    late_route = Route(late.shape[0], late_out, late, late_land, route_send, route_recv, devices)
    mode_route = Route(mode_out.shape[0], mode_out, None, None, route_send, route_recv, 2 * devices)

    barrier = pltpu.get_barrier_semaphore()
    take = [
        pltpu.make_async_copy(source, target, local_sems.at[i])
        for i, (source, target) in enumerate(((trow_any, trow_ref), (spec_any, spec_ref), (table_any, table_ref)))
    ]
    put_mode = pltpu.make_async_copy(mode_out, mode_any, local_sems.at[3])
    put_early = pltpu.make_async_copy(early_out, early_any, local_sems.at[4])
    for copy in take:
        copy.start()

    def greet(i, _):
        pl.semaphore_signal(barrier, inc=1, device_id=other(i)[1], device_id_type=MESH)
        return 0

    lax.fori_loop(0, devices - 1, greet, 0)
    for p in range(parts):
        outgoing[p, 0:2, :] = samples_ref[2 * p]
        outgoing[p, 2:4, :] = samples_ref[2 * p + 1]
        outgoing[p, 4:6, :] = target_ref[2 * p : 2 * p + 2, :]
        outgoing[p, 6:8, :] = mask_ref[2 * p : 2 * p + 2, :].astype(F32)
    incoming[pts] = outgoing[pts]
    for i in range(NVEC_ROWS - 1):
        vec_ref[i : i + 1, :] = vectors_ref[i * D : (i + 1) * D].reshape(1, D)
    last = vectors_ref.shape[0] - (NVEC_ROWS - 1) * D
    vec_ref[NVEC_ROWS - 1 :, :last] = vectors_ref[(NVEC_ROWS - 1) * D :].reshape(1, last)
    total = count * points
    steps = points // ROWS
    rows_all = total // ROWS
    blocks = head_blocks(D)
    block_f = jnp.where(blocks, 1.0, 0.0).astype(F32)
    block_b = block_f.astype(BF16)
    mean_weight = above(block_b, block_b)
    centre = (
        jnp.where(
            lax.broadcasted_iota(jnp.int32, (D, D), 0) == lax.broadcasted_iota(jnp.int32, (D, D), 1),
            1.0,
            0.0,
        ).astype(F32)
        - block_f * (HEADS / D)
    )
    eye = jnp.where(
        lax.broadcasted_iota(jnp.int32, (D, D), 0) == lax.broadcasted_iota(jnp.int32, (D, D), 1), 1.0, 0.0
    ).astype(F32)

    def vector(label, layer):
        start, length = vector_table()[label, layer]
        if length == 2 * D:
            row = start // D
            return beside(vec_ref[row : row + 1, :], vec_ref[row + 1 : row + 2, :])
        row = start // D
        if length == D:
            return vec_ref[row : row + 1, :]
        offset = start - row * D
        piece = vec_ref[row : row + 1, offset : offset + FREQ]
        return beside(piece, piece)

    def block(index):
        return pl.ds(pl.multiple_of(index * ROWS, ROWS), ROWS)

    wide_steps = points // WIDE

    def wide_block(index):
        return pl.ds(pl.multiple_of(index * WIDE, WIDE), WIDE)

    lift_rows = above(
        vector("lift_value", 0), vector("lift_coord", 0), vector("lift_bias", 0), jnp.zeros((5, D), F32)
    )

    def lift_weight(mixed):
        high, middle, low = [item.astype(F32) for item in thirds(mixed)]
        parts = []
        for i in range(2):
            hi, mi, lo = high[i : i + 1], middle[i : i + 1], low[i : i + 1]
            parts += [hi, hi, mi, mi, lo, hi]
        parts += [high[2:3], middle[2:3], low[2:3]]
        parts.append(jnp.zeros((D - 15, mixed.shape[1]), F32))
        return above(*parts).astype(BF16)

    def point_copy(k, start):
        other = lax.rem(pts + k, parts)
        sender = lax.rem(pts + parts - k, parts)
        return pltpu.make_async_remote_copy(
            src_ref=outgoing.at[other],
            dst_ref=incoming.at[pts if start else sender],
            send_sem=point_send.at[k - 1],
            recv_sem=point_recv.at[k - 1],
            device_id=(2 * x + core, other),
            device_id_type=MESH,
        )

    for layer in range(LAYERS):
        if layer == 1:
            pl.semaphore_wait(barrier, devices - 1)
            for k in range(1, parts):
                point_copy(k, True).start()
        weight = attn_ref[layer]
        keyed = beside(exact(weight[:, D : 2 * D], centre), exact(weight[:, 2 * D : 3 * D], centre))
        cent_keep[layer] = keyed
        if layer == 0:
            w0_kv[...] = lift_weight(exact(lift_rows, keyed))
        else:
            w_kv[...] = wide6_weight(keyed)
            pair, rest = tall6_weight(keyed.T)
            w_kvt[:, : 2 * D] = pair
            w_kvt[:, 2 * D :] = rest
        first, second = ffn_ref[layer, 0], ffn_ref[layer, 1]
        if layer:
            w_in[...] = wide6_weight(first)
            pair, rest = tall6_weight(first.T)
            w_int[:, : 2 * D] = pair
            w_int[:, 2 * D :] = rest
        pair, rest = tall6_weight(second.T)
        w_out0[layer] = pair
        w_out1[layer] = rest
        w_outt[layer] = wide6_weight(second)

    s_acc[...] = jnp.zeros_like(s_acc)
    coef_acc[...] = jnp.zeros_like(coef_acc)
    sq_acc[...] = jnp.zeros_like(sq_acc)
    p_acc[...] = jnp.zeros_like(p_acc)
    w2_acc[...] = jnp.zeros_like(w2_acc)
    w1_acc[...] = jnp.zeros_like(w1_acc)
    kv_acc[...] = jnp.zeros_like(kv_acc)
    v_acc[...] = jnp.zeros_like(v_acc)
    u_acc[...] = jnp.zeros_like(u_acc)
    vt_acc[...] = jnp.zeros_like(vt_acc)
    b_acc[...] = jnp.zeros_like(b_acc)

    for k in range(1, parts):
        point_copy(k, False).wait()
    whole = beside(*[incoming[p] for p in range(parts)])
    for s in range(count):
        value, coord = whole[2 * s : 2 * s + 1], whole[2 * s + 1 : 2 * s + 2]
        target, valid = whole[4 + s : 5 + s], whole[6 + s : 7 + s]
        one = jnp.ones_like(value)
        vh, vm, vl = [item.astype(F32) for item in thirds(value)]
        ch, cm, cl = [item.astype(F32) for item in thirds(coord)]
        th, tm, tl = [item.astype(F32) for item in thirds(target)]
        zero = jnp.zeros((D - 19, points), F32)
        stack = above(vh, vm, vh, vm, vh, vl, ch, cm, ch, cm, ch, cl, one, one, one, th, tm, tl, valid, zero)
        lifted[s * points : (s + 1) * points, :] = stack.T.astype(BF16)
        short = above(vh, vm, vl, ch, cm, cl, one, jnp.zeros((9, points), F32)).astype(BF16)
        for i in range(steps):
            lrows[s * steps + i] = short[:, i * ROWS : (i + 1) * ROWS]

    def head_scale(centred):
        high, low = halves(centred * centred)
        var = beside(
            dot(beside(high[:, :D], low[:, :D]), mean_weight), dot(beside(high[:, D:], low[:, D:]), mean_weight)
        )
        return lax.rsqrt(var * (HEADS / D) + NORM_EPS)

    def normalise(layer, where, s, centred):
        scale = head_scale(centred)
        normal = centred * scale
        if layer:
            x_keep[where, :] = normal
            r_keep[where, :] = scale
        high, low = halves(normal)
        s_acc[s] += dot(
            beside(high[:, :D], low[:, :D]), beside(high[:, D:], low[:, D:]), 0, 0
        )

    def quarters(value):
        half_row, half_col = value.shape[0] // 2, value.shape[1] // 2
        return (
            value[:half_row, :half_col]
            + value[half_row:, :half_col]
            + (value[:half_row, half_col:] + value[half_row:, half_col:])
        )

    def summarise(layer):
        weight = attn_ref[layer]
        key_gain = vector("key_gain", layer).reshape(1, D)
        value_gain = vector("value_gain", layer).reshape(1, D)
        key_column = jnp.sum(eye * key_gain, 1, keepdims=True)
        for s in range(count):
            plain = jnp.where(blocks, quarters(s_acc[s]), 0.0) * (1.0 / points)
            summary = key_column * plain * value_gain
            mixed = exact(summary, weight[:, 3 * D :])
            both = exact(weight[:, :D], mixed)
            n_keep[layer, s] = both
            small_keep[layer, s, 0] = plain
            small_keep[layer, s, 1] = summary
            small_keep[layer, s, 2] = mixed
            if layer == 0:
                rows = exact(lift_rows, eye + both)
                mid_rows[s] = rows
                w0_g[s] = lift_weight(rows)
                w0_u[s] = lift_weight(exact(rows, ffn_ref[0, 0]))
            else:
                pair, rest = tall6_weight(both)
                wz[s, : 2 * D, :] = pair
                wz[s, 2 * D :, :D] = rest
                nt_keep[s] = even4_weight(both.T)

    def feed(layer, index, mid, inner):
        where = block(index)
        act, slope = gelu_pair(inner + vector("inner_bias", layer))
        slope_keep[layer, where, :] = slope
        pieces = thirds(act)
        act_keep[layer, where, :] = beside(pieces[0], pieces[1])
        return mid + tall6(pieces, (w_out0[layer], w_out1[layer])) + vector("outer_bias", layer)

    def front_zero(index, _):
        where = wide_block(index)
        normalise(0, where, index // wide_steps, dot(lifted[where, :], w0_kv[...]))
        return 0

    lax.fori_loop(0, count * wide_steps, front_zero, 0)
    summarise(0)
    s_acc[...] = jnp.zeros_like(s_acc)

    def layer_zero(index, _):
        where = block(index)
        s = index // steps
        data = lifted[where, :]
        out = feed(0, index, dot(data, w0_g[s]), dot(data, w0_u[s]))
        d_keep[where, :] = out
        pieces = thirds(out)
        h1_keep[where, :] = beside(pieces[0], pieces[1])
        h2_keep[where, 2 * D :] = pieces[2]
        normalise(1, where, s, wide6(pieces, w_kv[...]))
        return 0

    lax.fori_loop(0, rows_all, layer_zero, 0)
    summarise(1)
    s_acc[...] = jnp.zeros_like(s_acc)

    def pieces_of(ref, where, number=3):
        value = ref[where, : number * D]
        return [value[:, i * D : (i + 1) * D] for i in range(number)]

    def layer_one(index, _):
        where = block(index)
        s = index // steps
        pieces = pieces_of(h1_keep, where, 2) + [h2_keep[where, 2 * D :]]
        mid = d_keep[where, :] + tall6(pieces, (wz[s, : 2 * D, :], wz[s, 2 * D :, :D]))
        pieces = thirds(mid)
        mid_keep[where, :] = beside(pieces[0], pieces[1])
        out = feed(1, index, mid, wide6(pieces, w_in[...]))
        h2_keep[where, :] = beside(*thirds(out))
        return 0

    lax.fori_loop(0, rows_all, layer_one, 0)

    def dense_rows(part):
        start = D + (part - 1) * FREQ if part else 0
        return turned_ref[:, start : start + (FREQ if part else D)].T

    proj0, proj1 = tall6_weight(doubled(dense_rows(0)))
    locals6 = [tall6_weight(doubled(dense_rows(part))) for part in (1, 2, 3)]
    turned6 = [tall6_weight(doubled(dense_rows(part).T)) for part in (1, 2, 3)]
    own = lax.broadcasted_iota(jnp.int32, (2 * count * MODES, MODES * D), 1) // D == lax.rem(
        lax.broadcasted_iota(jnp.int32, (2 * count * MODES, MODES * D), 0), MODES
    )

    def mode_rows(coef):
        cosine, sine = coef[:MODES], coef[MODES:]
        c = [cosine[:, s * FREQ : (s + 1) * FREQ] for s in range(count)]
        d = [sine[:, s * FREQ : (s + 1) * FREQ] for s in range(count)]
        return above(
            *[beside(c[s], d[s]) for s in range(count)], *[beside(d[s], -c[s]) for s in range(count)]
        )

    def spread_rows(rows):
        return jnp.where(own, beside(*([rows] * MODES)), 0.0)

    def unpack(rows):
        lead = count * MODES
        return above(
            *[beside(*[rows[j * lead + s * MODES : j * lead + (s + 1) * MODES] for s in range(count)]) for j in (0, 1)]
        )

    def pack(value):
        return above(
            *[
                value[j * MODES : (j + 1) * MODES, s * FREQ : (s + 1) * FREQ]
                for j in (0, 1)
                for s in range(count)
            ]
        )

    def set_stack(value):
        high, middle, low = thirds(value)
        stack_ref[...] = above(
            high, high, middle, middle, low, high, jnp.zeros((4 * MODES, D), BF16)
        )

    def take_coef(index, high, low):
        both = beside(high, low)
        each = both.shape[0] // ROWS
        for i in range(each):
            coef_acc[...] += dot(trow_ref[index * each + i], both[i * ROWS : (i + 1) * ROWS])

    def mix_forward(layer):
        coef = quarters(coef_acc[...]) * (1.0 / math.sqrt(points))
        coef_acc[...] = jnp.zeros_like(coef_acc)
        rows = mode_rows(coef)
        coef_keep[layer] = rows
        set_stack(unpack(exact(spread_rows(rows), spec_ref[layer])) * (1.0 / math.sqrt(MODES)))

    def mix_back(layer):
        cot = pack(quarters(coef_acc[...])) * (1.0 / math.sqrt(MODES))
        coef_acc[...] = jnp.zeros_like(coef_acc)
        kept_rows = coef_keep[layer]
        padded = beside(cot, jnp.zeros_like(cot))
        for k in range(MODES):
            for r in range(2 * count):
                mode_send[layer * MODES + k, r : r + 1, :] = kept_rows[r * MODES + k : r * MODES + k + 1]
                mode_send[layer * MODES + k, 4 + r : 5 + r, :] = padded[r * MODES + k : r * MODES + k + 1]
        wide = jnp.where(own, exact(cot, spec_ref[layer], 1, 1), 0.0)
        kept = wide[:, :D]
        for k in range(1, MODES):
            kept = kept + wide[:, k * D : (k + 1) * D]
        lead = count * MODES
        first, second = kept[:lead], kept[lead:]
        rows = above(first[:, :FREQ] - second[:, FREQ:], first[:, FREQ:] + second[:, :FREQ])
        set_stack(unpack(rows) * (1.0 / math.sqrt(points)))

    def project_step(index, _):
        where = wide_block(index)
        first = h2_keep[wide_block(index), :]
        second = h2_keep[wide_block(index + wide_steps), :]
        pieces = [beside(first[:, i * D : (i + 1) * D], second[:, i * D : (i + 1) * D]) for i in range(3)]
        field = tall6(pieces, (proj0, proj1)) + vector("proj_bias", 0)
        pieces = thirds(field)
        z_keep[0, where, :] = beside(*pieces)
        take_coef(index, pieces[0], pieces[1])
        return 0

    for copy in take:
        copy.wait()
    lax.fori_loop(0, wide_steps, project_step, 0)
    mix_forward(0)

    def fourier_field(layer, where):
        pieces = pieces_of(z_keep.at[layer], where)
        inner = dot(table_ref[where, :], stack_ref[...]) + (
            tall6(pieces, locals6[layer]) + vector("fourier_bias", layer)
        )
        return gelu_pair(inner)

    def fourier_one(index, _):
        where = wide_block(index)
        field, slope = fourier_field(0, where)
        d_keep[where, :] = slope
        pieces = thirds(field)
        z_keep[1, where, :] = beside(*pieces)
        take_coef(index, pieces[0], pieces[1])
        return 0

    lax.fori_loop(0, wide_steps, fourier_one, 0)
    mix_forward(1)

    lane = lax.broadcasted_iota(jnp.int32, (2 * D, 2 * D), 1)
    row = lax.broadcasted_iota(jnp.int32, (2 * D, 2 * D), 0)
    inner_row = lax.rem(row, D)
    same = row // D == lax.rem(lane, D) // FREQ
    pick_target = (lane < D) & (inner_row >= 15) & (inner_row < 18)
    pick_mask = (lane >= D) & (inner_row == 18)
    spread = jnp.where(same & (pick_target | pick_mask), 1.0, 0.0).astype(BF16)
    out_row = vector("head_out", 0)
    out_column = jnp.sum(eye * out_row, 1, keepdims=True)
    half_blocks = (
        lax.broadcasted_iota(jnp.int32, (D, D), 0) // FREQ == lax.broadcasted_iota(jnp.int32, (D, D), 1) // FREQ
    )
    out_weight = tall6_weight(jnp.where(half_blocks, out_column, 0.0))

    def pair_product(first, second):
        return dot(beside(*first), beside(*second), 0, 0)

    def loss_step(index, _):
        where = block(index)
        field, slope = fourier_field(1, where)
        pieces = thirds(field)
        hidden, hidden_slope = gelu_pair(tall6(pieces, locals6[2]) + vector("head_bias", 0))
        pred = tall6(thirds(hidden), out_weight)
        known = dot(beside(lifted[where, :], lifted[block(index + steps), :]), spread)
        diff = pred - known[:, :D]
        valid = known[:, D:]
        cot = (2.0 * valid) * diff
        b_acc[0:8, :D] += column_sum(valid * diff * diff)
        b_acc[8:16, :D] += column_sum(valid)
        b_acc[16:24, :D] += column_sum(hidden * cot)
        cot = cot * out_row * hidden_slope
        b_acc[24:32, :D] += column_sum(cot)
        split = thirds(cot)
        sq_acc[2] += pair_product(pieces[:2], split[:2])
        cot = tall6(split, turned6[2]) * slope
        b_acc[32:40, :D] += column_sum(cot)
        split = thirds(cot)
        e_keep[where, :] = beside(*split)
        sq_acc[1] += pair_product(pieces_of(z_keep.at[1], where, 2), split[:2])
        take_coef(index, *split[:2])
        return 0

    lax.fori_loop(0, steps, loss_step, 0)
    mix_back(1)

    def fourier_cot(layer, where):
        return tall6(pieces_of(e_keep, where), turned6[layer]) + dot(table_ref[where, :], stack_ref[...])

    def fourier_back(index, _):
        where = wide_block(index)
        cot = fourier_cot(1, where) * d_keep[where, :]
        b_acc[40:48, :D] += column_sum(cot)
        split = thirds(cot)
        e_keep[where, :] = beside(*split)
        sq_acc[0] += pair_product(pieces_of(z_keep.at[0], where, 2), split[:2])
        take_coef(index, *split[:2])
        return 0

    lax.fori_loop(0, wide_steps, fourier_back, 0)
    mix_back(0)
    mode_land[mine] = mode_send[mine]
    to_each(lambda r: mode_send.at[r], mode_land, lambda r: r, mine, mode_sends, mode_recvs, devices - 1, True)
    proj_back = wide6_weight(doubled(turned_ref[:, :D]))

    def project_back(index, _):
        where = wide_block(index)
        later = wide_block(index + wide_steps)
        cot = fourier_cot(0, where)
        b_acc[48:56, :D] += column_sum(cot)
        split = thirds(cot)
        first = pieces_of(h2_keep, where, 2)
        second = pieces_of(h2_keep, later, 2)
        p_acc[...] += dot(beside(first[0], second[0], first[1], second[1]), beside(*split[:2]), 0, 0)
        rows = wide6(split, proj_back)
        d_keep[where, :] = rows[:, :D]
        d_keep[later, :] = rows[:, D:]
        return 0

    lax.fori_loop(0, wide_steps, project_back, 0)

    def feed_back(layer, index, cot):
        where = block(index)
        base = 56 + layer * 16
        b_acc[base : base + 8, :D] += column_sum(cot)
        split = thirds(cot)
        act = act_keep[layer, where, :]
        w2_acc[layer] += dot(beside(*split[:2]), act[:, :FF], 0, 0)
        w2_acc[layer, :D, :] += dot(split[0], act[:, FF:], 0, 0)
        inner = wide6(split, w_outt[layer]) * slope_keep[layer, where, :]
        b_acc[base + 8 : base + 16, :] += column_sum(inner)
        return split, thirds(inner)

    def layer_one_back(index, _):
        @pl.when(index == 1)
        def _():
            to_each(lambda r: mode_send.at[r], mode_land, lambda r: r, mine, mode_sends, mode_recvs, devices - 1, False)
            landed = mode_land[...].reshape(devices * 8, D)
            shifted = above(landed[4:], landed[:4])
            row = lax.broadcasted_iota(jnp.int32, landed.shape, 0)
            product = exact(jnp.where(lax.rem(row, 8) < 4, landed, 0.0), shifted[:, :FREQ], 0, 0)
            mode_out[mode_route.area(mode_route.own, FREQ), :] = beside(product[:FREQ], product[FREQ:])
            mode_route.start(2)

        where = block(index)
        cot = d_keep[where, :]
        _, pieces = feed_back(1, index, cot)
        high, low = pieces[:2]
        mid = mid_keep[where, :]
        w1_acc[...] += dot(mid, high, 0, 0)
        w1_acc[:D, :] += dot(mid[:, :D], low, 0, 0)
        cot = cot + tall6(pieces, (w_int[:, : 2 * D], w_int[:, 2 * D :]))
        d_keep[where, :] = cot
        s_acc[index // steps] += pair_product(pieces_of(h1_keep, where, 2), halves(cot))
        return 0

    lax.fori_loop(0, rows_all, layer_one_back, 0)

    def attend_back(layer, products):
        weight = attn_ref[layer]
        query, outer = weight[:, :D], weight[:, 3 * D :]
        key_gain, value_gain = vector("key_gain", layer), vector("value_gain", layer)
        key_column = jnp.sum(eye * key_gain, 1, keepdims=True)
        key_total = jnp.zeros((D, 1), F32)
        value_total = jnp.zeros((1, D), F32)
        query_grad = jnp.zeros((D, D), F32)
        outer_grad = jnp.zeros((D, D), F32)
        for s in range(count):
            plain, summary, mixed = small_keep[layer, s, 0], small_keep[layer, s, 1], small_keep[layer, s, 2]
            turned = exact(query, products[s], 0, 0)
            outer_grad += exact(summary, turned, 0, 0)
            if layer:
                query_grad += exact(products[s], mixed, 1, 1)
            cot = jnp.where(blocks, exact(turned, outer, 1, 1), 0.0)
            both = cot * plain
            key_total += jnp.sum(both * value_gain, 1, keepdims=True)
            value_total += jnp.sum(both * key_column, 0, keepdims=True)
            scaled = key_column * cot * value_gain * (1.0 / points)
            t_keep[s, 0] = even4_weight(scaled.T)
            t_keep[s, 1] = even4_weight(scaled)
        if layer:
            early[5 * D + FREQ : 6 * D + FREQ, :] = query_grad
            early[6 * D + FREQ : 7 * D + FREQ, :] = outer_grad
        else:
            late[6 * D : 7 * D, :] = outer_grad
        return jnp.sum(eye * key_total, 0, keepdims=True), value_total

    for i in range(2):
        half = slice(i * D, (i + 1) * D)
        early[i * D : (i + 1) * D, :] = w1_acc[:D, half] + w1_acc[D:, half]
        early[(2 + i) * D : (3 + i) * D, :] = w2_acc[1, :D, half] + w2_acc[1, D:, half]
    sums = p_acc[...]
    sums = fold(sums[: 2 * D] + sums[2 * D :])
    early[4 * D : 4 * D + FREQ, :] = (sums[:D, :FREQ] + sums[D:, FREQ:]).T
    squares = []
    for part in range(3):
        sums = quarters(sq_acc[part])
        squares.append((sums[:FREQ, :FREQ] + sums[FREQ:, FREQ:]).T)
    early[4 * D + FREQ : 5 * D, :] = beside(squares[0], squares[1])
    early[5 * D : 5 * D + FREQ, :] = beside(squares[2], jnp.zeros_like(squares[2]))
    early[7 * D + FREQ :, :] = jnp.zeros((D // 2, D), F32)
    gains = [None, None]
    gains[1] = attend_back(1, [quarters(s_acc[s]) for s in range(count)])

    def norm_back(s, normal, scale):
        key, value = normal[:, :D], normal[:, D:]
        key_cot = even4(halves(value), t_keep[s, 0])
        value_cot = even4(halves(key), t_keep[s, 1])
        mean = dot(beside(*halves(key_cot * key)), mean_weight) * (HEADS / D)
        return beside(scale[:, :D] * (key_cot - key * mean), scale[:, D:] * (value_cot - value * mean))

    early_route.start(0)

    def middle_back(index, _):
        @pl.when(index == 1)
        def _():
            mode_route.step(2)
            early_route.step(0)

        where = block(index)
        s = index // steps
        cot = norm_back(s, x_keep[where, :], r_keep[where, :])
        pieces = thirds(cot)
        high, low = pieces[:2]
        kept = h1_keep[where, :]
        kv_acc[...] += dot(kept, high, 0, 0)
        kv_acc[:D, :] += dot(kept[:, :D], low, 0, 0)
        out = d_keep[where, :]
        out = (
            out
            + even4(halves(out), nt_keep[s])
            + tall6(pieces, (w_kvt[:, : 2 * D], w_kvt[:, 2 * D :]))
        )
        outer, inner = feed_back(0, index, out)
        v_acc[s] += dot(lrows[index], beside(*outer[:2]))
        u_acc[s] += dot(lrows[index], beside(*inner[:2]))
        return 0

    lax.fori_loop(0, rows_all, middle_back, 0)
    mode_route.finish(3)
    put_mode.start()
    early_route.step(1)

    def lift_sum(value):
        value = fold(value)
        return above(
            value[0:1] + value[1:2] + value[2:3],
            value[3:4] + value[4:5] + value[5:6],
            value[6:7],
            jnp.zeros((5, value.shape[1]), F32),
        )

    inner_rows = [lift_sum(u_acc[s]) for s in range(count)]
    value_rows = [lift_sum(v_acc[s]) + exact(inner_rows[s], ffn_ref[0, 0], 1, 1) for s in range(count)]
    gains[0] = attend_back(0, [exact(lift_rows, value_rows[s], 0, 0) for s in range(count)])

    query_rows = jnp.zeros((8, D), F32)
    lift_part = jnp.zeros((8, D), F32)
    inner_grad = jnp.zeros((D, FF), F32)
    for s in range(count):
        query_rows += exact(value_rows[s], small_keep[0, s, 2], 1, 1)
        lift_part += value_rows[s] + exact(value_rows[s], n_keep[0, s], 1, 1)
        inner_grad += exact(mid_rows[s], inner_rows[s], 0, 0)
    for i in range(2):
        half = slice(i * D, (i + 1) * D)
        late[i * D : (i + 1) * D, :] = exact(kv_acc[:D, half] + kv_acc[D:, half], centre)
        late[(2 + i) * D : (3 + i) * D, :] = w2_acc[0, :D, half] + w2_acc[0, D:, half]
        late[(4 + i) * D : (5 + i) * D, :] = inner_grad[:, half]

    def bias(slot, width=D):
        return jnp.sum(b_acc[slot * 8 : slot * 8 + 8, :width], 0, keepdims=True)

    rows = [jnp.zeros((3, D), F32)]
    for layer in range(LAYERS):
        inner = bias(8 + 2 * layer, FF)
        rows += [gains[layer][0], gains[layer][1], inner[:, :D], inner[:, D:], bias(7 + 2 * layer)]
    short = [fold(bias(slot)) for slot in (6, 5, 4, 3, 2)]
    rows += [beside(short[0], short[1]), beside(short[2], short[3]), beside(short[4], jnp.zeros((1, FREQ), F32))]
    late[7 * D : 7 * D + 16, :] = above(*rows)
    lanes = lax.broadcasted_iota(jnp.int32, (1, D), 1)
    first = jnp.where(lax.rem(lanes, FREQ) == 0, bias(0), 0.0)
    second = jnp.where(lax.rem(lanes, FREQ) == 0, bias(1), 0.0)
    late[7 * D + 16 : 7 * D + 24, :] = above(first, second, jnp.zeros((6, D), F32))
    late[7 * D + 24 : 7 * D + 32, :] = query_rows
    late[7 * D + 32 : 7 * D + 40, :] = lift_part
    late[7 * D + 40 :, :] = jnp.zeros((D - 40, D), F32)
    late_route.start(0)

    def front_back(index, _):
        @pl.when(index == 1)
        def _():
            late_route.step(0)

        centred = dot(lifted[block(index), :], w0_kv[...])
        scale = head_scale(centred)
        cot = norm_back(index // steps, centred * scale, scale)
        vt_acc[...] += dot(lrows[index], beside(*halves(cot)))
        return 0

    lax.fori_loop(0, rows_all, front_back, 0)
    turned = lift_sum(vt_acc[...])
    tail_send[...] = above(turned[:4, :D], turned[:4, D:])
    swap = pltpu.make_async_remote_copy(
        src_ref=tail_send,
        dst_ref=tail_swap,
        send_sem=tail_sends.at[devices // 2 - 1],
        recv_sem=tail_recvs.at[devices // 2 - 1],
        device_id=device_of(x, 1 - core, z, y),
        device_id_type=MESH,
    )
    swap.start()
    late_route.step(1)
    swap.wait()
    tail_pair[...] = tail_send[...] + tail_swap[...]
    tail_land[place] = tail_pair[...]
    to_each(lambda r: tail_pair, tail_land, lambda r: r - 16 * core, mine, tail_sends, tail_recvs, devices // 2 - 1, True)
    early_route.step(2)
    early_route.finish(3)
    put_early.start()
    to_each(lambda r: tail_pair, tail_land, lambda r: r - 16 * core, mine, tail_sends, tail_recvs, devices // 2 - 1, False)
    late_route.step(2)
    late_route.finish(3)
    put_mode.wait()
    put_early.wait()
    summed = jnp.sum(tail_land[...], 0)
    zero = jnp.zeros((4, 2 * D), F32)
    turned = above(beside(summed[:4], summed[4:]), zero)
    joined = exact(lift_rows, turned, 0, 0)
    tail_out[:D, :] = exact(lift_rows, late_out[7 * D + 24 : 7 * D + 32, :], 0, 0)
    tail_out[D : 2 * D, :] = exact(joined[:, :D], centre)
    tail_out[2 * D : 3 * D, :] = exact(joined[:, D:], centre)
    tail_out[3 * D :, :] = late_out[7 * D + 32 : 7 * D + 40, :] + exact(turned, cent_keep[0], 1, 1)


def tables(points):
    order = np.arange(MODES)[:, None]
    angle = (order * np.arange(points)[None, :]) % points * (2.0 * math.pi / points)
    full = np.concatenate([np.cos(angle), np.sin(angle)], 0).astype(np.float32)
    kind = np.dtype(ml_dtypes.bfloat16)
    high = full.astype(kind)
    rest = full - high.astype(np.float32)
    middle = rest.astype(kind)
    low = (rest - middle.astype(np.float32)).astype(kind)
    zero = np.zeros((4 * MODES, points), kind)
    column = np.concatenate([high, middle, high, middle, high, low, zero], 0).T
    row = np.concatenate([high, middle], 0).reshape(4 * MODES, points // ROWS, ROWS).transpose(1, 0, 2)
    return np.ascontiguousarray(column), np.ascontiguousarray(row)


def summed_grads(samples_in, target, mask, attn_w, ffn_w, spec_w, turned_w, vectors):
    parts = samples_in.shape[0] // 2
    count, points = 2, samples_in.shape[2] * parts
    devices = FLAYERS * MODES
    total = count * points
    steps = points // ROWS
    column, row = tables(points)
    vmem = pl.BlockSpec(memory_space=pltpu.VMEM)
    anywhere = pl.BlockSpec(memory_space=pl.ANY)
    first = [
        ((parts, 8, samples_in.shape[2]), F32),
        ((parts, 8, samples_in.shape[2]), F32),
        ((NVEC_ROWS, D), F32),
        ((8 * D, D), F32),
        ((8 * D, D), F32),
        ((8 * D, D), F32),
        ((8 * D, D), F32),
        ((devices, 8, D), F32),
        ((devices, 8, D), F32),
        ((8, D), F32),
        ((8, D), F32),
        ((8, D), F32),
        ((devices // 2, 8, D), F32),
    ]
    numbers = (3 * devices, 3 * devices, parts - 1, parts - 1, devices - 1, devices - 1, devices // 2, devices // 2)
    scratch = [
        ((total, D), BF16),
        ((total // ROWS, 16, ROWS), BF16),
        ((6 * D, 2 * D), BF16),
        ((4 * D, 3 * D), BF16),
        ((6 * D, FF), BF16),
        ((2 * FF, 3 * D), BF16),
        ((count, D, FF), BF16),
        ((count, 8, D), F32),
        ((LAYERS, 2 * FF, 2 * D), BF16),
        ((LAYERS, 2 * FF, D), BF16),
        ((LAYERS, 6 * D, FF), BF16),
        ((total, 2 * D), F32),
        ((total, 2 * D), F32),
        ((LAYERS, total, FF), F32),
        ((LAYERS, total, 2 * FF), BF16),
        ((total, 2 * D), BF16),
        ((total, 2 * D), BF16),
        ((total, 3 * D), BF16),
        ((FLAYERS, points, 3 * D), BF16),
        ((points, 3 * D), BF16),
        ((count, 2 * D, 2 * D), F32),
        ((D, 2 * D), BF16),
        ((count, D, D), BF16),
        ((LAYERS, count, D, D), F32),
        ((LAYERS, count, 3, D, D), F32),
        ((count, 2 * D, 2 * D), BF16),
        ((LAYERS, D, 2 * D), F32),
        ((4 * MODES, 2 * D), F32),
        ((FLAYERS, 2 * count * MODES, D), F32),
        ((2 * D, D), BF16),
        ((3, 2 * D, 2 * D), F32),
        ((4 * D, 2 * D), F32),
        ((LAYERS, 2 * D, FF), F32),
        ((2 * D, FF), F32),
        ((2 * D, 2 * D), F32),
        ((count, 16, 2 * D), F32),
        ((count, 16, 2 * FF), F32),
        ((16, 4 * D), F32),
        ((96, FF), F32),
        ((total, D), F32),
        ((count, 2, 2 * D, 2 * D), BF16),
        ((count, 4 * D, 2 * D), BF16),
    ]
    shapes = [(8 * D, D), (8 * D, D), (devices * FREQ, D), (3 * D + 8, D)]
    return pl.pallas_call(
        step_kernel,
        out_shape=[jax.ShapeDtypeStruct(shape, F32) for shape in shapes],
        in_specs=[vmem] * 5 + [anywhere] + [vmem] * 2 + [anywhere] * 2,
        out_specs=[anywhere, vmem, anywhere, vmem],
        scratch_shapes=[
            pltpu.VMEM(spec_w.shape, F32),
            pltpu.VMEM(column.shape, BF16),
            pltpu.VMEM(row.shape, BF16),
            pltpu.VMEM(shapes[0], F32),
            pltpu.VMEM(shapes[2], F32),
            pltpu.SemaphoreType.DMA((5,)),
        ]
        + [pltpu.VMEM(*item) for item in first]
        + [pltpu.SemaphoreType.DMA((number,)) for number in numbers]
        + [pltpu.VMEM(*item) for item in scratch],
        compiler_params=pltpu.CompilerParams(
            vmem_limit_bytes=64 * 2**20 - 2**17, collective_id=0, has_side_effects=True
        ),
    )(
        samples_in,
        target,
        mask,
        attn_w,
        ffn_w,
        spec_w,
        turned_w,
        vectors,
        jnp.asarray(column),
        jnp.asarray(row),
    )


def update_kernel(
    early,
    late,
    modes,
    tail,
    vectors,
    vector_m,
    vector_v,
    attn_w,
    ffn_w,
    spec_w,
    turned_w,
    attn_m,
    ffn_m,
    spec_m,
    turned_m,
    attn_v,
    ffn_v,
    spec_v,
    turned_v,
    loss_out,
    count_out,
    weight_out,
    update_out,
    ratio_out,
    vector_m_out,
    vector_v_out,
    vector_w_out,
    vector_low_out,
    *rest,
):
    outs, scratch = rest[:16], rest[16:]
    ins = (attn_w, ffn_w, spec_w, turned_w, attn_m, ffn_m, spec_m, turned_m, attn_v, ffn_v, spec_v, turned_v)
    held, fresh = scratch[:12], scratch[12:28]
    flat, in_sems, out_sems = scratch[28:]

    blocks = [(2, 0), (2, 1), (1, 1), (0, 1), (0, 0), (1, 0), (3, None)]

    def view(ref, part):
        return ref if part is None else ref.at[part]

    def load(slot, kind):
        array, part = blocks[slot]
        number = kind * 4 + array
        return pltpu.make_async_copy(
            view(ins[number], part), view(held[number], part), in_sems.at[slot * 3 + kind]
        )

    def store(slot, kind):
        array, part = blocks[slot]
        number = kind * 4 + array
        return pltpu.make_async_copy(
            view(fresh[number], part), view(outs[number], part), out_sems.at[slot * 4 + kind]
        )

    for slot in range(len(blocks)):
        for kind in range(3):
            load(slot, kind).start()
    misc = late[7 * D + 16 : 7 * D + 24, :]
    loss_out[0] = jnp.sum(misc[0:1])
    valid = jnp.sum(misc[1:2], keepdims=True)
    count_out[0] = jnp.sum(misc[1:2])
    scale = 1.0 / valid

    def moved(weight, grad, first, second):
        first_new = BETA_ONE * first + (1.0 - BETA_ONE) * grad
        second_new = BETA_TWO * second + (1.0 - BETA_TWO) * grad * grad
        update = (
            first_new
            / (1.0 - BETA_ONE**STEP)
            / (jnp.sqrt(second_new / (1.0 - BETA_TWO**STEP)) + ADAM_EPS)
            + DECAY * weight
        )
        return first_new, second_new, update

    def note(slot, weight_sum, update_sum):
        weight_norm, update_norm = jnp.sqrt(weight_sum), jnp.sqrt(update_sum)
        ratio = weight_norm / (update_norm + ADAM_EPS)
        weight_out[slot] = weight_norm[0, 0]
        update_out[slot] = update_norm[0, 0]
        ratio_out[slot] = ratio[0, 0]
        return RATE * ratio

    def total(sums):
        return sum(jnp.sum(value, keepdims=True) for value in sums.values())

    for i in range(NVEC_ROWS):
        start = i * D
        size = min(D, flat.shape[0] - start)
        row = tail[3 * D + i : 3 * D + i + 1, :] if i < 3 else late[7 * D + i : 7 * D + i + 1, :]
        flat[start : start + size] = (row * scale)[:, :size].reshape(size)
    weight = vectors[...]
    first_new, second_new, update = moved(weight, flat[...], vector_m[...], vector_v[...])
    vector_m_out[...] = first_new
    vector_v_out[...] = second_new
    rate = note(
        7,
        jnp.sum(weight * weight).reshape(1, 1),
        jnp.sum(update * update).reshape(1, 1),
    )
    flat[...] = jnp.broadcast_to(rate, (1, D)).reshape(D)[0] * update
    weight = weight - flat[...]
    vector_w_out[...] = weight
    vector_low_out[...] = weight.astype(BF16)

    def grad_blocks(array, part):
        if array == 0:
            if part:
                places = [(early, 5 * D + FREQ), (late, 0), (late, D), (early, 6 * D + FREQ)]
            else:
                places = [(tail, 0), (tail, D), (tail, 2 * D), (late, 6 * D)]
            return [
                (ref, start, D, 0, (slice(None), slice(j * D, (j + 1) * D)))
                for j, (ref, start) in enumerate(places)
            ]
        if array == 1:
            ref, starts = (early, (0, 1, 2, 3)) if part else (late, (4, 5, 2, 3))
            return [
                (ref, starts[j] * D, D, 0, (j // 2, slice(None), slice(j % 2 * D, j % 2 * D + D)))
                for j in range(4)
            ]
        if array == 3:
            return [
                (early, 4 * D, FREQ, 0, (slice(None), slice(0, D))),
                (early, 4 * D + FREQ, FREQ, 0, (slice(None), slice(D, 2 * D))),
                (early, 5 * D, FREQ, 0, (slice(None), slice(2 * D, 2 * D + FREQ))),
            ]
        return [
            (modes, (part * MODES + k) * FREQ, FREQ, j * FREQ, (k, j))
            for k in range(MODES)
            for j in range(2)
        ]

    for slot, (array, part) in enumerate(blocks):
        for kind in range(3):
            load(slot, kind).wait()
        weight_ref, first_ref, second_ref = [view(held[kind * 4 + array], part) for kind in range(3)]
        first_out, second_out, weight_new, low_out = [view(fresh[kind * 4 + array], part) for kind in range(4)]
        pieces = grad_blocks(array, part)
        weight_sums, update_sums = {}, {}
        for ref, start, rows, lane, where in pieces:
            weight = weight_ref[where]
            width = weight.shape[1]
            grad = ref[start : start + rows, lane : lane + width] * scale
            first_new, second_new, update = moved(weight, grad, first_ref[where], second_ref[where])
            first_out[where] = first_new
            second_out[where] = second_new
            weight_new[where] = update
            weight_sums[width] = weight_sums.get(width, 0.0) + column_sum(weight * weight)
            update_sums[width] = update_sums.get(width, 0.0) + column_sum(update * update)
        store(slot, 0).start()
        store(slot, 1).start()
        place = (0 + part if array == 0 else 2 + part if array == 1 else 4 + part) if part is not None else 6
        rate = note(place, total(weight_sums), total(update_sums))
        for ref, start, rows, lane, where in pieces:
            weight = weight_ref[where] - rate * weight_new[where]
            weight_new[where] = weight
            low_out[where] = weight.astype(BF16)
        store(slot, 2).start()
        store(slot, 3).start()
    for slot in range(len(blocks)):
        for kind in range(4):
            store(slot, kind).wait()


def fast_body(samples_in, target, mask, attn_w, ffn_w, spec_w, dense_w, vectors, *moments):
    flat_spec = spec_w.reshape(FLAYERS, MODES * 2 * FREQ, FREQ)
    grads = summed_grads(samples_in, target, mask, attn_w, ffn_w, flat_spec, dense_w.T, vectors)
    sets = [
        (attn_w, ffn_w, spec_w, dense_w.T),
        (moments[0], moments[1], moments[2], moments[3].T),
        (moments[5], moments[6], moments[7], moments[8].T),
    ]
    vmem = pl.BlockSpec(memory_space=pltpu.VMEM)
    smem = pl.BlockSpec(memory_space=pltpu.SMEM)
    anywhere = pl.BlockSpec(memory_space=pl.ANY)
    shapes = [item.shape for item in sets[0]]
    kinds = (F32, F32, F32, BF16)
    scalar = [jax.ShapeDtypeStruct((1,), F32)] * 2 + [jax.ShapeDtypeStruct((8,), F32)] * 3
    line = [jax.ShapeDtypeStruct(vectors.shape, kind) for kind in kinds]
    arrays = [jax.ShapeDtypeStruct(shape, kind) for kind in kinds for shape in shapes]
    out = pl.pallas_call(
        update_kernel,
        out_shape=scalar + line + arrays,
        in_specs=[vmem] * 7 + [anywhere] * 12,
        out_specs=[smem] * 5 + [vmem] * 4 + [anywhere] * 16,
        scratch_shapes=[pltpu.VMEM(shape, F32) for _ in range(3) for shape in shapes]
        + [pltpu.VMEM(shape, kind) for kind in kinds for shape in shapes]
        + [pltpu.VMEM(vectors.shape, F32), pltpu.SemaphoreType.DMA((21,)), pltpu.SemaphoreType.DMA((28,))],
        compiler_params=pltpu.CompilerParams(vmem_limit_bytes=60 * 2**20),
    )(*grads, vectors, moments[4], moments[9], *sets[0], *sets[1], *sets[2])
    loss_sum, valid_count, weight_norms, update_norms, ratios = out[:5]
    line, arrays = out[5:9], out[9:]
    results = [loss_sum.reshape(()), valid_count.reshape(())]
    for array in range(4):
        for kind in range(4):
            item = arrays[kind * 4 + array]
            results.append(item.T if array == 3 else item)
    return tuple(results + list(line) + [weight_norms, update_norms, ratios])


def choose_body(*arrays):
    samples_in = arrays[0]
    dp, parts = lax.axis_size("dp"), lax.axis_size("pts")
    fits = dp * parts == FLAYERS * MODES and dp == 4 and samples_in.shape[0] == 2 * parts
    return (fast_body if fits and samples_in.shape[2] * parts % WIDE == 0 else body)(*arrays)


def solution(mesh):
    placed = (
        P("dp", None, "pts"),
        P("dp", "pts"),
        P("dp", "pts"),
        P(),
        P(),
        P(),
        P(),
        P(),
        P(),
        P(),
        P(),
        P(),
        P(),
        P(),
        P(),
        P(),
        P(),
        P(),
    )
    return jax.shard_map(
        choose_body,
        mesh=mesh,
        in_specs=placed,
        out_specs=(
            P(),
            P(),
            P(),
            P(),
            P(),
            P(),
            P(),
            P(),
            P(),
            P(),
            P(),
            P(),
            P(),
            P(),
            P(),
            P(),
            P(),
            P(),
            P(),
            P(),
            P(),
            P(),
            P(),
            P(),
            P(),
        ),
        check_vma=False,
    )
```
